32 devices in a mesh: sub: 32 (over z, y, x, core).
Axes of the slice: x: 2, y: 2, z: 4, core: 2. Of those that a mesh axis runs over, the one named last changes fastest.
Arguments:
- right_side: bfloat16 [32, 1024, 128], P('sub'), may hold values from -6 to 6
- schur: bfloat16 [32, 1024, 1024], P('sub'), may hold values from -1 to 2
- neumann: bfloat16 [32, 1024, 1024], P('sub'), may hold values from -1 to 1
- weights: float32 [32, 1024], P('sub'), may hold values from 0.25 to 1
- neighbours: int32 [32, 4], P('sub'), may hold values from -1 to 31, as said below
- counts: int32 [32], P('sub'), may hold values from 512 to 1024, as said below
- shared_rows: int32 [32, 4, 128], P('sub'), may hold values from 0 to 1023, as said below
Outputs:
- solution: float32 [32, 1024, 128], P('sub')
The draws below stay inside these ranges and needn't reach their ends.
Inputs may be any that keep to these rules, and one draw needn't show every extreme that they name: `neighbours`: slot 0 holds s + 1, slot 1 s - 1, slot 2 s + 16, slot 3 s - 16 where that link exists, else -1; links are symmetric: s names t in a slot exactly when t names s in the opposite slot. Subdomains 32 - 2 and 31 are always linked. `counts`: every subdomain has at least 512 nodes in use; some subdomain uses all 1024. `shared_rows`: every entry of subdomain s is below counts[s]; entries of one list may repeat.
All inputs are finite; a program needn't handle non-finite values.
Results may differ from the reference program's by a relative error of at most 0.0075.
Values may be sent and summed in bfloat16 or wider, within the bound.
No kernel may reach another device: no remote copies, remote signals or barrier semaphores. Data moves between devices by JAX's collectives and lax.ppermute only.
A program may use at most 64 MiB of HBM per device.

```python
import math
import jax
import jax.numpy as jnp
from jax import lax

NI = 1024
LEADS = 128
SHARE = 128
ITERS = 4
SUBS = 32


def common_counts(key):
    base = jax.random.randint(jax.random.fold_in(key, 11), (SUBS,), NI // 2, NI + 1)
    top = jax.random.randint(jax.random.fold_in(key, 12), (), 0, SUBS)
    base = base.at[top].set(NI)
    base = base.at[(top + 1) % SUBS].set(NI // 2)
    return (base.astype(jnp.int32), top)


def draw_counts(key, part):
    used, top = common_counts(key)
    return used


def draw_shared_rows(key, part):
    used, top = common_counts(key)
    raw = jax.random.randint(jax.random.fold_in(key, 13), (SUBS, 4, SHARE), 0, 1048576)
    rows = (raw % used[:, None, None]).astype(jnp.int32)
    rows = rows.at[top, 0, 0].set(NI - 1)
    rows = rows.at[top, 0, 1].set(0)
    return rows.astype(jnp.int32)


def draw_neighbours(key, part):
    index = jnp.arange(SUBS)
    near = (jax.random.randint(jax.random.fold_in(key, 21), (SUBS,), 0, 4) < 3) & (index + 1 < SUBS)
    near = near | (index == SUBS - 2)
    far = (jax.random.randint(jax.random.fold_in(key, 22), (SUBS,), 0, 4) < 3) & (index + 16 < SUBS)
    slot_up = jnp.where(near, index + 1, -1)
    slot_down = jnp.where(jnp.roll(near, 1) & (index >= 1), index - 1, -1)
    slot_far_up = jnp.where(far, index + 16, -1)
    slot_far_down = jnp.where(jnp.roll(far, 16) & (index >= 16), index - 16, -1)
    return jnp.stack([slot_up, slot_down, slot_far_up, slot_far_down], 1).astype(jnp.int32)


def dominant(key, spread, low, high):
    shape = (SUBS, NI, NI)
    off = jax.random.normal(jax.random.fold_in(key, 1), shape, jnp.float32) * (spread / math.sqrt(NI))
    diag = jax.random.uniform(jax.random.fold_in(key, 2), (SUBS, NI, 1), jnp.float32, low, high)
    eye = (jnp.arange(NI)[:, None] == jnp.arange(NI)[None, :]).astype(jnp.float32)
    return (off * (1.0 - eye) + eye * diag).astype(jnp.bfloat16)


def draw_schur(key, part):
    return dominant(jax.random.fold_in(key, 31), 0.25, 1.0, 2.0)


def draw_neumann(key, part):
    return dominant(jax.random.fold_in(key, 32), 0.15, 0.5, 1.0)


def block_levels(stream_key, shape, pieces, smallest, high):
    loudness = 1.0
    for position, blocks in pieces:
        draws = jax.random.uniform(jax.random.fold_in(jax.random.fold_in(stream_key, 6), position), (blocks,), jnp.float32, smallest / len(pieces), high / len(pieces))
        loudness = loudness * jnp.repeat(jnp.exp(draws), shape[position] // blocks).reshape((-1,) + (1,) * (len(shape) - 1 - position))
    return loudness


def centred(own_key, dims, scale, most, shards=(), kind=jnp.bfloat16):
    loudness = block_levels(own_key, dims, shards, -0.22, 0.18) if shards else 1.0
    result = jax.random.normal(own_key, dims, jnp.float32) * scale * loudness
    return jnp.minimum(jnp.maximum(result, -most), most).astype(kind)


def setup_inputs(seed: int = 0) -> dict:
    key_of = jax.random.split(jax.random.key(seed), 8)
    right_side = centred(key_of[0], (SUBS, NI, LEADS), 1.0, 6.0, ((0, 32),))
    schur = draw_schur(jax.random.fold_in(key_of[7], 71), 0)
    neumann = draw_neumann(jax.random.fold_in(key_of[7], 71), 0)
    weights = jnp.clip(jnp.exp(math.log(1.0) - 1.3862944 * jax.random.uniform(key_of[3], (SUBS, NI), jnp.float32) ** block_levels(key_of[3], (SUBS, NI), ((0, 32),), -0.2, 0.2)), 0.25, 1.0)
    neighbours = draw_neighbours(jax.random.fold_in(key_of[7], 71), 0)
    counts = draw_counts(jax.random.fold_in(key_of[7], 71), 0)
    shared_rows = draw_shared_rows(jax.random.fold_in(key_of[7], 71), 0)
    return dict(right_side=right_side, schur=schur, neumann=neumann, weights=weights, neighbours=neighbours, counts=counts, shared_rows=shared_rows)


link_offsets = (1, -1, 16, -16)
opposite_slot = (1, 0, 3, 2)
damping_factor = 0.7


def shift_rows(packed, offset):
    total_subs = packed.shape[0]
    padding = jnp.zeros((abs(offset),) + packed.shape[1:], packed.dtype)
    if offset > 0:
        return jnp.concatenate([packed[offset:], padding], 0)
    return jnp.concatenate([padding, packed[:total_subs + offset]], 0)


def assemble(own, sent, shared_rows, live):
    total = own
    sub_index = jnp.arange(own.shape[0])[:, None]
    for slot in range(4):
        packed = sent[sub_index, shared_rows[:, opposite_slot[slot]]]
        received = shift_rows(packed, link_offsets[slot]).astype(jnp.float32)
        received = received * live[:, slot][:, None, None]
        total = total.at[sub_index, shared_rows[:, slot]].add(received)
    return total


def reference(right_side, schur, neumann, weights, neighbours, counts, shared_rows):
    width = schur.shape[1]
    mask = (jnp.arange(width)[None, :] < counts[:, None]).astype(jnp.float32)[:, :, None]
    live = (neighbours >= 0).astype(jnp.float32)
    weight = weights[:, :, None]
    rhs = right_side.astype(jnp.float32)
    solution = jnp.zeros(right_side.shape, jnp.float32)
    for step in range(ITERS):
        current = solution.astype(jnp.bfloat16)
        product = lax.map(lambda pair: jnp.dot(pair[0].T, pair[1], preferred_element_type=jnp.float32), (schur, current))
        local = mask * (rhs - product)
        residual = assemble(local, local.astype(jnp.bfloat16), shared_rows, live)
        scaled = (weight * residual).astype(jnp.bfloat16)
        correction = lax.map(lambda pair: jnp.dot(pair[0], pair[1], preferred_element_type=jnp.float32), (neumann, scaled))
        weighted = mask * weight * correction
        update = assemble(weighted, weighted.astype(jnp.bfloat16), shared_rows, live)
        solution = solution + damping_factor * update
    return solution
```

```python
import jax
import jax.numpy as jnp
from jax import lax
from jax.sharding import PartitionSpec as P

ITERS = 4
FAR = 16
DAMPING = 0.7


def swaps(count):
    near = [(i, i ^ 1) for i in range(count)]
    cross = [(i, ((i + 1) ^ 1) - 1) for i in range(count)]
    cross = [(i, j % count) for i, j in cross]
    blocks = count // FAR
    far = [(i, i ^ FAR) for i in range(count)] if blocks > 1 else []
    pairs = [far, near, cross]
    if blocks > 2:
        again = [(i, (((i // FAR + 1) ^ 1) - 1) % blocks * FAR + i % FAR) for i in range(count)]
        pairs = [far, again, near, cross]
    return [p for p in pairs if p]


def slots_of(index, count):
    odd = index % 2
    block = index // FAR % 2
    far, again = 2 + block, 3 - block
    if count // FAR > 2:
        return [far, again, odd, 1 - odd]
    return [far, odd, 1 - odd]


def body(right_side, schur, neumann, weights, neighbours, counts, shared_rows):
    rhs16 = right_side[0]
    rhs = rhs16.astype(jnp.float32)
    s_mat = schur[0]
    n_mat = neumann[0]
    weight = weights[0][:, None]
    count = counts[0]
    width = s_mat.shape[0]
    share = shared_rows.shape[2]
    subs = lax.axis_size("sub")
    routes = swaps(subs)
    slots = slots_of(lax.axis_index("sub"), subs)
    rows = jnp.concatenate([lax.dynamic_index_in_dim(shared_rows[0], k, 0, False) for k in slots])
    live = jnp.concatenate(
        [jnp.broadcast_to(lax.dynamic_index_in_dim(neighbours[0], k, 0, True) >= 0, (share,)) for k in slots]
    )
    mask = (jnp.arange(width) < count).astype(jnp.float32)[:, None]
    hot = (jnp.arange(width)[:, None] == rows[None, :]) & live[None, :]
    placer = hot.astype(jnp.bfloat16)
    picked_weight = jnp.sum(jnp.where(hot, weight, 0.0), 0)[:, None]
    picked_rhs = lax.dot_general(placer, rhs16, (((0,), (0,)), ((), ())), preferred_element_type=jnp.float32)
    picked_s = jnp.dot(s_mat, placer, preferred_element_type=jnp.float32).astype(jnp.bfloat16)
    picked_n = lax.dot_general(
        placer, n_mat, (((0,), (0,)), ((), ())), preferred_element_type=jnp.float32
    ).astype(jnp.bfloat16)
    mask_weight = mask * weight

    def exchange(packed):
        parts = [
            lax.ppermute(packed[k * share : (k + 1) * share], "sub", route) for k, route in enumerate(routes)
        ]
        return jnp.dot(placer, jnp.concatenate(parts, 0), preferred_element_type=jnp.float32)

    def transposed(mat, block):
        return lax.dot_general(mat, block, (((0,), (0,)), ((), ())), preferred_element_type=jnp.float32)

    solution = jnp.zeros(rhs.shape, jnp.float32)
    for step in range(ITERS):
        current = solution.astype(jnp.bfloat16)
        arrived = exchange((picked_rhs - transposed(picked_s, current)).astype(jnp.bfloat16))
        local = mask * (rhs - transposed(s_mat, current))
        scaled = (weight * (local + arrived)).astype(jnp.bfloat16)
        sent = picked_weight * jnp.dot(picked_n, scaled, preferred_element_type=jnp.float32)
        arrived = exchange(sent.astype(jnp.bfloat16))
        weighted = mask_weight * jnp.dot(n_mat, scaled, preferred_element_type=jnp.float32)
        solution = solution + DAMPING * (weighted + arrived)
    return solution[None]


def solution(mesh):
    in_specs = (
        P("sub", None, None),
        P("sub", None, None),
        P("sub", None, None),
        P("sub", None),
        P("sub", None),
        P("sub"),
        P("sub", None, None),
    )
    out_specs = P("sub", None, None)
    return jax.shard_map(body, mesh=mesh, in_specs=in_specs, out_specs=out_specs, check_vma=False)
```

```python
import jax
import jax.numpy as jnp
from jax import lax
from jax.sharding import PartitionSpec as P

ITERS = 4
FAR = 16
DAMPING = 0.7


def swaps(count):
    near = [(i, i ^ 1) for i in range(count)]
    cross = [(i, ((i + 1) ^ 1) - 1) for i in range(1, count - 1)]
    blocks = count // FAR
    far = [(i, i ^ FAR) for i in range(count)] if blocks > 1 else []
    pairs = [far, near, cross]
    if blocks > 2:
        again = [(i, (((i // FAR + 1) ^ 1) - 1) % blocks * FAR + i % FAR) for i in range(count)]
        pairs = [far, again, near, cross]
    return [p for p in pairs if p]


def slots_of(index, count):
    odd = index % 2
    block = index // FAR % 2
    far, again = 2 + block, 3 - block
    if count // FAR > 2:
        return [far, again, odd, 1 - odd]
    return [far, odd, 1 - odd]


def body(right_side, schur, neumann, weights, neighbours, counts, shared_rows):
    rhs16 = right_side[0]
    rhs = rhs16.astype(jnp.float32)
    s_mat = schur[0]
    n_mat = neumann[0]
    weight = weights[0][:, None]
    count = counts[0]
    width = s_mat.shape[0]
    share = shared_rows.shape[2]
    subs = lax.axis_size("sub")
    routes = swaps(subs)
    slots = slots_of(lax.axis_index("sub"), subs)
    rows = jnp.concatenate([lax.dynamic_index_in_dim(shared_rows[0], k, 0, False) for k in slots])
    live = jnp.concatenate(
        [jnp.broadcast_to(lax.dynamic_index_in_dim(neighbours[0], k, 0, True) >= 0, (share,)) for k in slots]
    )
    mask = (jnp.arange(width) < count).astype(jnp.float32)[:, None]
    hot = (jnp.arange(width)[:, None] == rows[None, :]) & live[None, :]
    placer = hot.astype(jnp.bfloat16)
    picked_weight = jnp.sum(jnp.where(hot, weight, 0.0), 0)[:, None]
    picked_rhs = lax.dot_general(placer, rhs16, (((0,), (0,)), ((), ())), preferred_element_type=jnp.float32)
    picked_s = jnp.dot(s_mat, placer, preferred_element_type=jnp.float32).astype(jnp.bfloat16)
    picked_n = lax.dot_general(
        placer, n_mat, (((0,), (0,)), ((), ())), preferred_element_type=jnp.float32
    ).astype(jnp.bfloat16)
    mask_weight = mask * weight

    def exchange(packed):
        parts = [
            lax.ppermute(packed[k * share : (k + 1) * share], "sub", route) for k, route in enumerate(routes)
        ]
        return jnp.dot(placer, jnp.concatenate(parts, 0), preferred_element_type=jnp.float32)

    def transposed(mat, block):
        return lax.dot_general(mat, block, (((0,), (0,)), ((), ())), preferred_element_type=jnp.float32)

    solution = jnp.zeros(rhs.shape, jnp.float32)
    for step in range(ITERS):
        current = solution.astype(jnp.bfloat16)
        arrived = exchange((picked_rhs - transposed(picked_s, current)).astype(jnp.bfloat16))
        local = mask * (rhs - transposed(s_mat, current))
        scaled = (weight * (local + arrived)).astype(jnp.bfloat16)
        sent = picked_weight * jnp.dot(picked_n, scaled, preferred_element_type=jnp.float32)
        arrived = exchange(sent.astype(jnp.bfloat16))
        weighted = mask_weight * jnp.dot(n_mat, scaled, preferred_element_type=jnp.float32)
        solution = solution + DAMPING * (weighted + arrived)
    return solution[None]


def solution(mesh):
    in_specs = (
        P("sub", None, None),
        P("sub", None, None),
        P("sub", None, None),
        P("sub", None),
        P("sub", None),
        P("sub"),
        P("sub", None, None),
    )
    out_specs = P("sub", None, None)
    return jax.shard_map(body, mesh=mesh, in_specs=in_specs, out_specs=out_specs, check_vma=False)
```

```python
import jax
import jax.numpy as jnp
from jax import lax
from jax.sharding import PartitionSpec as P

ITERS = 4
FAR = 16
DAMPING = 0.7


def body(right_side, schur, neumann, weights, neighbours, counts, shared_rows):
    rhs16 = right_side[0]
    rhs = rhs16.astype(jnp.float32)
    s_mat = schur[0]
    n_mat = neumann[0]
    weight = weights[0][:, None]
    count = counts[0]
    width = s_mat.shape[0]
    share = shared_rows.shape[2]
    subs = lax.axis_size("sub")
    index = lax.axis_index("sub")
    near = [(i, i ^ 1) for i in range(subs)]
    blocks = subs // FAR
    again = [(i, (((i // FAR + 1) ^ 1) - 1) % blocks * FAR + i % FAR) for i in range(subs)] if blocks > 2 else []
    span = 2 * FAR
    teams = []
    for base in range(0, subs, span):
        for j in range(0, FAR, 2):
            teams.append([base + (j + 1) % span, base + (j + 2) % span, base + (j + 1 + FAR) % span, base + (j + 2 + FAR) % span])
    turned = (index + span - 1) % span
    place = turned % 2 + 2 * (turned // FAR)
    odd = index % 2
    block = index // FAR % 2
    slots = []
    for q in range(4):
        gap = q ^ place
        slots.append(jnp.where(gap == 1, 1 - odd, jnp.where(gap == 2, 2 + block, -1)))
    slots.append(odd)
    if again:
        slots.append(3 - block)
    rows = jnp.concatenate([lax.dynamic_index_in_dim(shared_rows[0], jnp.maximum(k, 0), 0, False) for k in slots])
    live = jnp.concatenate(
        [jnp.broadcast_to((lax.dynamic_index_in_dim(neighbours[0], jnp.maximum(k, 0), 0, True) >= 0) & (k >= 0), (share,)) for k in slots]
    )
    mask = (jnp.arange(width) < count).astype(jnp.float32)[:, None]
    hot = (jnp.arange(width)[:, None] == rows[None, :]) & live[None, :]
    placer = hot.astype(jnp.bfloat16)
    picked_weight = jnp.sum(jnp.where(hot, weight, 0.0), 0)[:, None]
    picked_rhs = lax.dot_general(placer, rhs16, (((0,), (0,)), ((), ())), preferred_element_type=jnp.float32)
    picked_s = jnp.dot(s_mat, placer, preferred_element_type=jnp.float32).astype(jnp.bfloat16)
    picked_n = lax.dot_general(
        placer, n_mat, (((0,), (0,)), ((), ())), preferred_element_type=jnp.float32
    ).astype(jnp.bfloat16)
    mask_weight = mask * weight

    def exchange(packed):
        parts = [lax.ppermute(packed[4 * share : 5 * share], "sub", near)]
        if again:
            parts.append(lax.ppermute(packed[5 * share : 6 * share], "sub", again))
        out = lax.all_to_all(packed[: 4 * share].reshape(4, share, -1), "sub", 0, 0, axis_index_groups=teams)
        parts = [out.reshape(4 * share, -1)] + parts
        return jnp.dot(placer, jnp.concatenate(parts, 0), preferred_element_type=jnp.float32)

    def transposed(mat, block):
        return lax.dot_general(mat, block, (((0,), (0,)), ((), ())), preferred_element_type=jnp.float32)

    solution = jnp.zeros(rhs.shape, jnp.float32)
    for step in range(ITERS):
        current = solution.astype(jnp.bfloat16)
        arrived = exchange((picked_rhs - transposed(picked_s, current)).astype(jnp.bfloat16))
        local = mask * (rhs - transposed(s_mat, current))
        scaled = (weight * (local + arrived)).astype(jnp.bfloat16)
        sent = picked_weight * jnp.dot(picked_n, scaled, preferred_element_type=jnp.float32)
        arrived = exchange(sent.astype(jnp.bfloat16))
        weighted = mask_weight * jnp.dot(n_mat, scaled, preferred_element_type=jnp.float32)
        solution = solution + DAMPING * (weighted + arrived)
    return solution[None]


def solution(mesh):
    in_specs = (
        P("sub", None, None),
        P("sub", None, None),
        P("sub", None, None),
        P("sub", None),
        P("sub", None),
        P("sub"),
        P("sub", None, None),
    )
    out_specs = P("sub", None, None)
    return jax.shard_map(body, mesh=mesh, in_specs=in_specs, out_specs=out_specs, check_vma=False)
```

```python
import jax
import jax.numpy as jnp
from jax import lax
from jax.sharding import PartitionSpec as P

ITERS = 4
FAR = 16
DAMPING = 0.7


def swaps(count):
    near = [(i, i ^ 1) for i in range(count)]
    cross = [(i, ((i + 1) ^ 1) - 1) for i in range(count)]
    cross = [(i, j % count) for i, j in cross]
    blocks = count // FAR
    far = [(i, i ^ FAR) for i in range(count)] if blocks > 1 else []
    pairs = [cross, near, far]
    if blocks > 2:
        again = [(i, (((i // FAR + 1) ^ 1) - 1) % blocks * FAR + i % FAR) for i in range(count)]
        pairs = [cross, near, far, again]
    return [p for p in pairs if p]


def slots_of(index, count):
    odd = index % 2
    block = index // FAR % 2
    far, again = 2 + block, 3 - block
    if count // FAR > 2:
        return [1 - odd, odd, far, again]
    return [1 - odd, odd, far]


def body(right_side, schur, neumann, weights, neighbours, counts, shared_rows):
    rhs16 = right_side[0]
    rhs = rhs16.astype(jnp.float32)
    s_mat = schur[0]
    n_mat = neumann[0]
    weight = weights[0][:, None]
    count = counts[0]
    width = s_mat.shape[0]
    share = shared_rows.shape[2]
    subs = lax.axis_size("sub")
    routes = swaps(subs)
    slots = slots_of(lax.axis_index("sub"), subs)
    rows = jnp.concatenate([lax.dynamic_index_in_dim(shared_rows[0], k, 0, False) for k in slots])
    live = jnp.concatenate(
        [jnp.broadcast_to(lax.dynamic_index_in_dim(neighbours[0], k, 0, True) >= 0, (share,)) for k in slots]
    )
    mask = (jnp.arange(width) < count).astype(jnp.float32)[:, None]
    hot = (jnp.arange(width)[:, None] == rows[None, :]) & live[None, :]
    placer = hot.astype(jnp.bfloat16)
    picked_weight = jnp.sum(jnp.where(hot, weight, 0.0), 0)[:, None]
    picked_rhs = lax.dot_general(placer, rhs16, (((0,), (0,)), ((), ())), preferred_element_type=jnp.float32)
    picked_s = jnp.dot(s_mat, placer, preferred_element_type=jnp.float32).astype(jnp.bfloat16)
    picked_n = lax.dot_general(
        placer, n_mat, (((0,), (0,)), ((), ())), preferred_element_type=jnp.float32
    ).astype(jnp.bfloat16)
    mask_weight = mask * weight

    def exchange(packed):
        parts = [
            lax.ppermute(packed[k * share : (k + 1) * share], "sub", route) for k, route in enumerate(routes)
        ]
        return jnp.dot(placer, jnp.concatenate(parts, 0), preferred_element_type=jnp.float32)

    def transposed(mat, block):
        return lax.dot_general(mat, block, (((0,), (0,)), ((), ())), preferred_element_type=jnp.float32)

    solution = jnp.zeros(rhs.shape, jnp.float32)
    for step in range(ITERS):
        current = solution.astype(jnp.bfloat16)
        arrived = exchange((picked_rhs - transposed(picked_s, current)).astype(jnp.bfloat16))
        local = mask * (rhs - transposed(s_mat, current))
        scaled = (weight * (local + arrived)).astype(jnp.bfloat16)
        sent = picked_weight * jnp.dot(picked_n, scaled, preferred_element_type=jnp.float32)
        arrived = exchange(sent.astype(jnp.bfloat16))
        weighted = mask_weight * jnp.dot(n_mat, scaled, preferred_element_type=jnp.float32)
        solution = solution + DAMPING * (weighted + arrived)
    return solution[None]


def solution(mesh):
    in_specs = (
        P("sub", None, None),
        P("sub", None, None),
        P("sub", None, None),
        P("sub", None),
        P("sub", None),
        P("sub"),
        P("sub", None, None),
    )
    out_specs = P("sub", None, None)
    return jax.shard_map(body, mesh=mesh, in_specs=in_specs, out_specs=out_specs, check_vma=False)
```

```python
import jax
import jax.numpy as jnp
from jax import lax
from jax.sharding import PartitionSpec as P

ITERS = 4
FAR = 16
DAMPING = 0.7


def swaps(count):
    near = [(i, i ^ 1) for i in range(count)]
    cross = [(i, ((i + 1) ^ 1) - 1) for i in range(1, count - 1)] + [(0, 0), (count - 1, count - 1)]
    blocks = count // FAR
    far = [(i, i ^ FAR) for i in range(count)] if blocks > 1 else []
    pairs = [cross, near, far]
    if blocks > 2:
        again = [(i, (((i // FAR + 1) ^ 1) - 1) % blocks * FAR + i % FAR) for i in range(count)]
        pairs = [cross, near, far, again]
    return [p for p in pairs if p]


def slots_of(index, count):
    odd = index % 2
    block = index // FAR % 2
    far, again = 2 + block, 3 - block
    if count // FAR > 2:
        return [1 - odd, odd, far, again]
    return [1 - odd, odd, far]


def body(right_side, schur, neumann, weights, neighbours, counts, shared_rows):
    rhs16 = right_side[0]
    rhs = rhs16.astype(jnp.float32)
    s_mat = schur[0]
    n_mat = neumann[0]
    weight = weights[0][:, None]
    count = counts[0]
    width = s_mat.shape[0]
    share = shared_rows.shape[2]
    subs = lax.axis_size("sub")
    routes = swaps(subs)
    slots = slots_of(lax.axis_index("sub"), subs)
    rows = jnp.concatenate([lax.dynamic_index_in_dim(shared_rows[0], k, 0, False) for k in slots])
    live = jnp.concatenate(
        [jnp.broadcast_to(lax.dynamic_index_in_dim(neighbours[0], k, 0, True) >= 0, (share,)) for k in slots]
    )
    mask = (jnp.arange(width) < count).astype(jnp.float32)[:, None]
    hot = (jnp.arange(width)[:, None] == rows[None, :]) & live[None, :]
    placer = hot.astype(jnp.bfloat16)
    picked_weight = jnp.sum(jnp.where(hot, weight, 0.0), 0)[:, None]
    picked_rhs = lax.dot_general(placer, rhs16, (((0,), (0,)), ((), ())), preferred_element_type=jnp.float32)
    picked_s = jnp.dot(s_mat, placer, preferred_element_type=jnp.float32).astype(jnp.bfloat16)
    picked_n = lax.dot_general(
        placer, n_mat, (((0,), (0,)), ((), ())), preferred_element_type=jnp.float32
    ).astype(jnp.bfloat16)
    mask_weight = mask * weight

    def exchange(packed):
        parts = [
            lax.ppermute(packed[k * share : (k + 1) * share], "sub", route) for k, route in enumerate(routes)
        ]
        return jnp.dot(placer, jnp.concatenate(parts, 0), preferred_element_type=jnp.float32)

    def transposed(mat, block):
        return lax.dot_general(mat, block, (((0,), (0,)), ((), ())), preferred_element_type=jnp.float32)

    solution = jnp.zeros(rhs.shape, jnp.float32)
    for step in range(ITERS):
        current = solution.astype(jnp.bfloat16)
        arrived = exchange((picked_rhs - transposed(picked_s, current)).astype(jnp.bfloat16))
        local = mask * (rhs - transposed(s_mat, current))
        scaled = (weight * (local + arrived)).astype(jnp.bfloat16)
        sent = picked_weight * jnp.dot(picked_n, scaled, preferred_element_type=jnp.float32)
        arrived = exchange(sent.astype(jnp.bfloat16))
        weighted = mask_weight * jnp.dot(n_mat, scaled, preferred_element_type=jnp.float32)
        solution = solution + DAMPING * (weighted + arrived)
    return solution[None]


def solution(mesh):
    in_specs = (
        P("sub", None, None),
        P("sub", None, None),
        P("sub", None, None),
        P("sub", None),
        P("sub", None),
        P("sub"),
        P("sub", None, None),
    )
    out_specs = P("sub", None, None)
    return jax.shard_map(body, mesh=mesh, in_specs=in_specs, out_specs=out_specs, check_vma=False)
```

```python
import jax
import jax.numpy as jnp
from jax import lax
from jax.sharding import PartitionSpec as P

ITERS = 4
FAR = 16
DAMPING = 0.7


def swaps(count):
    near = [(i, i ^ 1) for i in range(count)]
    cross = [(i, ((i + 1) ^ 1) - 1) for i in range(count)]
    cross = [(i, j % count) for i, j in cross]
    blocks = count // FAR
    far = [(i, i ^ FAR) for i in range(count)] if blocks > 1 else []
    pairs = [cross, near, far]
    if blocks > 2:
        again = [(i, (((i // FAR + 1) ^ 1) - 1) % blocks * FAR + i % FAR) for i in range(count)]
        pairs = [cross, near, far, again]
    return [p for p in pairs if p]


def slots_of(index, count):
    odd = index % 2
    block = index // FAR % 2
    far, again = 2 + block, 3 - block
    if count // FAR > 2:
        return [1 - odd, odd, far, again]
    return [1 - odd, odd, far]


def body(right_side, schur, neumann, weights, neighbours, counts, shared_rows):
    rhs16 = right_side[0]
    rhs = rhs16.astype(jnp.float32)
    s_mat = schur[0]
    n_mat = neumann[0]
    weight = weights[0][:, None]
    count = counts[0]
    width = s_mat.shape[0]
    share = shared_rows.shape[2]
    subs = lax.axis_size("sub")
    routes = swaps(subs)
    slots = slots_of(lax.axis_index("sub"), subs)
    rows = jnp.concatenate([lax.dynamic_index_in_dim(shared_rows[0], k, 0, False) for k in slots])
    live = jnp.concatenate(
        [jnp.broadcast_to(lax.dynamic_index_in_dim(neighbours[0], k, 0, True) >= 0, (share,)) for k in slots]
    )
    mask = (jnp.arange(width) < count).astype(jnp.float32)[:, None]
    hot = (jnp.arange(width)[:, None] == rows[None, :]) & live[None, :]
    placer = hot.astype(jnp.bfloat16)
    picked_weight = jnp.sum(jnp.where(hot, weight, 0.0), 0)[:, None]

    def transposed(mat, block):
        return lax.dot_general(mat, block, (((0,), (0,)), ((), ())), preferred_element_type=jnp.float32)

    def times(mat, block):
        return jnp.dot(mat, block, preferred_element_type=jnp.float32)

    def exchange(packed):
        parts = [
            lax.ppermute(packed[k * share : (k + 1) * share], "sub", route) for k, route in enumerate(routes)
        ]
        return jnp.concatenate(parts, 0)

    picked_rhs = transposed(placer, rhs16)
    arrived = exchange(picked_rhs.astype(jnp.bfloat16))

    picked_n = transposed(placer, n_mat).astype(jnp.bfloat16)
    picked_s = times(s_mat, placer).astype(jnp.bfloat16)
    small_n = times(picked_n, placer).astype(jnp.bfloat16)
    small_s = transposed(picked_s, placer).astype(jnp.bfloat16)
    mask_weight = mask * weight

    local = mask * rhs
    solution = jnp.zeros(rhs.shape, jnp.float32)
    for step in range(ITERS):
        if step:
            sent = sent_base - DAMPING * times(small_s, arrived)
            came = arrived
            arrived = exchange(sent.astype(jnp.bfloat16))
            solution = solution + DAMPING * times(placer, came)
            local = mask * (rhs - transposed(s_mat, solution.astype(jnp.bfloat16)))
        sent_base = picked_weight * times(picked_n, (weight * local).astype(jnp.bfloat16))
        sent = sent_base + picked_weight * times(small_n, (picked_weight * arrived).astype(jnp.bfloat16))
        came = arrived
        arrived = exchange(sent.astype(jnp.bfloat16))
        scaled = (weight * (local + times(placer, came))).astype(jnp.bfloat16)
        solution = solution + DAMPING * (mask_weight * times(n_mat, scaled))
        if step < ITERS - 1:
            sent_base = picked_rhs - transposed(picked_s, solution.astype(jnp.bfloat16))
    return (solution + DAMPING * times(placer, arrived))[None]


def solution(mesh):
    in_specs = (
        P("sub", None, None),
        P("sub", None, None),
        P("sub", None, None),
        P("sub", None),
        P("sub", None),
        P("sub"),
        P("sub", None, None),
    )
    out_specs = P("sub", None, None)
    return jax.shard_map(body, mesh=mesh, in_specs=in_specs, out_specs=out_specs, check_vma=False)
```

```python
import functools

import jax
import jax.numpy as jnp
from jax import lax
from jax.experimental import pallas as pl
from jax.experimental.pallas import tpu as pltpu
from jax.sharding import PartitionSpec as P

ITERS = 4
FAR = 16
DAMPING = 0.7
LIMIT = 16 * 2**20
F32 = jnp.float32
BF16 = jnp.bfloat16


def swaps(count):
    near = [(i, i ^ 1) for i in range(count)]
    cross = [(i, (((i + 1) ^ 1) - 1) % count) for i in range(count)]
    blocks = count // FAR
    far = [(i, i ^ FAR) for i in range(count)] if blocks > 1 else []
    again = [(i, (((i // FAR + 1) ^ 1) - 1) % blocks * FAR + i % FAR) for i in range(count)] if blocks > 2 else []
    return [pairs for pairs in (cross, near, far, again) if pairs]


def slots_of(index, count):
    odd = lax.rem(index, 2)
    block = lax.rem(lax.div(index, FAR), 2)
    slots = [1 - odd, odd, 2 + block, 3 - block]
    return slots[: 2 + (count // FAR > 1) + (count // FAR > 2)]


def times(a, b):
    return jnp.dot(a, b, preferred_element_type=F32)


def times_t(a, b):
    return lax.dot_general(a, b, (((1,), (1,)), ((), ())), preferred_element_type=F32)


def gather(refs):
    return jnp.concatenate([ref[...] for ref in refs], 1)


def scatter(refs, block):
    share = refs[0].shape[1]
    for k, ref in enumerate(refs):
        ref[...] = block[:, k * share : (k + 1) * share].astype(ref.dtype)


def open_kernel(subs, links, rows_ref, live_ref, rhs_ref, hot_ref, turned_ref, picked_ref, *out_refs):
    width, share = rhs_ref.shape[1], rows_ref.shape[2]
    slots = slots_of(lax.axis_index("sub"), subs)
    place = lax.broadcasted_iota(jnp.int32, (width, share), 0)
    turned = rhs_ref[0].T
    turned_ref[...] = turned
    for k, slot in enumerate(slots):
        row = jnp.where(live_ref[0, slot] >= 0, rows_ref[0, pl.ds(slot, 1), :], -1)
        hot = jnp.where(place == row, 1.0, 0.0).astype(BF16)
        part = pl.ds(k * share, share)
        hot_ref[:, part] = hot
        message = times(turned, hot).astype(BF16)
        picked_ref[:, part] = message
        out_refs[k][...] = message


def pick_n_kernel(
    hot_ref, turned_ref, n_ref, weight_ref, count_ref, n_pick_ref, n_small_ref, same_ref, inner_ref, mask_ref, local_ref, base_ref, first_ref, chosen_ref
):
    hot = hot_ref[...]
    width, total = hot.shape
    weight = weight_ref[...]
    hot_t = hot.T
    n_pick = times(hot_t, n_ref[0]).astype(BF16)
    n_pick_ref[...] = n_pick
    same = times(hot_t, hot)
    same_ref[...] = same.astype(BF16)
    earlier = lax.broadcasted_iota(jnp.int32, same.shape, 0) < lax.broadcasted_iota(jnp.int32, same.shape, 1)
    repeats = jnp.sum(jnp.where(earlier, same, 0.0), 0, keepdims=True)
    first = jnp.where(repeats > 0.0, 0.0, 1.0)
    first_ref[...] = jnp.broadcast_to(first, first_ref.shape)
    n_small_ref[...] = (times(n_pick, hot) * first).astype(BF16)
    hits = times_t(jnp.ones((8, total), BF16), hot)[:1]
    inner = jnp.where(hits > 0.0, 0.0, 1.0)
    inner_ref[...] = jnp.broadcast_to(inner, inner_ref.shape)
    place = lax.broadcasted_iota(jnp.int32, (1, width), 1)
    mask = jnp.where(place < count_ref[0], 1.0, 0.0)
    mask_ref[...] = jnp.broadcast_to(mask, mask_ref.shape)
    high = weight.astype(BF16)
    rest = weight - high.astype(F32)
    middle = rest.astype(BF16)
    low = (rest - middle.astype(F32)).astype(BF16)
    pieces = [times(jnp.broadcast_to(piece, (8, width)), hot) for piece in (high, middle, low)]
    chosen = (pieces[0] + pieces[1]) + pieces[2]
    chosen_ref[...] = chosen
    local = mask * turned_ref[...].astype(F32)
    local_ref[...] = local
    base_ref[...] = times_t((weight * local * inner).astype(BF16), n_pick)


def update_path_kernel(links, *refs):
    arrived_refs, refs = refs[:links], refs[links:]
    same_ref, n_small_ref, chosen_ref, local_ref, base_ref, state_ref, state_out_ref = refs[:7]
    chosen = chosen_ref[:1]
    residual = local_ref[...].astype(F32) + times(gather(arrived_refs), same_ref[...])
    scaled = (chosen * residual).astype(BF16)
    sent = chosen * (base_ref[...] + times_t(scaled, n_small_ref[...]))
    scatter(refs[7:], sent)
    state_out_ref[...] = state_ref[...] + DAMPING * sent


def first_update_path_kernel(links, *refs):
    arrived_refs, refs = refs[:links], refs[links:]
    same_ref, n_small_ref, chosen_ref, local_ref, base_ref, state_out_ref = refs[:6]
    chosen = chosen_ref[:1]
    residual = local_ref[...].astype(F32) + times(gather(arrived_refs), same_ref[...])
    scaled = (chosen * residual).astype(BF16)
    sent = chosen * (base_ref[...] + times_t(scaled, n_small_ref[...]))
    scatter(refs[6:], sent)
    state_out_ref[...] = DAMPING * sent


def residual_path_kernel(links, *refs):
    arrived_refs, refs = refs[:links], refs[links:]
    same_ref, s_small_ref, base_ref, state_ref, state_out_ref, local_ref = refs[:6]
    state = state_ref[...] + DAMPING * times(gather(arrived_refs), same_ref[...])
    state_out_ref[...] = state
    local = base_ref[...] - times(state.astype(BF16), s_small_ref[...])
    local_ref[...] = local
    scatter(refs[6:], local)


def corrected(links, arrived_refs, hot_ref, n_ref, weight_ref, mask_ref, local_ref):
    weight = weight_ref[...]
    residual = local_ref[...] + times_t(gather(arrived_refs), hot_ref[...])
    scaled = (weight * residual).astype(BF16)
    return mask_ref[:1] * weight * times_t(scaled, n_ref[0])


def first_update_kernel(links, *refs):
    arrived_refs, refs = refs[:links], refs[links:]
    hot_ref, n_ref, s_ref, weight_ref, mask_ref, inner_ref, first_ref, local_ref, picked_ref = refs[:9]
    state_out_ref, base_ref, s_pick_ref, s_small_ref = refs[9:]
    state = DAMPING * corrected(links, arrived_refs, hot_ref, n_ref, weight_ref, mask_ref, local_ref)
    state_out_ref[...] = state
    hot = hot_ref[...]
    s_pick = times(s_ref[0], hot).astype(BF16)
    s_pick_ref[...] = s_pick
    alone = (hot.astype(F32) * first_ref[:1]).astype(BF16)
    s_small_ref[...] = times(alone.T, s_pick).astype(BF16)
    base_ref[...] = picked_ref[...].astype(F32) - times((state * inner_ref[:1]).astype(BF16), s_pick)


def update_kernel(links, *refs):
    arrived_refs, refs = refs[:links], refs[links:]
    hot_ref, n_ref, weight_ref, mask_ref, inner_ref, local_ref, picked_ref, s_pick_ref, state_ref = refs[:9]
    state_out_ref, base_ref = refs[9:]
    state = state_ref[...] + DAMPING * corrected(links, arrived_refs, hot_ref, n_ref, weight_ref, mask_ref, local_ref)
    state_out_ref[...] = state
    base_ref[...] = picked_ref[...].astype(F32) - times((state * inner_ref[:1]).astype(BF16), s_pick_ref[...])


def last_update_kernel(links, *refs):
    arrived_refs, refs = refs[:links], refs[links:]
    hot_ref, n_ref, weight_ref, mask_ref, local_ref, state_ref, state_out_ref = refs
    state_out_ref[...] = state_ref[...] + DAMPING * corrected(
        links, arrived_refs, hot_ref, n_ref, weight_ref, mask_ref, local_ref
    )


def residual_kernel(links, *refs):
    arrived_refs, refs = refs[:links], refs[links:]
    hot_ref, s_ref, turned_ref, weight_ref, mask_ref, inner_ref, n_pick_ref, state_ref = refs[:8]
    state_out_ref, local_ref, base_ref = refs[8:]
    state = state_ref[...] + DAMPING * times_t(gather(arrived_refs), hot_ref[...])
    state_out_ref[...] = state
    local = mask_ref[:1] * (turned_ref[...].astype(F32) - times(state.astype(BF16), s_ref[0]))
    local_ref[...] = local
    base_ref[...] = times_t((weight_ref[...] * local * inner_ref[:1]).astype(BF16), n_pick_ref[...])


def close_kernel(links, *refs):
    arrived_refs, (hot_ref, state_ref, out_ref) = refs[:links], refs[links:]
    state = state_ref[...] + DAMPING * times_t(gather(arrived_refs), hot_ref[...])
    out_ref[0] = state.T


def run(kernel, operands, results, flops, scalars=()):
    specs = [
        pl.BlockSpec(memory_space=pltpu.SMEM if k in scalars else pltpu.VMEM) for k in range(len(operands))
    ]
    moved = sum(a.size * a.dtype.itemsize for a in (*operands, *results))
    return pl.pallas_call(
        kernel,
        out_shape=results,
        in_specs=specs,
        out_specs=[pl.BlockSpec(memory_space=pltpu.VMEM)] * len(results),
        compiler_params=pltpu.CompilerParams(vmem_limit_bytes=LIMIT),
        cost_estimate=pl.CostEstimate(flops=flops, bytes_accessed=moved, transcendentals=0),
    )(*operands)


def body(right_side, schur, neumann, weights, neighbours, counts, shared_rows):
    width, leads = right_side.shape[1:]
    share = shared_rows.shape[2]
    subs = lax.axis_size("sub")
    routes = swaps(subs)
    links = len(routes)
    total = links * share

    def array(rows, columns, kind=F32):
        return jax.ShapeDtypeStruct((rows, columns), kind)

    messages = [array(leads, share, BF16)] * links
    full, some = array(leads, width), array(leads, total)
    small = array(total, total, BF16)
    row = array(8, width)
    picks = 2 * leads * total * width
    whole = 2 * leads * width * width
    path = 4 * leads * total * total

    def exchange(parts):
        return [lax.ppermute(part, "sub", route) for part, route in zip(parts, routes)]

    hot, turned, picked, *sent = run(
        functools.partial(open_kernel, subs, links),
        [shared_rows, neighbours, right_side],
        [array(width, total, BF16), array(leads, width, BF16), array(leads, total, BF16), *messages],
        picks,
        scalars=(1,),
    )
    arrived = exchange(sent)
    n_pick, n_small, same, inner, mask, local, base, first, chosen = run(
        pick_n_kernel,
        [hot, turned, neumann, weights, counts],
        [array(total, width, BF16), small, small, row, row, full, some, array(8, total), array(8, total)],
        2 * total * width * width + 4 * total * total * width + picks,
        scalars=(4,),
    )
    near = picked
    for step in range(ITERS):
        came = arrived
        if step == 0:
            near_state, *sent = run(
                functools.partial(first_update_path_kernel, links),
                [*came, same, n_small, chosen, near, base],
                [some, *messages],
                path,
            )
        else:
            near_state, *sent = run(
                functools.partial(update_path_kernel, links),
                [*came, same, n_small, chosen, near, base, near_state],
                [some, *messages],
                path,
            )
        arrived = exchange(sent)
        if step == 0:
            state, base, s_pick, s_small = run(
                functools.partial(first_update_kernel, links),
                [*came, hot, neumann, schur, weights, mask, inner, first, local, picked],
                [full, some, array(width, total, BF16), small],
                whole + 2 * picks + 2 * total * width * (width + total),
            )
        elif step < ITERS - 1:
            state, base = run(
                functools.partial(update_kernel, links),
                [*came, hot, neumann, weights, mask, inner, local, picked, s_pick, state],
                [full, some],
                whole + 2 * picks,
            )
        else:
            (state,) = run(
                functools.partial(last_update_kernel, links),
                [*came, hot, neumann, weights, mask, local, state],
                [full],
                whole + picks,
            )
            break
        came = arrived
        near_state, near, *sent = run(
            functools.partial(residual_path_kernel, links),
            [*came, same, s_small, base, near_state],
            [some, some, *messages],
            path,
        )
        arrived = exchange(sent)
        state, local, base = run(
            functools.partial(residual_kernel, links),
            [*came, hot, schur, turned, weights, mask, inner, n_pick, state],
            [full, full, some],
            whole + 2 * picks,
        )
    (out,) = run(
        functools.partial(close_kernel, links),
        [*arrived, hot, state],
        [jax.ShapeDtypeStruct((1, width, leads), F32)],
        picks,
    )
    return out


def solution(mesh):
    in_specs = (
        P("sub", None, None),
        P("sub", None, None),
        P("sub", None, None),
        P("sub", None),
        P("sub", None),
        P("sub"),
        P("sub", None, None),
    )
    out_specs = P("sub", None, None)
    return jax.shard_map(body, mesh=mesh, in_specs=in_specs, out_specs=out_specs, check_vma=False)
```

```python
import functools

import jax
import jax.numpy as jnp
from jax import lax
from jax.experimental import pallas as pl
from jax.experimental.pallas import tpu as pltpu
from jax.sharding import PartitionSpec as P

ITERS = 4
FAR = 16
DAMPING = 0.7
LIMIT = 16 * 2**20
F32 = jnp.float32
BF16 = jnp.bfloat16


TURNS = (1, 5, 9, 13)


def swaps(count):
    blocks = count // FAR
    near = [i ^ 1 for i in range(count)]
    far = [i ^ FAR for i in range(count)]
    if blocks != 2:
        cross = [(((i + 1) ^ 1) - 1) % count for i in range(count)]
        again = [(((i // FAR + 1) ^ 1) - 1) % blocks * FAR + i % FAR for i in range(count)]
        pairings = [far, again, cross, near] if blocks > 2 else [cross, near]
    else:
        split = [[None] * count, [None] * count]
        for i in range(1, count - 1):
            split[cross_half(i)][i] = ((i + 1) ^ 1) - 1
        for half in split:
            free = [i for i in range(count) if half[i] is None]
            alone = [i for i in free if i ^ 1 not in free]
            mates = dict(zip(alone[::2], alone[1::2])) | dict(zip(alone[1::2], alone[::2]))
            for i in free:
                half[i] = mates.get(i, i ^ 1)
        pairings = [far, *split, near]
    return [list(enumerate(pairing)) for pairing in pairings]


def cross_half(index):
    edge = (index - 1) // 2 if isinstance(index, int) else lax.div(index - 1, 2)
    half = 0
    for turn in TURNS:
        half = half + (edge >= turn) * 1 if isinstance(index, int) else half + jnp.where(edge >= turn, 1, 0)
    return half % 2 if isinstance(index, int) else lax.rem(half, 2)


def slots_of(index, count):
    odd = lax.rem(index, 2)
    block = lax.rem(lax.div(index, FAR), 2)
    blocks = count // FAR
    far = [2 + block] if blocks > 1 else []
    again = [3 - block] if blocks > 2 else []
    return [*far, *again, 1 - odd, odd]


def times(a, b):
    return jnp.dot(a, b, preferred_element_type=F32)


def times_t(a, b):
    return lax.dot_general(a, b, (((1,), (1,)), ((), ())), preferred_element_type=F32)


def gather(links, refs):
    parts = [ref[...] for ref in refs]
    if len(parts) > links:
        half = cross_half(lax.axis_index("sub"))
        mine = jnp.where(half == 0, parts[1].astype(F32), parts[2].astype(F32))
        parts[1:3] = [mine.astype(BF16)]
    return jnp.concatenate(parts, 1)


def scatter(links, refs, block):
    share = refs[0].shape[1]
    columns = [0, 1, 1, 2] if len(refs) > links else range(links)
    for k, ref in zip(columns, refs):
        ref[...] = block[:, k * share : (k + 1) * share].astype(ref.dtype)


def open_kernel(subs, links, rows_ref, live_ref, rhs_ref, hot_ref, turned_ref, picked_ref, *out_refs):
    width, share = rhs_ref.shape[1], rows_ref.shape[2]
    slots = slots_of(lax.axis_index("sub"), subs)
    place = lax.broadcasted_iota(jnp.int32, (width, share), 0)
    turned = rhs_ref[0].T
    turned_ref[...] = turned
    for k, slot in enumerate(slots):
        row = jnp.where(live_ref[0, slot] >= 0, rows_ref[0, pl.ds(slot, 1), :], -1)
        hot = jnp.where(place == row, 1.0, 0.0).astype(BF16)
        part = pl.ds(k * share, share)
        hot_ref[:, part] = hot
        picked_ref[:, part] = times(turned, hot).astype(BF16)
    scatter(links, out_refs, picked_ref[...])


def pick_n_kernel(
    hot_ref, turned_ref, n_ref, weight_ref, count_ref, n_pick_ref, n_small_ref, same_ref, inner_ref, mask_ref, local_ref, base_ref, first_ref, chosen_ref
):
    hot = hot_ref[...]
    width, total = hot.shape
    weight = weight_ref[...]
    hot_t = hot.T
    n_pick = times(hot_t, n_ref[0]).astype(BF16)
    n_pick_ref[...] = n_pick
    same = times(hot_t, hot)
    same_ref[...] = same.astype(BF16)
    earlier = lax.broadcasted_iota(jnp.int32, same.shape, 0) < lax.broadcasted_iota(jnp.int32, same.shape, 1)
    repeats = jnp.sum(jnp.where(earlier, same, 0.0), 0, keepdims=True)
    first = jnp.where(repeats > 0.0, 0.0, 1.0)
    first_ref[...] = jnp.broadcast_to(first, first_ref.shape)
    n_small_ref[...] = (times(n_pick, hot) * first).astype(BF16)
    hits = times_t(jnp.ones((8, total), BF16), hot)[:1]
    inner = jnp.where(hits > 0.0, 0.0, 1.0)
    inner_ref[...] = jnp.broadcast_to(inner, inner_ref.shape)
    place = lax.broadcasted_iota(jnp.int32, (1, width), 1)
    mask = jnp.where(place < count_ref[0], 1.0, 0.0)
    mask_ref[...] = jnp.broadcast_to(mask, mask_ref.shape)
    high = weight.astype(BF16)
    rest = weight - high.astype(F32)
    middle = rest.astype(BF16)
    low = (rest - middle.astype(F32)).astype(BF16)
    pieces = [times(jnp.broadcast_to(piece, (8, width)), hot) for piece in (high, middle, low)]
    chosen = (pieces[0] + pieces[1]) + pieces[2]
    chosen_ref[...] = chosen
    local = mask * turned_ref[...].astype(F32)
    local_ref[...] = local
    base_ref[...] = times_t((weight * local * inner).astype(BF16), n_pick)


def update_path_kernel(trips, links, *refs):
    arrived_refs, refs = refs[:trips], refs[trips:]
    same_ref, n_small_ref, chosen_ref, local_ref, base_ref, state_ref, state_out_ref = refs[:7]
    chosen = chosen_ref[:1]
    residual = local_ref[...].astype(F32) + times(gather(links, arrived_refs), same_ref[...])
    scaled = (chosen * residual).astype(BF16)
    sent = chosen * (base_ref[...] + times_t(scaled, n_small_ref[...]))
    scatter(links, refs[7:], sent)
    state_out_ref[...] = state_ref[...] + DAMPING * sent


def first_update_path_kernel(trips, links, *refs):
    arrived_refs, refs = refs[:trips], refs[trips:]
    same_ref, n_small_ref, chosen_ref, local_ref, base_ref, state_out_ref = refs[:6]
    chosen = chosen_ref[:1]
    residual = local_ref[...].astype(F32) + times(gather(links, arrived_refs), same_ref[...])
    scaled = (chosen * residual).astype(BF16)
    sent = chosen * (base_ref[...] + times_t(scaled, n_small_ref[...]))
    scatter(links, refs[6:], sent)
    state_out_ref[...] = DAMPING * sent


def residual_path_kernel(trips, links, *refs):
    arrived_refs, refs = refs[:trips], refs[trips:]
    same_ref, s_small_ref, base_ref, state_ref, state_out_ref, local_ref = refs[:6]
    state = state_ref[...] + DAMPING * times(gather(links, arrived_refs), same_ref[...])
    state_out_ref[...] = state
    local = base_ref[...] - times(state.astype(BF16), s_small_ref[...])
    local_ref[...] = local
    scatter(links, refs[6:], local)


def corrected(links, arrived_refs, hot_ref, n_ref, weight_ref, mask_ref, local_ref):
    weight = weight_ref[...]
    residual = local_ref[...] + times_t(gather(links, arrived_refs), hot_ref[...])
    scaled = (weight * residual).astype(BF16)
    return mask_ref[:1] * weight * times_t(scaled, n_ref[0])


def first_update_kernel(trips, links, *refs):
    arrived_refs, refs = refs[:trips], refs[trips:]
    hot_ref, n_ref, s_ref, weight_ref, mask_ref, inner_ref, first_ref, local_ref, picked_ref = refs[:9]
    state_out_ref, base_ref, s_pick_ref, s_small_ref = refs[9:]
    state = DAMPING * corrected(links, arrived_refs, hot_ref, n_ref, weight_ref, mask_ref, local_ref)
    state_out_ref[...] = state
    hot = hot_ref[...]
    s_pick = times(s_ref[0], hot).astype(BF16)
    s_pick_ref[...] = s_pick
    alone = (hot.astype(F32) * first_ref[:1]).astype(BF16)
    s_small_ref[...] = times(alone.T, s_pick).astype(BF16)
    base_ref[...] = picked_ref[...].astype(F32) - times((state * inner_ref[:1]).astype(BF16), s_pick)


def update_kernel(trips, links, *refs):
    arrived_refs, refs = refs[:trips], refs[trips:]
    hot_ref, n_ref, weight_ref, mask_ref, inner_ref, local_ref, picked_ref, s_pick_ref, state_ref = refs[:9]
    state_out_ref, base_ref = refs[9:]
    state = state_ref[...] + DAMPING * corrected(links, arrived_refs, hot_ref, n_ref, weight_ref, mask_ref, local_ref)
    state_out_ref[...] = state
    base_ref[...] = picked_ref[...].astype(F32) - times((state * inner_ref[:1]).astype(BF16), s_pick_ref[...])


def last_update_kernel(trips, links, *refs):
    arrived_refs, refs = refs[:trips], refs[trips:]
    hot_ref, n_ref, weight_ref, mask_ref, local_ref, state_ref, state_out_ref = refs
    state_out_ref[...] = state_ref[...] + DAMPING * corrected(
        links, arrived_refs, hot_ref, n_ref, weight_ref, mask_ref, local_ref
    )


def residual_kernel(trips, links, *refs):
    arrived_refs, refs = refs[:trips], refs[trips:]
    hot_ref, s_ref, turned_ref, weight_ref, mask_ref, inner_ref, n_pick_ref, state_ref = refs[:8]
    state_out_ref, local_ref, base_ref = refs[8:]
    state = state_ref[...] + DAMPING * times_t(gather(links, arrived_refs), hot_ref[...])
    state_out_ref[...] = state
    local = mask_ref[:1] * (turned_ref[...].astype(F32) - times(state.astype(BF16), s_ref[0]))
    local_ref[...] = local
    base_ref[...] = times_t((weight_ref[...] * local * inner_ref[:1]).astype(BF16), n_pick_ref[...])


def close_kernel(trips, links, *refs):
    arrived_refs, (hot_ref, state_ref, out_ref) = refs[:trips], refs[trips:]
    state = state_ref[...] + DAMPING * times_t(gather(links, arrived_refs), hot_ref[...])
    out_ref[0] = state.T


def run(kernel, operands, results, flops, scalars=()):
    specs = [
        pl.BlockSpec(memory_space=pltpu.SMEM if k in scalars else pltpu.VMEM) for k in range(len(operands))
    ]
    moved = sum(a.size * a.dtype.itemsize for a in (*operands, *results))
    return pl.pallas_call(
        kernel,
        out_shape=results,
        in_specs=specs,
        out_specs=[pl.BlockSpec(memory_space=pltpu.VMEM)] * len(results),
        compiler_params=pltpu.CompilerParams(vmem_limit_bytes=LIMIT),
        cost_estimate=pl.CostEstimate(flops=flops, bytes_accessed=moved, transcendentals=0),
    )(*operands)


def body(right_side, schur, neumann, weights, neighbours, counts, shared_rows):
    width, leads = right_side.shape[1:]
    share = shared_rows.shape[2]
    subs = lax.axis_size("sub")
    routes = swaps(subs)
    trips = len(routes)
    links = len(slots_of(0, subs))
    total = links * share

    def array(rows, columns, kind=F32):
        return jax.ShapeDtypeStruct((rows, columns), kind)

    messages = [array(leads, share, BF16)] * trips
    full, some = array(leads, width), array(leads, total)
    small = array(total, total, BF16)
    row = array(8, width)
    picks = 2 * leads * total * width
    whole = 2 * leads * width * width
    path = 4 * leads * total * total

    def exchange(parts):
        return [lax.ppermute(part, "sub", route) for part, route in zip(parts, routes)]

    hot, turned, picked, *sent = run(
        functools.partial(open_kernel, subs, links),
        [shared_rows, neighbours, right_side],
        [array(width, total, BF16), array(leads, width, BF16), array(leads, total, BF16), *messages],
        picks,
        scalars=(1,),
    )
    arrived = exchange(sent)
    n_pick, n_small, same, inner, mask, local, base, first, chosen = run(
        pick_n_kernel,
        [hot, turned, neumann, weights, counts],
        [array(total, width, BF16), small, small, row, row, full, some, array(8, total), array(8, total)],
        2 * total * width * width + 4 * total * total * width + picks,
        scalars=(4,),
    )
    near = picked
    for step in range(ITERS):
        came = arrived
        if step == 0:
            near_state, *sent = run(
                functools.partial(first_update_path_kernel, trips, links),
                [*came, same, n_small, chosen, near, base],
                [some, *messages],
                path,
            )
        else:
            near_state, *sent = run(
                functools.partial(update_path_kernel, trips, links),
                [*came, same, n_small, chosen, near, base, near_state],
                [some, *messages],
                path,
            )
        arrived = exchange(sent)
        if step == 0:
            state, base, s_pick, s_small = run(
                functools.partial(first_update_kernel, trips, links),
                [*came, hot, neumann, schur, weights, mask, inner, first, local, picked],
                [full, some, array(width, total, BF16), small],
                whole + 2 * picks + 2 * total * width * (width + total),
            )
        elif step < ITERS - 1:
            state, base = run(
                functools.partial(update_kernel, trips, links),
                [*came, hot, neumann, weights, mask, inner, local, picked, s_pick, state],
                [full, some],
                whole + 2 * picks,
            )
        else:
            (state,) = run(
                functools.partial(last_update_kernel, trips, links),
                [*came, hot, neumann, weights, mask, local, state],
                [full],
                whole + picks,
            )
            break
        came = arrived
        near_state, near, *sent = run(
            functools.partial(residual_path_kernel, trips, links),
            [*came, same, s_small, base, near_state],
            [some, some, *messages],
            path,
        )
        arrived = exchange(sent)
        state, local, base = run(
            functools.partial(residual_kernel, trips, links),
            [*came, hot, schur, turned, weights, mask, inner, n_pick, state],
            [full, full, some],
            whole + 2 * picks,
        )
    (out,) = run(
        functools.partial(close_kernel, trips, links),
        [*arrived, hot, state],
        [jax.ShapeDtypeStruct((1, width, leads), F32)],
        picks,
    )
    return out


def solution(mesh):
    in_specs = (
        P("sub", None, None),
        P("sub", None, None),
        P("sub", None, None),
        P("sub", None),
        P("sub", None),
        P("sub"),
        P("sub", None, None),
    )
    out_specs = P("sub", None, None)
    return jax.shard_map(body, mesh=mesh, in_specs=in_specs, out_specs=out_specs, check_vma=False)
```

```python
import functools

import jax
import jax.numpy as jnp
from jax import lax
from jax.experimental import pallas as pl
from jax.experimental.pallas import tpu as pltpu
from jax.sharding import PartitionSpec as P

ITERS = 4
FAR = 16
DAMPING = 0.7
LIMIT = 16 * 2**20
PIECES = 4
F32 = jnp.float32
BF16 = jnp.bfloat16


TURNS = (1, 5, 9, 13)


def swaps(count):
    blocks = count // FAR
    near = [i ^ 1 for i in range(count)]
    far = [i ^ FAR for i in range(count)]
    if blocks != 2:
        cross = [(((i + 1) ^ 1) - 1) % count for i in range(count)]
        again = [(((i // FAR + 1) ^ 1) - 1) % blocks * FAR + i % FAR for i in range(count)]
        pairings = [far, again, cross, near] if blocks > 2 else [cross, near]
    else:
        split = [[None] * count, [None] * count]
        for i in range(1, count - 1):
            split[cross_half(i)][i] = ((i + 1) ^ 1) - 1
        for half in split:
            free = [i for i in range(count) if half[i] is None]
            alone = [i for i in free if i ^ 1 not in free]
            mates = dict(zip(alone[::2], alone[1::2])) | dict(zip(alone[1::2], alone[::2]))
            for i in free:
                half[i] = mates.get(i, i ^ 1)
        pairings = [far, *split, near]
    return [list(enumerate(pairing)) for pairing in pairings]


def cross_half(index):
    edge = (index - 1) // 2 if isinstance(index, int) else lax.div(index - 1, 2)
    half = 0
    for turn in TURNS:
        half = half + (edge >= turn) * 1 if isinstance(index, int) else half + jnp.where(edge >= turn, 1, 0)
    return half % 2 if isinstance(index, int) else lax.rem(half, 2)


def slots_of(index, count):
    odd = lax.rem(index, 2)
    block = lax.rem(lax.div(index, FAR), 2)
    blocks = count // FAR
    far = [2 + block] if blocks > 1 else []
    again = [3 - block] if blocks > 2 else []
    return [*far, *again, 1 - odd, odd]


def times(a, b):
    return jnp.dot(a, b, preferred_element_type=F32)


def times_t(a, b):
    return lax.dot_general(a, b, (((1,), (1,)), ((), ())), preferred_element_type=F32)


def gather(links, refs):
    parts = [ref[...] for ref in refs]
    if len(parts) > links:
        half = cross_half(lax.axis_index("sub"))
        mine = jnp.where(half == 0, parts[1].astype(F32), parts[2].astype(F32))
        parts[1:3] = [mine.astype(BF16)]
    return jnp.concatenate(parts, 1)


def scatter(links, refs, block):
    share = refs[0].shape[1]
    columns = [0, 1, 1, 2] if len(refs) > links else range(links)
    for k, ref in zip(columns, refs):
        ref[...] = block[:, k * share : (k + 1) * share].astype(ref.dtype)


def open_kernel(
    trips,
    links,
    subs,
    rows_in,
    near_in,
    rhs_in,
    weight_in,
    n_in,
    s_in,
    hot_ref,
    turned_ref,
    picked_ref,
    weight_ref,
    n_ref,
    s_ref,
    *refs,
):
    out_refs, (rows_ref, near_ref, rhs_ref, sems) = refs[:trips], refs[trips:]
    pairs = [
        (rows_in, rows_ref),
        (near_in, near_ref),
        (rhs_in, rhs_ref),
        (weight_in, weight_ref),
        (n_in, n_ref),
        (s_in, s_ref),
    ]
    copies = [pltpu.make_async_copy(source, target, sems.at[k]) for k, (source, target) in enumerate(pairs)]
    for copy in copies:
        copy.start()
    width, share = rhs_ref.shape[1], rows_ref.shape[2]
    slots = slots_of(lax.axis_index("sub"), subs)
    place = lax.broadcasted_iota(jnp.int32, (width, share), 0)
    copies[0].wait()
    copies[1].wait()
    near = near_ref[...].astype(F32)
    lane = lax.broadcasted_iota(jnp.int32, near.shape, 1)
    for k, slot in enumerate(slots):
        partner = jnp.sum(jnp.where(lane == slot, near, 0.0), 1, keepdims=True)
        row = jnp.where(partner >= 0.0, rows_ref[0, pl.ds(slot, 1), :], -1)
        hot_ref[:, pl.ds(k * share, share)] = jnp.where(place == row, 1.0, 0.0).astype(BF16)
    copies[2].wait()
    turned = rhs_ref[0].T
    turned_ref[...] = turned
    picked = times(turned, hot_ref[...]).astype(BF16)
    picked_ref[...] = picked
    scatter(links, out_refs, picked)
    for copy in copies[3:]:
        copy.wait()


def pick_n_kernel(
    hot_ref,
    turned_ref,
    n_ref,
    weight_ref,
    count_ref,
    hot_t_ref,
    n_pick_ref,
    n_small_ref,
    same_ref,
    inner_ref,
    mask_ref,
    local_ref,
    base_ref,
    row_ref,
):
    hot = hot_ref[...]
    width, total = hot.shape
    weight = weight_ref[...]
    hot_t = hot.T
    hot_t_ref[...] = hot_t
    n_pick = times(hot_t, n_ref[0]).astype(BF16)
    n_pick_ref[...] = n_pick
    n_small_ref[...] = times(n_pick, hot).astype(BF16)
    same = times(hot_t, hot)
    same_ref[...] = same.astype(BF16)
    earlier = lax.broadcasted_iota(jnp.int32, same.shape, 0) < lax.broadcasted_iota(jnp.int32, same.shape, 1)
    repeats = jnp.sum(jnp.where(earlier, same, 0.0), 0, keepdims=True)
    first = jnp.where(repeats > 0.0, 0.0, 1.0)
    hits = jnp.sum(hot_t.astype(F32), 0, keepdims=True)
    inner = jnp.where(hits > 0.0, 0.0, 1.0)
    inner_ref[...] = jnp.broadcast_to(inner, inner_ref.shape)
    high = weight.astype(BF16).astype(F32)
    middle = (weight - high).astype(BF16).astype(F32)
    low = weight - high - middle
    level = lax.broadcasted_iota(jnp.int32, (8, width), 0)
    pieces = jnp.where(level == 0, high, jnp.where(level == 1, middle, jnp.where(level == 2, low, 0.0)))
    pieces = times(pieces.astype(BF16), hot)
    chosen = (pieces[0:1] + pieces[1:2]) + pieces[2:3]
    row_ref[0:1] = chosen
    row_ref[1:2] = chosen * first
    row_ref[2:3] = first
    row_ref[3:8] = jnp.zeros((5, total), F32)
    mask = jnp.where(lax.broadcasted_iota(jnp.int32, mask_ref.shape, 1) < count_ref[0], 1.0, 0.0)
    mask_ref[...] = mask
    local = mask[:1] * turned_ref[...].astype(F32)
    local_ref[...] = local
    base_ref[...] = times_t((weight * local * inner).astype(BF16), n_pick)


def update_path_kernel(trips, links, step, last, *refs):
    arrived_refs, refs = refs[:trips], refs[trips:]
    same_ref, n_small_ref, row_ref, local_ref, base_ref = refs[:5]
    refs = refs[5:]
    residual = local_ref[...].astype(F32) + times(gather(links, arrived_refs), same_ref[...])
    scaled = (row_ref[1:2] * residual).astype(BF16)
    sent = row_ref[0:1] * (base_ref[...] + times_t(scaled, n_small_ref[...]))
    if last:
        scatter(links, refs, sent)
    elif step == 0:
        scatter(links, refs[1:], sent)
        refs[0][...] = DAMPING * sent
    else:
        scatter(links, refs[2:], sent)
        refs[1][...] = refs[0][...] + DAMPING * sent


def residual_path_kernel(trips, links, *refs):
    arrived_refs, refs = refs[:trips], refs[trips:]
    same_ref, s_small_ref, row_ref, base_ref, state_ref, state_out_ref, local_ref = refs[:7]
    state = state_ref[...] + DAMPING * times(gather(links, arrived_refs), same_ref[...])
    state_out_ref[...] = state
    local = base_ref[...] - times((state * row_ref[2:3]).astype(BF16), s_small_ref[...])
    local_ref[...] = local
    scatter(links, refs[7:], local)


def corrected(links, arrived_refs, hot_ref, n_ref, weight_ref, mask_ref, local_ref):
    weight = weight_ref[...]
    residual = local_ref[...] + times_t(gather(links, arrived_refs), hot_ref[...])
    scaled = (weight * residual).astype(BF16)
    return mask_ref[:1] * weight * times_t(scaled, n_ref[0])


def first_update_kernel(trips, links, *refs):
    arrived_refs, refs = refs[:trips], refs[trips:]
    hot_ref, hot_t_ref, n_ref, s_ref, weight_ref, mask_ref, inner_ref, local_ref, picked_ref = refs[:9]
    state_out_ref, base_ref, s_pick_ref, s_small_ref = refs[9:]
    state = DAMPING * corrected(links, arrived_refs, hot_ref, n_ref, weight_ref, mask_ref, local_ref)
    state_out_ref[...] = state
    s_pick = times(s_ref[0], hot_ref[...]).astype(BF16)
    s_pick_ref[...] = s_pick
    s_small_ref[...] = times(hot_t_ref[...], s_pick).astype(BF16)
    base_ref[...] = picked_ref[...].astype(F32) - times((state * inner_ref[:1]).astype(BF16), s_pick)


def update_kernel(trips, links, *refs):
    arrived_refs, refs = refs[:trips], refs[trips:]
    hot_ref, n_ref, weight_ref, mask_ref, inner_ref, local_ref, picked_ref, s_pick_ref, state_ref = refs[:9]
    state_out_ref, base_ref = refs[9:]
    state = state_ref[...] + DAMPING * corrected(links, arrived_refs, hot_ref, n_ref, weight_ref, mask_ref, local_ref)
    state_out_ref[...] = state
    base_ref[...] = picked_ref[...].astype(F32) - times((state * inner_ref[:1]).astype(BF16), s_pick_ref[...])


def last_update_kernel(trips, links, *refs):
    arrived_refs, refs = refs[:trips], refs[trips:]
    hot_ref, n_ref, weight_ref, mask_ref, local_ref, state_ref, state_out_ref = refs
    update = corrected(links, arrived_refs, hot_ref, n_ref, weight_ref, mask_ref, local_ref)
    state_out_ref[...] = (state_ref[...] + DAMPING * update).T


def residual_kernel(trips, links, *refs):
    arrived_refs, refs = refs[:trips], refs[trips:]
    hot_ref, s_ref, turned_ref, weight_ref, mask_ref, inner_ref, n_pick_ref, state_ref = refs[:8]
    state_out_ref, local_ref, base_ref = refs[8:]
    state = state_ref[...] + DAMPING * times_t(gather(links, arrived_refs), hot_ref[...])
    state_out_ref[...] = state
    local = mask_ref[:1] * (turned_ref[...].astype(F32) - times(state.astype(BF16), s_ref[0]))
    local_ref[...] = local
    base_ref[...] = times_t((weight_ref[...] * local * inner_ref[:1]).astype(BF16), n_pick_ref[...])


def close_kernel(trips, links, *refs):
    arrived_refs, (hot_ref, state_ref, out_ref, piece_ref, sems) = refs[:trips], refs[trips:]
    arrived = gather(links, arrived_refs)
    rows = state_ref.shape[0] // PIECES
    copies = []
    for k in range(PIECES):
        part = pl.ds(k * rows, rows)
        piece_ref[part, :] = state_ref[part, :] + DAMPING * times_t(hot_ref[part, :], arrived)
        copies.append(pltpu.make_async_copy(piece_ref.at[part, :], out_ref.at[0, part, :], sems.at[k]))
        copies[k].start()
    for copy in copies:
        copy.wait()


def run(kernel, operands, results, flops, inputs=pltpu.VMEM, outputs=pltpu.VMEM, scalars=(), scratch=()):
    if inputs is pltpu.HBM:
        operands = [pltpu.with_memory_space_constraint(a, inputs) for a in operands]
    moved = sum(a.size * a.dtype.itemsize for a in (*operands, *results))
    return pl.pallas_call(
        kernel,
        out_shape=results,
        in_specs=[pl.BlockSpec(memory_space=pltpu.SMEM if k in scalars else inputs) for k in range(len(operands))],
        out_specs=[pl.BlockSpec(memory_space=outputs)] * len(results),
        scratch_shapes=scratch,
        compiler_params=pltpu.CompilerParams(vmem_limit_bytes=LIMIT),
        cost_estimate=pl.CostEstimate(flops=flops, bytes_accessed=moved, transcendentals=0),
    )(*operands)


def body(right_side, schur, neumann, weights, neighbours, counts, shared_rows):
    width, leads = right_side.shape[1:]
    share = shared_rows.shape[2]
    subs = lax.axis_size("sub")
    routes = swaps(subs)
    trips = len(routes)
    links = len(slots_of(0, subs))
    total = links * share

    def array(rows, columns, kind=F32):
        return jax.ShapeDtypeStruct((rows, columns), kind)

    def same_as(a):
        return jax.ShapeDtypeStruct(a.shape, a.dtype)

    messages = [array(leads, share, BF16)] * trips
    full, some = array(leads, width), array(leads, total)
    small = array(total, total, BF16)
    row = array(8, width)
    picks = 2 * leads * total * width
    whole = 2 * leads * width * width
    path = 4 * leads * total * total

    def exchange(parts):
        return [lax.ppermute(part, "sub", route) for part, route in zip(parts, routes)]

    def bound(kernel, *settings):
        return functools.partial(kernel, trips, links, *settings)

    hot, turned, picked, weight, n_mat, s_mat, *sent = run(
        bound(open_kernel, subs),
        [shared_rows, neighbours, right_side, weights, neumann, schur],
        [
            array(width, total, BF16),
            array(leads, width, BF16),
            array(leads, total, BF16),
            same_as(weights),
            same_as(neumann),
            same_as(schur),
            *messages,
        ],
        picks,
        inputs=pltpu.HBM,
        scratch=[
            pltpu.VMEM(shared_rows.shape, jnp.int32),
            pltpu.VMEM(neighbours.shape, jnp.int32),
            pltpu.VMEM(right_side.shape, BF16),
            pltpu.SemaphoreType.DMA((6,)),
        ],
    )
    arrived = exchange(sent)
    hot_t, n_pick, n_small, same, inner, mask, local, base, rows = run(
        pick_n_kernel,
        [hot, turned, n_mat, weight, counts],
        [array(total, width, BF16), array(total, width, BF16), small, small, row, row, full, some, array(8, total)],
        2 * total * width * width + 4 * total * total * width + picks,
        scalars=(4,),
    )
    near = picked
    near_state = None
    for step in range(ITERS):
        came, last = arrived, step == ITERS - 1
        operands = [*came, same, n_small, rows, near, base]
        if step and not last:
            operands.append(near_state)
        kernel = bound(update_path_kernel, step, last)
        if last:
            sent = run(kernel, operands, messages, path)
            arrived = exchange(sent)
            (state,) = run(
                bound(last_update_kernel),
                [*came, hot, n_mat, weight, mask, local, state],
                [array(width, leads)],
                whole + picks,
            )
            break
        near_state, *sent = run(kernel, operands, [some, *messages], path)
        arrived = exchange(sent)
        if step == 0:
            state, base, s_pick, s_small = run(
                bound(first_update_kernel),
                [*came, hot, hot_t, n_mat, s_mat, weight, mask, inner, local, picked],
                [full, some, array(width, total, BF16), small],
                whole + 2 * picks + 2 * total * width * (width + total),
            )
        else:
            state, base = run(
                bound(update_kernel),
                [*came, hot, n_mat, weight, mask, inner, local, picked, s_pick, state],
                [full, some],
                whole + 2 * picks,
            )
        came = arrived
        near_state, near, *sent = run(
            bound(residual_path_kernel),
            [*came, same, s_small, rows, base, near_state],
            [some, some, *messages],
            path,
        )
        arrived = exchange(sent)
        state, local, base = run(
            bound(residual_kernel),
            [*came, hot, s_mat, turned, weight, mask, inner, n_pick, state],
            [full, full, some],
            whole + 2 * picks,
        )
    (out,) = run(
        bound(close_kernel),
        [*arrived, hot, state],
        [jax.ShapeDtypeStruct((1, width, leads), F32)],
        picks,
        outputs=pltpu.HBM,
        scratch=[pltpu.VMEM((width, leads), F32), pltpu.SemaphoreType.DMA((PIECES,))],
    )
    return out


def solution(mesh):
    in_specs = (
        P("sub", None, None),
        P("sub", None, None),
        P("sub", None, None),
        P("sub", None),
        P("sub", None),
        P("sub"),
        P("sub", None, None),
    )
    out_specs = P("sub", None, None)
    return jax.shard_map(body, mesh=mesh, in_specs=in_specs, out_specs=out_specs, check_vma=False)
```

```python
import functools

import jax
import jax.numpy as jnp
from jax import lax
from jax.experimental import pallas as pl
from jax.experimental.pallas import tpu as pltpu
from jax.sharding import PartitionSpec as P

ITERS = 4
FAR = 16
DAMPING = 0.7
LIMIT = 16 * 2**20
PIECES = 4
F32 = jnp.float32
BF16 = jnp.bfloat16


FAR_TURNS = (0, 0, 0, 2, 1, 0, 0, 1, 1, 0, 0, 0, 0, 0, 0, 0)
ODD_TURNS = (1, 0, 1, 0, 1, 1, 1, 1, 1, 0, 2, 0, 2, 1, 1)
FILL = ((), ((0, 3), (19, 21), (22, 31), (25, 26)), ((2, 18), (20, 23), (24, 27)))


def turns(count):
    far = [FAR_TURNS[i % FAR] for i in range(count)]
    odd = [ODD_TURNS[(i - 1) // 2] if 0 < i < count - 1 else -1 for i in range(count)]
    return far, odd


def mixed(count):
    return count == 2 * FAR


def swaps(count):
    blocks = count // FAR
    near = [i ^ 1 for i in range(count)]
    far = [i ^ FAR for i in range(count)]
    odd = [(((i + 1) ^ 1) - 1) % count for i in range(count)]
    if mixed(count):
        far_turns, odd_turns = turns(count)
        pairings = []
        for turn, fill in enumerate(FILL):
            pairing = list(near)
            for i, j in fill:
                pairing[i], pairing[j] = j, i
            for i in range(count):
                if far_turns[i] == turn:
                    pairing[i] = far[i]
                elif odd_turns[i] == turn:
                    pairing[i] = odd[i]
            pairings.append(pairing)
        pairings.append(near)
    else:
        again = [(((i // FAR + 1) ^ 1) - 1) % blocks * FAR + i % FAR for i in range(count)]
        pairings = ([far] if blocks > 1 else []) + ([again] if blocks > 2 else []) + [odd, near]
    for pairing in pairings:
        assert all(pairing[j] == i != j for i, j in enumerate(pairing))
    return [list(enumerate(pairing)) for pairing in pairings]


def is_turn(own_turns, turn):
    bits = sum(1 << i for i, own in enumerate(own_turns) if own == turn)
    bits = bits - (1 << 32) if bits >> 31 else bits
    return lax.shift_right_logical(jnp.int32(bits), lax.axis_index("sub")) & 1 == 1


def slots_of(index, count):
    odd = lax.rem(index, 2)
    block = lax.rem(lax.div(index, FAR), 2)
    blocks = count // FAR
    far = [2 + block] if blocks > 1 else []
    again = [3 - block] if blocks > 2 else []
    return [*far, *again, 1 - odd, odd]


def times(a, b):
    return jnp.dot(a, b, preferred_element_type=F32)


def times_t(a, b):
    return lax.dot_general(a, b, (((1,), (1,)), ((), ())), preferred_element_type=F32)


def gather(links, refs):
    parts = [ref[...] for ref in refs]
    if len(parts) > links:
        values = [part.astype(F32) for part in parts[:3]]
        picked = []
        for own in turns(2 * FAR):
            later = jnp.where(is_turn(own, 1), values[1], values[2])
            picked.append(jnp.where(is_turn(own, 0), values[0], later).astype(BF16))
        parts = [*picked, parts[3]]
    return jnp.concatenate(parts, 1)


def scatter(links, refs, block):
    share = refs[0].shape[1]
    parts = [block[:, k * share : (k + 1) * share].astype(F32) for k in range(links)]
    if len(refs) > links:
        far, odd, near = parts
        own, _ = turns(2 * FAR)
        parts = [*(jnp.where(is_turn(own, turn), far, odd) for turn in range(3)), near]
    for ref, part in zip(refs, parts):
        ref[...] = part.astype(BF16)


def open_kernel(
    trips,
    links,
    subs,
    rows_in,
    near_in,
    rhs_in,
    weight_in,
    n_in,
    s_in,
    hot_ref,
    turned_ref,
    picked_ref,
    weight_ref,
    n_ref,
    s_ref,
    *refs,
):
    out_refs, (rows_ref, near_ref, rhs_ref, sems) = refs[:trips], refs[trips:]
    pairs = [
        (rows_in, rows_ref),
        (near_in, near_ref),
        (rhs_in, rhs_ref),
        (weight_in, weight_ref),
        (n_in, n_ref),
        (s_in, s_ref),
    ]
    copies = [pltpu.make_async_copy(source, target, sems.at[k]) for k, (source, target) in enumerate(pairs)]
    for copy in copies:
        copy.start()
    width, share = rhs_ref.shape[1], rows_ref.shape[2]
    slots = slots_of(lax.axis_index("sub"), subs)
    place = lax.broadcasted_iota(jnp.int32, (width, share), 0)
    copies[0].wait()
    copies[1].wait()
    near = near_ref[...].astype(F32)
    lane = lax.broadcasted_iota(jnp.int32, near.shape, 1)
    for k, slot in enumerate(slots):
        partner = jnp.sum(jnp.where(lane == slot, near, 0.0), 1, keepdims=True)
        row = jnp.where(partner >= 0.0, rows_ref[0, pl.ds(slot, 1), :], -1)
        hot_ref[:, pl.ds(k * share, share)] = jnp.where(place == row, 1.0, 0.0).astype(BF16)
    copies[2].wait()
    turned = rhs_ref[0].T
    turned_ref[...] = turned
    picked = times(turned, hot_ref[...]).astype(BF16)
    picked_ref[...] = picked
    scatter(links, out_refs, picked)
    for copy in copies[3:]:
        copy.wait()


def pick_n_kernel(
    hot_ref,
    turned_ref,
    n_ref,
    weight_ref,
    count_ref,
    hot_t_ref,
    n_pick_ref,
    n_small_ref,
    same_ref,
    inner_ref,
    mask_ref,
    local_ref,
    base_ref,
    row_ref,
):
    hot = hot_ref[...]
    width, total = hot.shape
    weight = weight_ref[...]
    hot_t = hot.T
    hot_t_ref[...] = hot_t
    n_pick = times(hot_t, n_ref[0]).astype(BF16)
    n_pick_ref[...] = n_pick
    n_small_ref[...] = times(n_pick, hot).astype(BF16)
    same = times(hot_t, hot)
    same_ref[...] = same.astype(BF16)
    earlier = lax.broadcasted_iota(jnp.int32, same.shape, 0) < lax.broadcasted_iota(jnp.int32, same.shape, 1)
    repeats = jnp.sum(jnp.where(earlier, same, 0.0), 0, keepdims=True)
    first = jnp.where(repeats > 0.0, 0.0, 1.0)
    hits = jnp.sum(hot_t.astype(F32), 0, keepdims=True)
    inner = jnp.where(hits > 0.0, 0.0, 1.0)
    inner_ref[...] = jnp.broadcast_to(inner, inner_ref.shape)
    high = weight.astype(BF16).astype(F32)
    middle = (weight - high).astype(BF16).astype(F32)
    low = weight - high - middle
    level = lax.broadcasted_iota(jnp.int32, (8, width), 0)
    pieces = jnp.where(level == 0, high, jnp.where(level == 1, middle, jnp.where(level == 2, low, 0.0)))
    pieces = times(pieces.astype(BF16), hot)
    chosen = (pieces[0:1] + pieces[1:2]) + pieces[2:3]
    row_ref[0:1] = chosen
    row_ref[1:2] = chosen * first
    row_ref[2:3] = first
    row_ref[3:8] = jnp.zeros((5, total), F32)
    mask = jnp.where(lax.broadcasted_iota(jnp.int32, mask_ref.shape, 1) < count_ref[0], 1.0, 0.0)
    mask_ref[...] = mask
    local = mask[:1] * turned_ref[...].astype(F32)
    local_ref[...] = local
    base_ref[...] = times_t((weight * local * inner).astype(BF16), n_pick)


def update_path_kernel(trips, links, step, last, *refs):
    arrived_refs, refs = refs[:trips], refs[trips:]
    same_ref, n_small_ref, row_ref, local_ref, base_ref = refs[:5]
    refs = refs[5:]
    residual = local_ref[...].astype(F32) + times(gather(links, arrived_refs), same_ref[...])
    scaled = (row_ref[1:2] * residual).astype(BF16)
    sent = row_ref[0:1] * (base_ref[...] + times_t(scaled, n_small_ref[...]))
    if last:
        scatter(links, refs, sent)
    elif step == 0:
        scatter(links, refs[1:], sent)
        refs[0][...] = DAMPING * sent
    else:
        scatter(links, refs[2:], sent)
        refs[1][...] = refs[0][...] + DAMPING * sent


def residual_path_kernel(trips, links, last, *refs):
    arrived_refs, refs = refs[:trips], refs[trips:]
    same_ref, s_small_ref, row_ref, base_ref, state_ref, local_ref = refs[:6]
    state = state_ref[...] + DAMPING * times(gather(links, arrived_refs), same_ref[...])
    if last:
        refs = refs[6:]
    else:
        refs[6][...] = state
        refs = refs[7:]
    local = base_ref[...] - times((state * row_ref[2:3]).astype(BF16), s_small_ref[...])
    local_ref[...] = local
    scatter(links, refs, local)


def corrected(links, arrived_refs, hot_ref, n_ref, weight_ref, mask_ref, local_ref):
    weight = weight_ref[...]
    residual = local_ref[...] + times_t(gather(links, arrived_refs), hot_ref[...])
    scaled = (weight * residual).astype(BF16)
    return mask_ref[:1] * weight * times_t(scaled, n_ref[0])


def first_update_kernel(trips, links, *refs):
    arrived_refs, refs = refs[:trips], refs[trips:]
    hot_ref, hot_t_ref, n_ref, s_ref, weight_ref, mask_ref, inner_ref, local_ref, picked_ref = refs[:9]
    state_out_ref, base_ref, s_pick_ref, s_small_ref = refs[9:]
    state = DAMPING * corrected(links, arrived_refs, hot_ref, n_ref, weight_ref, mask_ref, local_ref)
    state_out_ref[...] = state
    s_pick = times(s_ref[0], hot_ref[...]).astype(BF16)
    s_pick_ref[...] = s_pick
    s_small_ref[...] = times(hot_t_ref[...], s_pick).astype(BF16)
    base_ref[...] = picked_ref[...].astype(F32) - times((state * inner_ref[:1]).astype(BF16), s_pick)


def update_kernel(trips, links, *refs):
    arrived_refs, refs = refs[:trips], refs[trips:]
    hot_ref, n_ref, weight_ref, mask_ref, inner_ref, local_ref, picked_ref, s_pick_ref, state_ref = refs[:9]
    state_out_ref, base_ref = refs[9:]
    state = state_ref[...] + DAMPING * corrected(links, arrived_refs, hot_ref, n_ref, weight_ref, mask_ref, local_ref)
    state_out_ref[...] = state
    base_ref[...] = picked_ref[...].astype(F32) - times((state * inner_ref[:1]).astype(BF16), s_pick_ref[...])


def last_update_kernel(trips, links, *refs):
    arrived_refs, refs = refs[:trips], refs[trips:]
    hot_ref, n_ref, weight_ref, mask_ref, local_ref, state_ref, state_out_ref = refs
    update = corrected(links, arrived_refs, hot_ref, n_ref, weight_ref, mask_ref, local_ref)
    state_out_ref[...] = (state_ref[...] + DAMPING * update).T


def residual_kernel(trips, links, *refs):
    arrived_refs, refs = refs[:trips], refs[trips:]
    hot_ref, s_ref, turned_ref, weight_ref, mask_ref, inner_ref, n_pick_ref, state_ref = refs[:8]
    state_out_ref, local_ref, base_ref = refs[8:]
    state = state_ref[...] + DAMPING * times_t(gather(links, arrived_refs), hot_ref[...])
    state_out_ref[...] = state
    local = mask_ref[:1] * (turned_ref[...].astype(F32) - times(state.astype(BF16), s_ref[0]))
    local_ref[...] = local
    base_ref[...] = times_t((weight_ref[...] * local * inner_ref[:1]).astype(BF16), n_pick_ref[...])


def close_kernel(trips, links, *refs):
    arrived_refs, (hot_ref, state_ref, out_ref, piece_ref, sems) = refs[:trips], refs[trips:]
    arrived = gather(links, arrived_refs)
    rows = state_ref.shape[0] // PIECES
    copies = []
    for k in range(PIECES):
        part = pl.ds(k * rows, rows)
        piece_ref[part, :] = state_ref[part, :] + DAMPING * times_t(hot_ref[part, :], arrived)
        copies.append(pltpu.make_async_copy(piece_ref.at[part, :], out_ref.at[0, part, :], sems.at[k]))
        copies[k].start()
    for copy in copies:
        copy.wait()


def run(kernel, operands, results, flops, inputs=pltpu.VMEM, outputs=pltpu.VMEM, scalars=(), scratch=()):
    if inputs is pltpu.HBM:
        operands = [pltpu.with_memory_space_constraint(a, inputs) for a in operands]
    moved = sum(a.size * a.dtype.itemsize for a in (*operands, *results))
    return pl.pallas_call(
        kernel,
        out_shape=results,
        in_specs=[pl.BlockSpec(memory_space=pltpu.SMEM if k in scalars else inputs) for k in range(len(operands))],
        out_specs=[pl.BlockSpec(memory_space=outputs)] * len(results),
        scratch_shapes=scratch,
        compiler_params=pltpu.CompilerParams(vmem_limit_bytes=LIMIT),
        cost_estimate=pl.CostEstimate(flops=flops, bytes_accessed=moved, transcendentals=0),
    )(*operands)


def body(right_side, schur, neumann, weights, neighbours, counts, shared_rows):
    width, leads = right_side.shape[1:]
    share = shared_rows.shape[2]
    subs = lax.axis_size("sub")
    routes = swaps(subs)
    trips = len(routes)
    links = len(slots_of(0, subs))
    total = links * share

    def array(rows, columns, kind=F32):
        return jax.ShapeDtypeStruct((rows, columns), kind)

    def same_as(a):
        return jax.ShapeDtypeStruct(a.shape, a.dtype)

    messages = [array(leads, share, BF16)] * trips
    full, some = array(leads, width), array(leads, total)
    small = array(total, total, BF16)
    row = array(8, width)
    picks = 2 * leads * total * width
    whole = 2 * leads * width * width
    path = 4 * leads * total * total

    def exchange(parts):
        return [lax.ppermute(part, "sub", route) for part, route in zip(parts, routes)]

    def bound(kernel, *settings):
        return functools.partial(kernel, trips, links, *settings)

    hot, turned, picked, weight, n_mat, s_mat, *sent = run(
        bound(open_kernel, subs),
        [shared_rows, neighbours, right_side, weights, neumann, schur],
        [
            array(width, total, BF16),
            array(leads, width, BF16),
            array(leads, total, BF16),
            same_as(weights),
            same_as(neumann),
            same_as(schur),
            *messages,
        ],
        picks,
        inputs=pltpu.HBM,
        scratch=[
            pltpu.VMEM(shared_rows.shape, jnp.int32),
            pltpu.VMEM(neighbours.shape, jnp.int32),
            pltpu.VMEM(right_side.shape, BF16),
            pltpu.SemaphoreType.DMA((6,)),
        ],
    )
    arrived = exchange(sent)
    hot_t, n_pick, n_small, same, inner, mask, local, base, rows = run(
        pick_n_kernel,
        [hot, turned, n_mat, weight, counts],
        [array(total, width, BF16), array(total, width, BF16), small, small, row, row, full, some, array(8, total)],
        2 * total * width * width + 4 * total * total * width + picks,
        scalars=(4,),
    )
    near = picked
    near_state = None
    for step in range(ITERS):
        came, last = arrived, step == ITERS - 1
        operands = [*came, same, n_small, rows, near, base]
        if step and not last:
            operands.append(near_state)
        kernel = bound(update_path_kernel, step, last)
        if last:
            sent = run(kernel, operands, messages, path)
            arrived = exchange(sent)
            (state,) = run(
                bound(last_update_kernel),
                [*came, hot, n_mat, weight, mask, local, state],
                [array(width, leads)],
                whole + picks,
            )
            break
        near_state, *sent = run(kernel, operands, [some, *messages], path)
        arrived = exchange(sent)
        if step == 0:
            state, base, s_pick, s_small = run(
                bound(first_update_kernel),
                [*came, hot, hot_t, n_mat, s_mat, weight, mask, inner, local, picked],
                [full, some, array(width, total, BF16), small],
                whole + 2 * picks + 2 * total * width * (width + total),
            )
        else:
            state, base = run(
                bound(update_kernel),
                [*came, hot, n_mat, weight, mask, inner, local, picked, s_pick, state],
                [full, some],
                whole + 2 * picks,
            )
        came = arrived
        ends = step == ITERS - 2
        near, *sent = run(
            bound(residual_path_kernel, ends),
            [*came, same, s_small, rows, base, near_state],
            [some, *([] if ends else [some]), *messages],
            path,
        )
        if not ends:
            near_state, *sent = sent
        arrived = exchange(sent)
        state, local, base = run(
            bound(residual_kernel),
            [*came, hot, s_mat, turned, weight, mask, inner, n_pick, state],
            [full, full, some],
            whole + 2 * picks,
        )
    (out,) = run(
        bound(close_kernel),
        [*arrived, hot, state],
        [jax.ShapeDtypeStruct((1, width, leads), F32)],
        picks,
        outputs=pltpu.HBM,
        scratch=[pltpu.VMEM((width, leads), F32), pltpu.SemaphoreType.DMA((PIECES,))],
    )
    return out


def solution(mesh):
    in_specs = (
        P("sub", None, None),
        P("sub", None, None),
        P("sub", None, None),
        P("sub", None),
        P("sub", None),
        P("sub"),
        P("sub", None, None),
    )
    out_specs = P("sub", None, None)
    return jax.shard_map(body, mesh=mesh, in_specs=in_specs, out_specs=out_specs, check_vma=False)
```

```python
import functools

import jax
import jax.numpy as jnp
from jax import lax
from jax.experimental import pallas as pl
from jax.experimental.pallas import tpu as pltpu
from jax.sharding import PartitionSpec as P

ITERS = 4
FAR = 16
DAMPING = 0.7
LIMIT = 16 * 2**20
PIECES = 4
F32 = jnp.float32
BF16 = jnp.bfloat16


FAR_TURNS = (0, 0, 0, 0, 0, 2, 1, 1, 1, 0, 0, 0, 0, 0, 1, 2)
ODD_TURNS = (1, 1, 0, 0, 1, 1, 2, 1, 1, 1, 0, 0, 1, 1, 2)
FILL = ((), ((0, 5), (13, 21), (29, 31)), ((4, 12), (20, 28)))


def turns(count):
    far = [FAR_TURNS[i % FAR] for i in range(count)]
    odd = [ODD_TURNS[(i - 1) // 2] if 0 < i < count - 1 else -1 for i in range(count)]
    return far, odd


def mixed(count):
    return count == 2 * FAR


def swaps(count):
    blocks = count // FAR
    near = [i ^ 1 for i in range(count)]
    far = [i ^ FAR for i in range(count)]
    odd = [(((i + 1) ^ 1) - 1) % count for i in range(count)]
    if mixed(count):
        far_turns, odd_turns = turns(count)
        pairings = []
        for turn, fill in enumerate(FILL):
            pairing = list(near)
            for i, j in fill:
                pairing[i], pairing[j] = j, i
            for i in range(count):
                if far_turns[i] == turn:
                    pairing[i] = far[i]
                elif odd_turns[i] == turn:
                    pairing[i] = odd[i]
            pairings.append(pairing)
        pairings.append(near)
    else:
        again = [(((i // FAR + 1) ^ 1) - 1) % blocks * FAR + i % FAR for i in range(count)]
        pairings = ([far] if blocks > 1 else []) + ([again] if blocks > 2 else []) + [odd, near]
    for pairing in pairings:
        assert all(pairing[j] == i != j for i, j in enumerate(pairing))
    return [list(enumerate(pairing)) for pairing in pairings]


def is_turn(own_turns, turn):
    bits = sum(1 << i for i, own in enumerate(own_turns) if own == turn)
    bits = bits - (1 << 32) if bits >> 31 else bits
    return lax.shift_right_logical(jnp.int32(bits), lax.axis_index("sub")) & 1 == 1


def slots_of(index, count):
    odd = lax.rem(index, 2)
    block = lax.rem(lax.div(index, FAR), 2)
    blocks = count // FAR
    far = [2 + block] if blocks > 1 else []
    again = [3 - block] if blocks > 2 else []
    return [*far, *again, 1 - odd, odd]


def times(a, b):
    return jnp.dot(a, b, preferred_element_type=F32)


def times_t(a, b):
    return lax.dot_general(a, b, (((1,), (1,)), ((), ())), preferred_element_type=F32)


def gather(links, refs):
    parts = [ref[...] for ref in refs]
    if len(parts) > links:
        values = [part.astype(F32) for part in parts[:3]]
        picked = []
        for own in turns(2 * FAR):
            later = jnp.where(is_turn(own, 1), values[1], values[2])
            picked.append(jnp.where(is_turn(own, 0), values[0], later).astype(BF16))
        parts = [*picked, parts[3]]
    return jnp.concatenate(parts, 1)


def scatter(links, refs, block):
    share = refs[0].shape[1]
    parts = [block[:, k * share : (k + 1) * share].astype(F32) for k in range(links)]
    if len(refs) > links:
        far, odd, near = parts
        own, _ = turns(2 * FAR)
        parts = [*(jnp.where(is_turn(own, turn), far, odd) for turn in range(3)), near]
    for ref, part in zip(refs, parts):
        ref[...] = part.astype(BF16)


def open_kernel(
    trips,
    links,
    subs,
    rows_in,
    near_in,
    rhs_in,
    weight_in,
    n_in,
    s_in,
    hot_ref,
    turned_ref,
    picked_ref,
    weight_ref,
    n_ref,
    s_ref,
    *refs,
):
    out_refs, (rows_ref, near_ref, rhs_ref, sems) = refs[:trips], refs[trips:]
    pairs = [
        (rows_in, rows_ref),
        (near_in, near_ref),
        (rhs_in, rhs_ref),
        (weight_in, weight_ref),
        (n_in, n_ref),
        (s_in, s_ref),
    ]
    copies = [pltpu.make_async_copy(source, target, sems.at[k]) for k, (source, target) in enumerate(pairs)]
    for copy in copies:
        copy.start()
    width, share = rhs_ref.shape[1], rows_ref.shape[2]
    slots = slots_of(lax.axis_index("sub"), subs)
    place = lax.broadcasted_iota(jnp.int32, (width, share), 0)
    copies[0].wait()
    copies[1].wait()
    near = near_ref[...].astype(F32)
    lane = lax.broadcasted_iota(jnp.int32, near.shape, 1)
    for k, slot in enumerate(slots):
        partner = jnp.sum(jnp.where(lane == slot, near, 0.0), 1, keepdims=True)
        row = jnp.where(partner >= 0.0, rows_ref[0, pl.ds(slot, 1), :], -1)
        hot_ref[:, pl.ds(k * share, share)] = jnp.where(place == row, 1.0, 0.0).astype(BF16)
    copies[2].wait()
    turned = rhs_ref[0].T
    turned_ref[...] = turned
    picked = times(turned, hot_ref[...]).astype(BF16)
    picked_ref[...] = picked
    scatter(links, out_refs, picked)
    for copy in copies[3:]:
        copy.wait()


def pick_n_kernel(
    hot_ref,
    turned_ref,
    n_ref,
    weight_ref,
    count_ref,
    hot_t_ref,
    n_pick_ref,
    n_small_ref,
    same_ref,
    inner_ref,
    mask_ref,
    local_ref,
    base_ref,
    row_ref,
):
    hot = hot_ref[...]
    width, total = hot.shape
    weight = weight_ref[...]
    hot_t = hot.T
    hot_t_ref[...] = hot_t
    n_pick = times(hot_t, n_ref[0]).astype(BF16)
    n_pick_ref[...] = n_pick
    n_small_ref[...] = times(n_pick, hot).astype(BF16)
    same = times(hot_t, hot)
    same_ref[...] = same.astype(BF16)
    earlier = lax.broadcasted_iota(jnp.int32, same.shape, 0) < lax.broadcasted_iota(jnp.int32, same.shape, 1)
    repeats = jnp.sum(jnp.where(earlier, same, 0.0), 0, keepdims=True)
    first = jnp.where(repeats > 0.0, 0.0, 1.0)
    hits = jnp.sum(hot_t.astype(F32), 0, keepdims=True)
    inner = jnp.where(hits > 0.0, 0.0, 1.0)
    inner_ref[...] = jnp.broadcast_to(inner, inner_ref.shape)
    high = weight.astype(BF16).astype(F32)
    middle = (weight - high).astype(BF16).astype(F32)
    low = weight - high - middle
    level = lax.broadcasted_iota(jnp.int32, (8, width), 0)
    pieces = jnp.where(level == 0, high, jnp.where(level == 1, middle, jnp.where(level == 2, low, 0.0)))
    pieces = times(pieces.astype(BF16), hot)
    chosen = (pieces[0:1] + pieces[1:2]) + pieces[2:3]
    row_ref[0:1] = chosen
    row_ref[1:2] = chosen * first
    row_ref[2:3] = first
    row_ref[3:8] = jnp.zeros((5, total), F32)
    mask = jnp.where(lax.broadcasted_iota(jnp.int32, mask_ref.shape, 1) < count_ref[0], 1.0, 0.0)
    mask_ref[...] = mask
    local = mask[:1] * turned_ref[...].astype(F32)
    local_ref[...] = local
    base_ref[...] = times_t((weight * local * inner).astype(BF16), n_pick)


def update_path_kernel(trips, links, step, last, *refs):
    arrived_refs, refs = refs[:trips], refs[trips:]
    same_ref, n_small_ref, row_ref, local_ref, base_ref = refs[:5]
    refs = refs[5:]
    residual = local_ref[...].astype(F32) + times(gather(links, arrived_refs), same_ref[...])
    scaled = (row_ref[1:2] * residual).astype(BF16)
    sent = row_ref[0:1] * (base_ref[...] + times_t(scaled, n_small_ref[...]))
    if last:
        scatter(links, refs, sent)
    elif step == 0:
        scatter(links, refs[1:], sent)
        refs[0][...] = DAMPING * sent
    else:
        scatter(links, refs[2:], sent)
        refs[1][...] = refs[0][...] + DAMPING * sent


def residual_path_kernel(trips, links, last, *refs):
    arrived_refs, refs = refs[:trips], refs[trips:]
    same_ref, s_small_ref, row_ref, base_ref, state_ref, local_ref = refs[:6]
    state = state_ref[...] + DAMPING * times(gather(links, arrived_refs), same_ref[...])
    if last:
        refs = refs[6:]
    else:
        refs[6][...] = state
        refs = refs[7:]
    local = base_ref[...] - times((state * row_ref[2:3]).astype(BF16), s_small_ref[...])
    local_ref[...] = local
    scatter(links, refs, local)


def corrected(links, arrived_refs, hot_ref, n_ref, weight_ref, mask_ref, local_ref):
    weight = weight_ref[...]
    residual = local_ref[...] + times_t(gather(links, arrived_refs), hot_ref[...])
    scaled = (weight * residual).astype(BF16)
    return mask_ref[:1] * weight * times_t(scaled, n_ref[0])


def first_update_kernel(trips, links, *refs):
    arrived_refs, refs = refs[:trips], refs[trips:]
    hot_ref, hot_t_ref, n_ref, s_ref, weight_ref, mask_ref, inner_ref, local_ref, picked_ref = refs[:9]
    state_out_ref, base_ref, s_pick_ref, s_small_ref = refs[9:]
    state = DAMPING * corrected(links, arrived_refs, hot_ref, n_ref, weight_ref, mask_ref, local_ref)
    state_out_ref[...] = state
    s_pick = times(s_ref[0], hot_ref[...]).astype(BF16)
    s_pick_ref[...] = s_pick
    s_small_ref[...] = times(hot_t_ref[...], s_pick).astype(BF16)
    base_ref[...] = picked_ref[...].astype(F32) - times((state * inner_ref[:1]).astype(BF16), s_pick)


def update_kernel(trips, links, *refs):
    arrived_refs, refs = refs[:trips], refs[trips:]
    hot_ref, n_ref, weight_ref, mask_ref, inner_ref, local_ref, picked_ref, s_pick_ref, state_ref = refs[:9]
    state_out_ref, base_ref = refs[9:]
    state = state_ref[...] + DAMPING * corrected(links, arrived_refs, hot_ref, n_ref, weight_ref, mask_ref, local_ref)
    state_out_ref[...] = state
    base_ref[...] = picked_ref[...].astype(F32) - times((state * inner_ref[:1]).astype(BF16), s_pick_ref[...])


def last_update_kernel(trips, links, *refs):
    arrived_refs, refs = refs[:trips], refs[trips:]
    hot_ref, n_ref, weight_ref, mask_ref, local_ref, state_ref, state_out_ref = refs
    update = corrected(links, arrived_refs, hot_ref, n_ref, weight_ref, mask_ref, local_ref)
    state_out_ref[...] = (state_ref[...] + DAMPING * update).T


def residual_kernel(trips, links, *refs):
    arrived_refs, refs = refs[:trips], refs[trips:]
    hot_ref, s_ref, turned_ref, weight_ref, mask_ref, inner_ref, n_pick_ref, state_ref = refs[:8]
    state_out_ref, local_ref, base_ref = refs[8:]
    state = state_ref[...] + DAMPING * times_t(gather(links, arrived_refs), hot_ref[...])
    state_out_ref[...] = state
    local = mask_ref[:1] * (turned_ref[...].astype(F32) - times(state.astype(BF16), s_ref[0]))
    local_ref[...] = local
    base_ref[...] = times_t((weight_ref[...] * local * inner_ref[:1]).astype(BF16), n_pick_ref[...])


def close_kernel(trips, links, *refs):
    arrived_refs, (hot_ref, state_ref, out_ref, piece_ref, sems) = refs[:trips], refs[trips:]
    arrived = gather(links, arrived_refs)
    rows = state_ref.shape[0] // PIECES
    copies = []
    for k in range(PIECES):
        part = pl.ds(k * rows, rows)
        piece_ref[part, :] = state_ref[part, :] + DAMPING * times_t(hot_ref[part, :], arrived)
        copies.append(pltpu.make_async_copy(piece_ref.at[part, :], out_ref.at[0, part, :], sems.at[k]))
        copies[k].start()
    for copy in copies:
        copy.wait()


def run(kernel, operands, results, flops, inputs=pltpu.VMEM, outputs=pltpu.VMEM, scalars=(), scratch=()):
    if inputs is pltpu.HBM:
        operands = [pltpu.with_memory_space_constraint(a, inputs) for a in operands]
    moved = sum(a.size * a.dtype.itemsize for a in (*operands, *results))
    return pl.pallas_call(
        kernel,
        out_shape=results,
        in_specs=[pl.BlockSpec(memory_space=pltpu.SMEM if k in scalars else inputs) for k in range(len(operands))],
        out_specs=[pl.BlockSpec(memory_space=outputs)] * len(results),
        scratch_shapes=scratch,
        compiler_params=pltpu.CompilerParams(vmem_limit_bytes=LIMIT),
        cost_estimate=pl.CostEstimate(flops=flops, bytes_accessed=moved, transcendentals=0),
    )(*operands)


def body(right_side, schur, neumann, weights, neighbours, counts, shared_rows):
    width, leads = right_side.shape[1:]
    share = shared_rows.shape[2]
    subs = lax.axis_size("sub")
    routes = swaps(subs)
    trips = len(routes)
    links = len(slots_of(0, subs))
    total = links * share

    def array(rows, columns, kind=F32):
        return jax.ShapeDtypeStruct((rows, columns), kind)

    def same_as(a):
        return jax.ShapeDtypeStruct(a.shape, a.dtype)

    messages = [array(leads, share, BF16)] * trips
    full, some = array(leads, width), array(leads, total)
    small = array(total, total, BF16)
    row = array(8, width)
    picks = 2 * leads * total * width
    whole = 2 * leads * width * width
    path = 4 * leads * total * total

    def exchange(parts):
        return [lax.ppermute(part, "sub", route) for part, route in zip(parts, routes)]

    def bound(kernel, *settings):
        return functools.partial(kernel, trips, links, *settings)

    hot, turned, picked, weight, n_mat, s_mat, *sent = run(
        bound(open_kernel, subs),
        [shared_rows, neighbours, right_side, weights, neumann, schur],
        [
            array(width, total, BF16),
            array(leads, width, BF16),
            array(leads, total, BF16),
            same_as(weights),
            same_as(neumann),
            same_as(schur),
            *messages,
        ],
        picks,
        inputs=pltpu.HBM,
        scratch=[
            pltpu.VMEM(shared_rows.shape, jnp.int32),
            pltpu.VMEM(neighbours.shape, jnp.int32),
            pltpu.VMEM(right_side.shape, BF16),
            pltpu.SemaphoreType.DMA((6,)),
        ],
    )
    arrived = exchange(sent)
    hot_t, n_pick, n_small, same, inner, mask, local, base, rows = run(
        pick_n_kernel,
        [hot, turned, n_mat, weight, counts],
        [array(total, width, BF16), array(total, width, BF16), small, small, row, row, full, some, array(8, total)],
        2 * total * width * width + 4 * total * total * width + picks,
        scalars=(4,),
    )
    near = picked
    near_state = None
    for step in range(ITERS):
        came, last = arrived, step == ITERS - 1
        operands = [*came, same, n_small, rows, near, base]
        if step and not last:
            operands.append(near_state)
        kernel = bound(update_path_kernel, step, last)
        if last:
            sent = run(kernel, operands, messages, path)
            arrived = exchange(sent)
            (state,) = run(
                bound(last_update_kernel),
                [*came, hot, n_mat, weight, mask, local, state],
                [array(width, leads)],
                whole + picks,
            )
            break
        near_state, *sent = run(kernel, operands, [some, *messages], path)
        arrived = exchange(sent)
        if step == 0:
            state, base, s_pick, s_small = run(
                bound(first_update_kernel),
                [*came, hot, hot_t, n_mat, s_mat, weight, mask, inner, local, picked],
                [full, some, array(width, total, BF16), small],
                whole + 2 * picks + 2 * total * width * (width + total),
            )
        else:
            state, base = run(
                bound(update_kernel),
                [*came, hot, n_mat, weight, mask, inner, local, picked, s_pick, state],
                [full, some],
                whole + 2 * picks,
            )
        came = arrived
        ends = step == ITERS - 2
        near, *sent = run(
            bound(residual_path_kernel, ends),
            [*came, same, s_small, rows, base, near_state],
            [some, *([] if ends else [some]), *messages],
            path,
        )
        if not ends:
            near_state, *sent = sent
        arrived = exchange(sent)
        state, local, base = run(
            bound(residual_kernel),
            [*came, hot, s_mat, turned, weight, mask, inner, n_pick, state],
            [full, full, some],
            whole + 2 * picks,
        )
    (out,) = run(
        bound(close_kernel),
        [*arrived, hot, state],
        [jax.ShapeDtypeStruct((1, width, leads), F32)],
        picks,
        outputs=pltpu.HBM,
        scratch=[pltpu.VMEM((width, leads), F32), pltpu.SemaphoreType.DMA((PIECES,))],
    )
    return out


def solution(mesh):
    in_specs = (
        P("sub", None, None),
        P("sub", None, None),
        P("sub", None, None),
        P("sub", None),
        P("sub", None),
        P("sub"),
        P("sub", None, None),
    )
    out_specs = P("sub", None, None)
    return jax.shard_map(body, mesh=mesh, in_specs=in_specs, out_specs=out_specs, check_vma=False)
```

```python
import functools

import jax
import jax.numpy as jnp
from jax import lax
from jax.experimental import pallas as pl
from jax.experimental.pallas import tpu as pltpu
from jax.sharding import PartitionSpec as P

ITERS = 4
FAR = 16
DAMPING = 0.7
LIMIT = 16 * 2**20
PIECES = 4
F32 = jnp.float32
BF16 = jnp.bfloat16


FAR_TURNS = (0, 0, 0, 0, 0, 2, 1, 1, 1, 0, 0, 0, 0, 0, 1, 2)
ODD_TURNS = (1, 1, 0, 0, 1, 1, 2, 1, 1, 1, 0, 0, 1, 1, 2)
FILL = ((), ((0, 5), (13, 21), (29, 31)), ((4, 12), (20, 28)))


def turns(count):
    far = [FAR_TURNS[i % FAR] for i in range(count)]
    odd = [ODD_TURNS[(i - 1) // 2] if 0 < i < count - 1 else -1 for i in range(count)]
    return far, odd


def mixed(count):
    return count == 2 * FAR


def swaps(count):
    blocks = count // FAR
    near = [i ^ 1 for i in range(count)]
    far = [i ^ FAR for i in range(count)]
    odd = [(((i + 1) ^ 1) - 1) % count for i in range(count)]
    if mixed(count):
        far_turns, odd_turns = turns(count)
        pairings = []
        for turn, fill in enumerate(FILL):
            pairing = list(near)
            for i, j in fill:
                pairing[i], pairing[j] = j, i
            for i in range(count):
                if far_turns[i] == turn:
                    pairing[i] = far[i]
                elif odd_turns[i] == turn:
                    pairing[i] = odd[i]
            pairings.append(pairing)
        pairings.append(near)
    else:
        again = [(((i // FAR + 1) ^ 1) - 1) % blocks * FAR + i % FAR for i in range(count)]
        pairings = ([far] if blocks > 1 else []) + ([again] if blocks > 2 else []) + [odd, near]
    for pairing in pairings:
        assert all(pairing[j] == i != j for i, j in enumerate(pairing))
    return [list(enumerate(pairing)) for pairing in pairings]


def is_turn(own_turns, turn):
    bits = sum(1 << i for i, own in enumerate(own_turns) if own == turn)
    bits = bits - (1 << 32) if bits >> 31 else bits
    return lax.shift_right_logical(jnp.int32(bits), lax.axis_index("sub")) & 1 == 1


def slots_of(index, count):
    odd = lax.rem(index, 2)
    block = lax.rem(lax.div(index, FAR), 2)
    blocks = count // FAR
    far = [2 + block] if blocks > 1 else []
    again = [3 - block] if blocks > 2 else []
    return [*far, *again, 1 - odd, odd]


def times(a, b):
    return jnp.dot(a, b, preferred_element_type=F32)


def times_t(a, b):
    return lax.dot_general(a, b, (((1,), (1,)), ((), ())), preferred_element_type=F32)


def gather(links, refs):
    parts = [ref[...] for ref in refs]
    if len(parts) > links:
        values = [part.astype(F32) for part in parts[:3]]
        picked = []
        for own in turns(2 * FAR):
            later = jnp.where(is_turn(own, 1), values[1], values[2])
            picked.append(jnp.where(is_turn(own, 0), values[0], later).astype(BF16))
        parts = [*picked, parts[3]]
    return jnp.concatenate(parts, 1)


def scatter(links, refs, block):
    share = refs[0].shape[1]
    parts = [block[:, k * share : (k + 1) * share].astype(F32) for k in range(links)]
    if len(refs) > links:
        far, odd, near = parts
        own, _ = turns(2 * FAR)
        parts = [*(jnp.where(is_turn(own, turn), far, odd) for turn in range(3)), near]
    for ref, part in zip(refs, parts):
        ref[...] = part.astype(BF16)


def open_kernel(
    trips,
    links,
    subs,
    rows_in,
    near_in,
    rhs_in,
    weight_in,
    n_in,
    hot_ref,
    turned_ref,
    picked_ref,
    list_ref,
    weight_ref,
    n_ref,
    *refs,
):
    out_refs, (rows_ref, near_ref, rhs_ref, sems) = refs[:trips], refs[trips:]
    pairs = [
        (rows_in, rows_ref),
        (near_in, near_ref),
        (rhs_in, rhs_ref),
        (weight_in, weight_ref),
        (n_in, n_ref),
    ]
    copies = [pltpu.make_async_copy(source, target, sems.at[k]) for k, (source, target) in enumerate(pairs)]
    for copy in copies:
        copy.start()
    width, share = rhs_ref.shape[1], rows_ref.shape[2]
    slots = slots_of(lax.axis_index("sub"), subs)
    place = lax.broadcasted_iota(jnp.int32, (width, share), 0)
    copies[0].wait()
    copies[1].wait()
    near = near_ref[...].astype(F32)
    lane = lax.broadcasted_iota(jnp.int32, near.shape, 1)
    for k, slot in enumerate(slots):
        partner = jnp.sum(jnp.where(lane == slot, near, 0.0), 1, keepdims=True)
        row = jnp.where(partner >= 0.0, rows_ref[0, pl.ds(slot, 1), :], -1)
        list_ref[:, pl.ds(k * share, share)] = jnp.broadcast_to(row.astype(F32), (list_ref.shape[0], share))
        hot_ref[:, pl.ds(k * share, share)] = jnp.where(place == row, 1.0, 0.0).astype(BF16)
    copies[2].wait()
    turned = rhs_ref[0].T
    turned_ref[...] = turned
    picked = times(turned, hot_ref[...]).astype(BF16)
    picked_ref[...] = picked
    scatter(links, out_refs, picked)
    for copy in copies[3:]:
        copy.wait()


def pick_n_kernel(
    hot_ref,
    turned_ref,
    list_ref,
    n_ref,
    weight_ref,
    count_ref,
    s_in,
    hot_t_ref,
    n_pick_ref,
    n_small_ref,
    same_ref,
    inner_ref,
    mask_ref,
    local_ref,
    base_ref,
    row_ref,
    s_ref,
    sem,
):
    copy = pltpu.make_async_copy(s_in, s_ref, sem)
    copy.start()
    hot = hot_ref[...]
    width, total = hot.shape
    weight = weight_ref[...]
    side = 128
    listed = list_ref[:1]
    lane = lax.broadcasted_iota(jnp.int32, (side, side), 1).astype(F32)
    hits = [jnp.zeros((1, side), F32)] * (width // side)
    same = []
    for k in range(0, total, side):
        down = jnp.broadcast_to(listed[:, k : k + side], (side, side)).T
        for m in range(width // side):
            block = jnp.where(down == lane + float(m * side), 1.0, 0.0)
            hits[m] = hits[m] + jnp.sum(block, 0, keepdims=True)
            hot_t_ref[k : k + side, m * side : (m + 1) * side] = block.astype(BF16)
        wide = jnp.concatenate([down] * (total // side), 1)
        same.append(jnp.where((wide == listed) & (wide >= 0.0), 1.0, 0.0))
    same = jnp.concatenate(same, 0)
    same_ref[...] = same.astype(BF16)
    inner = jnp.where(jnp.concatenate(hits, 1) > 0.0, 0.0, 1.0)
    inner_ref[...] = jnp.broadcast_to(inner, inner_ref.shape)
    n_pick = times(hot_t_ref[...], n_ref[0]).astype(BF16)
    n_pick_ref[...] = n_pick
    n_small_ref[...] = times(n_pick, hot).astype(BF16)
    earlier = lax.broadcasted_iota(jnp.int32, same.shape, 0) < lax.broadcasted_iota(jnp.int32, same.shape, 1)
    repeats = jnp.sum(jnp.where(earlier, same, 0.0), 0, keepdims=True)
    first = jnp.where(repeats > 0.0, 0.0, 1.0)
    high = weight.astype(BF16).astype(F32)
    middle = (weight - high).astype(BF16).astype(F32)
    low = weight - high - middle
    level = lax.broadcasted_iota(jnp.int32, (8, width), 0)
    pieces = jnp.where(level == 0, high, jnp.where(level == 1, middle, jnp.where(level == 2, low, 0.0)))
    pieces = times(pieces.astype(BF16), hot)
    chosen = (pieces[0:1] + pieces[1:2]) + pieces[2:3]
    row_ref[0:1] = chosen
    row_ref[1:2] = chosen * first
    row_ref[2:3] = first
    row_ref[3:8] = jnp.zeros((5, total), F32)
    mask = jnp.where(lax.broadcasted_iota(jnp.int32, mask_ref.shape, 1) < count_ref[0], 1.0, 0.0)
    mask_ref[...] = mask
    local = mask[:1] * turned_ref[...].astype(F32)
    local_ref[...] = local
    base_ref[...] = times_t((weight * local * inner).astype(BF16), n_pick)
    copy.wait()


def update_path_kernel(trips, links, step, last, *refs):
    arrived_refs, refs = refs[:trips], refs[trips:]
    same_ref, n_small_ref, row_ref, local_ref, base_ref = refs[:5]
    refs = refs[5:]
    residual = local_ref[...].astype(F32) + times(gather(links, arrived_refs), same_ref[...])
    scaled = (row_ref[1:2] * residual).astype(BF16)
    sent = row_ref[0:1] * (base_ref[...] + times_t(scaled, n_small_ref[...]))
    if last:
        scatter(links, refs, sent)
    elif step == 0:
        scatter(links, refs[1:], sent)
        refs[0][...] = DAMPING * sent
    else:
        scatter(links, refs[2:], sent)
        refs[1][...] = refs[0][...] + DAMPING * sent


def residual_path_kernel(trips, links, last, *refs):
    arrived_refs, refs = refs[:trips], refs[trips:]
    same_ref, s_small_ref, row_ref, base_ref, state_ref, local_ref = refs[:6]
    state = state_ref[...] + DAMPING * times(gather(links, arrived_refs), same_ref[...])
    if last:
        refs = refs[6:]
    else:
        refs[6][...] = state
        refs = refs[7:]
    local = base_ref[...] - times((state * row_ref[2:3]).astype(BF16), s_small_ref[...])
    local_ref[...] = local
    scatter(links, refs, local)


def corrected(links, arrived_refs, hot_ref, n_ref, weight_ref, mask_ref, local_ref):
    weight = weight_ref[...]
    residual = local_ref[...] + times_t(gather(links, arrived_refs), hot_ref[...])
    scaled = (weight * residual).astype(BF16)
    return mask_ref[:1] * weight * times_t(scaled, n_ref[0])


def first_update_kernel(trips, links, *refs):
    arrived_refs, refs = refs[:trips], refs[trips:]
    hot_ref, hot_t_ref, n_ref, s_ref, weight_ref, mask_ref, inner_ref, local_ref, picked_ref = refs[:9]
    state_out_ref, base_ref, s_pick_ref, s_small_ref = refs[9:]
    state = DAMPING * corrected(links, arrived_refs, hot_ref, n_ref, weight_ref, mask_ref, local_ref)
    state_out_ref[...] = state
    s_pick = times(s_ref[0], hot_ref[...]).astype(BF16)
    s_pick_ref[...] = s_pick
    s_small_ref[...] = times(hot_t_ref[...], s_pick).astype(BF16)
    base_ref[...] = picked_ref[...].astype(F32) - times((state * inner_ref[:1]).astype(BF16), s_pick)


def update_kernel(trips, links, *refs):
    arrived_refs, refs = refs[:trips], refs[trips:]
    hot_ref, n_ref, weight_ref, mask_ref, inner_ref, local_ref, picked_ref, s_pick_ref, state_ref = refs[:9]
    state_out_ref, base_ref = refs[9:]
    state = state_ref[...] + DAMPING * corrected(links, arrived_refs, hot_ref, n_ref, weight_ref, mask_ref, local_ref)
    state_out_ref[...] = state
    base_ref[...] = picked_ref[...].astype(F32) - times((state * inner_ref[:1]).astype(BF16), s_pick_ref[...])


def last_update_kernel(trips, links, *refs):
    arrived_refs, refs = refs[:trips], refs[trips:]
    hot_ref, n_ref, weight_ref, mask_ref, local_ref, state_ref, state_out_ref = refs
    update = corrected(links, arrived_refs, hot_ref, n_ref, weight_ref, mask_ref, local_ref)
    state_out_ref[...] = (state_ref[...] + DAMPING * update).T


def residual_kernel(trips, links, *refs):
    arrived_refs, refs = refs[:trips], refs[trips:]
    hot_ref, s_ref, turned_ref, weight_ref, mask_ref, inner_ref, n_pick_ref, state_ref = refs[:8]
    state_out_ref, local_ref, base_ref = refs[8:]
    state = state_ref[...] + DAMPING * times_t(gather(links, arrived_refs), hot_ref[...])
    state_out_ref[...] = state
    local = mask_ref[:1] * (turned_ref[...].astype(F32) - times(state.astype(BF16), s_ref[0]))
    local_ref[...] = local
    base_ref[...] = times_t((weight_ref[...] * local * inner_ref[:1]).astype(BF16), n_pick_ref[...])


def close_kernel(trips, links, *refs):
    arrived_refs, (hot_ref, state_ref, out_ref, piece_ref, sems) = refs[:trips], refs[trips:]
    arrived = gather(links, arrived_refs)
    rows = state_ref.shape[0] // PIECES
    copies = []
    for k in range(PIECES):
        part = pl.ds(k * rows, rows)
        piece_ref[part, :] = state_ref[part, :] + DAMPING * times_t(hot_ref[part, :], arrived)
        copies.append(pltpu.make_async_copy(piece_ref.at[part, :], out_ref.at[0, part, :], sems.at[k]))
        copies[k].start()
    for copy in copies:
        copy.wait()


def run(kernel, operands, results, flops, spaces=(), outputs=pltpu.VMEM, scratch=()):
    spaces = [dict(spaces).get(k, pltpu.VMEM) for k in range(len(operands))]
    moved = sum(a.size * a.dtype.itemsize for a in (*operands, *results))
    operands = [
        pltpu.with_memory_space_constraint(a, space) if space is pltpu.HBM else a for a, space in zip(operands, spaces)
    ]
    return pl.pallas_call(
        kernel,
        out_shape=results,
        in_specs=[pl.BlockSpec(memory_space=space) for space in spaces],
        out_specs=[pl.BlockSpec(memory_space=outputs)] * len(results),
        scratch_shapes=scratch,
        compiler_params=pltpu.CompilerParams(vmem_limit_bytes=LIMIT),
        cost_estimate=pl.CostEstimate(flops=flops, bytes_accessed=moved, transcendentals=0),
    )(*operands)


def body(right_side, schur, neumann, weights, neighbours, counts, shared_rows):
    width, leads = right_side.shape[1:]
    share = shared_rows.shape[2]
    subs = lax.axis_size("sub")
    routes = swaps(subs)
    trips = len(routes)
    links = len(slots_of(0, subs))
    total = links * share

    def array(rows, columns, kind=F32):
        return jax.ShapeDtypeStruct((rows, columns), kind)

    def same_as(a):
        return jax.ShapeDtypeStruct(a.shape, a.dtype)

    messages = [array(leads, share, BF16)] * trips
    full, some = array(leads, width), array(leads, total)
    small = array(total, total, BF16)
    row = array(8, width)
    picks = 2 * leads * total * width
    whole = 2 * leads * width * width
    path = 4 * leads * total * total

    def exchange(parts):
        return [lax.ppermute(part, "sub", route) for part, route in zip(parts, routes)]

    def bound(kernel, *settings):
        return functools.partial(kernel, trips, links, *settings)

    hot, turned, picked, listed, weight, n_mat, *sent = run(
        bound(open_kernel, subs),
        [shared_rows, neighbours, right_side, weights, neumann],
        [
            array(width, total, BF16),
            array(leads, width, BF16),
            array(leads, total, BF16),
            array(8, total),
            same_as(weights),
            same_as(neumann),
            *messages,
        ],
        picks,
        spaces={k: pltpu.HBM for k in range(5)},
        scratch=[
            pltpu.VMEM(shared_rows.shape, jnp.int32),
            pltpu.VMEM(neighbours.shape, jnp.int32),
            pltpu.VMEM(right_side.shape, BF16),
            pltpu.SemaphoreType.DMA((5,)),
        ],
    )
    arrived = exchange(sent)
    hot_t, n_pick, n_small, same, inner, mask, local, base, rows, s_mat = run(
        pick_n_kernel,
        [hot, turned, listed, n_mat, weight, counts, schur],
        [
            array(total, width, BF16),
            array(total, width, BF16),
            small,
            small,
            row,
            row,
            full,
            some,
            array(8, total),
            same_as(schur),
        ],
        2 * total * width * width + 2 * total * total * width + picks,
        spaces={5: pltpu.SMEM, 6: pltpu.HBM},
        scratch=[pltpu.SemaphoreType.DMA],
    )
    near = picked
    near_state = None
    for step in range(ITERS):
        came, last = arrived, step == ITERS - 1
        operands = [*came, same, n_small, rows, near, base]
        if step and not last:
            operands.append(near_state)
        kernel = bound(update_path_kernel, step, last)
        if last:
            sent = run(kernel, operands, messages, path)
            arrived = exchange(sent)
            (state,) = run(
                bound(last_update_kernel),
                [*came, hot, n_mat, weight, mask, local, state],
                [array(width, leads)],
                whole + picks,
            )
            break
        near_state, *sent = run(kernel, operands, [some, *messages], path)
        arrived = exchange(sent)
        if step == 0:
            state, base, s_pick, s_small = run(
                bound(first_update_kernel),
                [*came, hot, hot_t, n_mat, s_mat, weight, mask, inner, local, picked],
                [full, some, array(width, total, BF16), small],
                whole + 2 * picks + 2 * total * width * (width + total),
            )
        else:
            state, base = run(
                bound(update_kernel),
                [*came, hot, n_mat, weight, mask, inner, local, picked, s_pick, state],
                [full, some],
                whole + 2 * picks,
            )
        came = arrived
        ends = step == ITERS - 2
        near, *sent = run(
            bound(residual_path_kernel, ends),
            [*came, same, s_small, rows, base, near_state],
            [some, *([] if ends else [some]), *messages],
            path,
        )
        if not ends:
            near_state, *sent = sent
        arrived = exchange(sent)
        state, local, base = run(
            bound(residual_kernel),
            [*came, hot, s_mat, turned, weight, mask, inner, n_pick, state],
            [full, full, some],
            whole + 2 * picks,
        )
    (out,) = run(
        bound(close_kernel),
        [*arrived, hot, state],
        [jax.ShapeDtypeStruct((1, width, leads), F32)],
        picks,
        outputs=pltpu.HBM,
        scratch=[pltpu.VMEM((width, leads), F32), pltpu.SemaphoreType.DMA((PIECES,))],
    )
    return out


def solution(mesh):
    in_specs = (
        P("sub", None, None),
        P("sub", None, None),
        P("sub", None, None),
        P("sub", None),
        P("sub", None),
        P("sub"),
        P("sub", None, None),
    )
    out_specs = P("sub", None, None)
    return jax.shard_map(body, mesh=mesh, in_specs=in_specs, out_specs=out_specs, check_vma=False)
```

```python
import functools

import jax
import jax.numpy as jnp
from jax import lax
from jax.experimental import pallas as pl
from jax.experimental.pallas import tpu as pltpu
from jax.sharding import PartitionSpec as P

ITERS = 4
FAR = 16
DAMPING = 0.7
LIMIT = 16 * 2**20
PIECES = 4
F32 = jnp.float32
BF16 = jnp.bfloat16


FAR_TURNS = (0, 0, 0, 0, 0, 2, 1, 1, 1, 0, 0, 0, 0, 0, 1, 2)
ODD_TURNS = (1, 1, 0, 0, 1, 1, 2, 1, 1, 1, 0, 0, 1, 1, 2)
FILL = ((), ((0, 5), (13, 21), (29, 31)), ((4, 12), (20, 28)))


def turns(count):
    far = [FAR_TURNS[i % FAR] for i in range(count)]
    odd = [ODD_TURNS[(i - 1) // 2] if 0 < i < count - 1 else -1 for i in range(count)]
    return far, odd


def mixed(count):
    return count == 2 * FAR


def swaps(count):
    blocks = count // FAR
    near = [i ^ 1 for i in range(count)]
    far = [i ^ FAR for i in range(count)]
    odd = [(((i + 1) ^ 1) - 1) % count for i in range(count)]
    if mixed(count):
        far_turns, odd_turns = turns(count)
        pairings = []
        for turn, fill in enumerate(FILL):
            pairing = list(near)
            for i, j in fill:
                pairing[i], pairing[j] = j, i
            for i in range(count):
                if far_turns[i] == turn:
                    pairing[i] = far[i]
                elif odd_turns[i] == turn:
                    pairing[i] = odd[i]
            pairings.append(pairing)
        pairings.append(near)
    else:
        again = [(((i // FAR + 1) ^ 1) - 1) % blocks * FAR + i % FAR for i in range(count)]
        pairings = ([far] if blocks > 1 else []) + ([again] if blocks > 2 else []) + [odd, near]
    for pairing in pairings:
        assert all(pairing[j] == i != j for i, j in enumerate(pairing))
    return [list(enumerate(pairing)) for pairing in pairings]


def is_turn(own_turns, turn):
    bits = sum(1 << i for i, own in enumerate(own_turns) if own == turn)
    bits = bits - (1 << 32) if bits >> 31 else bits
    return lax.shift_right_logical(jnp.int32(bits), lax.axis_index("sub")) & 1 == 1


def slots_of(index, count):
    odd = lax.rem(index, 2)
    block = lax.rem(lax.div(index, FAR), 2)
    blocks = count // FAR
    far = [2 + block] if blocks > 1 else []
    again = [3 - block] if blocks > 2 else []
    return [*far, *again, 1 - odd, odd]


def times(a, b):
    return jnp.dot(a, b, preferred_element_type=F32)


def times_t(a, b):
    return lax.dot_general(a, b, (((1,), (1,)), ((), ())), preferred_element_type=F32)


def together(refs):
    return jnp.concatenate([ref[...] for ref in refs], 1)


def gather(links, refs):
    parts = [ref[...] for ref in refs]
    if len(parts) > links:
        values = [part.astype(F32) for part in parts[:3]]
        picked = []
        for own in turns(2 * FAR):
            later = jnp.where(is_turn(own, 1), values[1], values[2])
            picked.append(jnp.where(is_turn(own, 0), values[0], later).astype(BF16))
        parts = [*picked, parts[3]]
    return jnp.concatenate(parts, 1)


def by_pairing(trips, links, blocks):
    if trips == links:
        return blocks
    far, odd, near = blocks
    far_turns, odd_turns = turns(2 * FAR)
    picked = []
    for turn in range(3):
        other = jnp.where(is_turn(odd_turns, turn), odd, jnp.zeros_like(odd))
        picked.append(jnp.where(is_turn(far_turns, turn), far, other))
    return [*picked, near]


def scatter(links, refs, block):
    share = refs[0].shape[1]
    parts = [block[:, k * share : (k + 1) * share].astype(F32) for k in range(links)]
    if len(refs) > links:
        far, odd, near = parts
        own, _ = turns(2 * FAR)
        parts = [*(jnp.where(is_turn(own, turn), far, odd) for turn in range(3)), near]
    for ref, part in zip(refs, parts):
        ref[...] = part.astype(BF16)


def open_kernel(
    trips,
    links,
    subs,
    rows_in,
    near_in,
    rhs_in,
    weight_in,
    n_in,
    hot_ref,
    turned_ref,
    picked_ref,
    list_ref,
    weight_ref,
    n_ref,
    *refs,
):
    out_refs, (rows_ref, near_ref, rhs_ref, sems) = refs[:trips], refs[trips:]
    pairs = [
        (rows_in, rows_ref),
        (near_in, near_ref),
        (rhs_in, rhs_ref),
        (weight_in, weight_ref),
        (n_in, n_ref),
    ]
    copies = [pltpu.make_async_copy(source, target, sems.at[k]) for k, (source, target) in enumerate(pairs)]
    for copy in copies:
        copy.start()
    width, share = rhs_ref.shape[1], rows_ref.shape[2]
    slots = slots_of(lax.axis_index("sub"), subs)
    place = lax.broadcasted_iota(jnp.int32, (width, share), 0)
    for copy in copies[:3]:
        copy.wait()
    turned = rhs_ref[0].T
    turned_ref[...] = turned
    near = near_ref[...].astype(F32)
    lane = lax.broadcasted_iota(jnp.int32, near.shape, 1)
    for k, slot in enumerate(slots):
        partner = jnp.sum(jnp.where(lane == slot, near, 0.0), 1, keepdims=True)
        row = jnp.where(partner >= 0.0, rows_ref[0, pl.ds(slot, 1), :], -1)
        list_ref[:, pl.ds(k * share, share)] = jnp.broadcast_to(row.astype(F32), (list_ref.shape[0], share))
        hot_ref[:, pl.ds(k * share, share)] = jnp.where(place == row, 1.0, 0.0).astype(BF16)
    picked = times(turned, hot_ref[...]).astype(BF16)
    picked_ref[...] = picked
    scatter(links, out_refs, picked)
    for copy in copies[3:]:
        copy.wait()


def pick_n_kernel(
    trips,
    links,
    hot_ref,
    turned_ref,
    list_ref,
    n_ref,
    weight_ref,
    count_ref,
    s_in,
    hot_t_ref,
    n_pick_ref,
    n_small_ref,
    same_ref,
    inner_ref,
    mask_ref,
    local_ref,
    base_ref,
    row_ref,
    s_ref,
    sem,
):
    copy = pltpu.make_async_copy(s_in, s_ref, sem)
    copy.start()
    hot = hot_ref[...]
    width, total = hot.shape
    weight = weight_ref[...]
    side = 128
    listed = list_ref[:1]
    lane = lax.broadcasted_iota(jnp.int32, (side, side), 1).astype(F32)
    hits = [jnp.zeros((1, side), F32)] * (width // side)
    same = []
    for k in range(0, total, side):
        down = jnp.broadcast_to(listed[:, k : k + side], (side, side)).T
        for m in range(width // side):
            block = jnp.where(down == lane + float(m * side), 1.0, 0.0)
            hits[m] = hits[m] + jnp.sum(block, 0, keepdims=True)
            hot_t_ref[k : k + side, m * side : (m + 1) * side] = block.astype(BF16)
        wide = jnp.concatenate([down] * (total // side), 1)
        same.append(jnp.where((wide == listed) & (wide >= 0.0), 1.0, 0.0))
    same_ref[...] = jnp.concatenate(by_pairing(trips, links, same), 0).astype(BF16)
    same = jnp.concatenate(same, 0)
    inner = jnp.where(jnp.concatenate(hits, 1) > 0.0, 0.0, 1.0)
    inner_ref[...] = jnp.broadcast_to(inner, inner_ref.shape)
    n_pick = times(hot_t_ref[...], n_ref[0]).astype(BF16)
    n_pick_ref[...] = n_pick
    earlier = lax.broadcasted_iota(jnp.int32, same.shape, 0) < lax.broadcasted_iota(jnp.int32, same.shape, 1)
    repeats = jnp.sum(jnp.where(earlier, same, 0.0), 0, keepdims=True)
    first = jnp.where(repeats > 0.0, 0.0, 1.0)
    high = weight.astype(BF16).astype(F32)
    middle = (weight - high).astype(BF16).astype(F32)
    low = weight - high - middle
    level = lax.broadcasted_iota(jnp.int32, (16, width), 0)
    pieces = jnp.where(level == 0, high, jnp.where(level == 1, middle, jnp.where(level == 2, low, 0.0)))
    chosen = times(jnp.concatenate([n_pick, pieces.astype(BF16)], 0), hot)
    n_small_ref[...] = chosen[:total].astype(BF16)
    pieces = chosen[total:]
    chosen = (pieces[0:1] + pieces[1:2]) + pieces[2:3]
    row_ref[0:1] = chosen
    row_ref[1:2] = chosen * first
    row_ref[2:3] = first
    row_ref[3:8] = jnp.zeros((5, total), F32)
    mask = jnp.where(lax.broadcasted_iota(jnp.int32, mask_ref.shape, 1) < count_ref[0], 1.0, 0.0)
    mask_ref[...] = mask
    local = mask[:1] * turned_ref[...].astype(F32)
    local_ref[...] = local
    base_ref[...] = times_t((weight * local * inner).astype(BF16), n_pick)
    copy.wait()


def update_path_kernel(trips, links, step, last, *refs):
    arrived_refs, refs = refs[:trips], refs[trips:]
    same_ref, n_small_ref, row_ref, local_ref, base_ref = refs[:5]
    refs = refs[5:]
    residual = local_ref[...].astype(F32) + times(together(arrived_refs), same_ref[...])
    scaled = (row_ref[1:2] * residual).astype(BF16)
    sent = row_ref[0:1] * (base_ref[...] + times_t(scaled, n_small_ref[...]))
    if last:
        scatter(links, refs, sent)
    elif step == 0:
        scatter(links, refs[1:], sent)
        refs[0][...] = DAMPING * sent
    else:
        scatter(links, refs[2:], sent)
        refs[1][...] = refs[0][...] + DAMPING * sent


def residual_path_kernel(trips, links, last, *refs):
    arrived_refs, refs = refs[:trips], refs[trips:]
    same_ref, s_small_ref, row_ref, base_ref, state_ref, local_ref = refs[:6]
    state = state_ref[...] + DAMPING * times(together(arrived_refs), same_ref[...])
    if last:
        refs = refs[6:]
    else:
        refs[6][...] = state
        refs = refs[7:]
    local = base_ref[...] - times((state * row_ref[2:3]).astype(BF16), s_small_ref[...])
    local_ref[...] = local
    scatter(links, refs, local)


def corrected(links, arrived_refs, hot_ref, n_ref, weight_ref, mask_ref, local_ref):
    weight = weight_ref[...]
    residual = local_ref[...] + times_t(gather(links, arrived_refs), hot_ref[...])
    scaled = (weight * residual).astype(BF16)
    return mask_ref[:1] * weight * times_t(scaled, n_ref[0])


def first_update_kernel(trips, links, *refs):
    arrived_refs, refs = refs[:trips], refs[trips:]
    hot_ref, hot_t_ref, n_ref, s_ref, weight_ref, mask_ref, inner_ref, local_ref, picked_ref = refs[:9]
    state_out_ref, base_ref, s_pick_ref, s_small_ref = refs[9:]
    state = DAMPING * corrected(links, arrived_refs, hot_ref, n_ref, weight_ref, mask_ref, local_ref)
    state_out_ref[...] = state
    s_pick = times(s_ref[0], hot_ref[...]).astype(BF16)
    s_pick_ref[...] = s_pick
    outer = jnp.concatenate([hot_t_ref[...], (state * inner_ref[:1]).astype(BF16)], 0)
    product = times(outer, s_pick)
    total = s_small_ref.shape[0]
    s_small_ref[...] = product[:total].astype(BF16)
    base_ref[...] = picked_ref[...].astype(F32) - product[total:]


def update_kernel(trips, links, *refs):
    arrived_refs, refs = refs[:trips], refs[trips:]
    hot_ref, n_ref, weight_ref, mask_ref, inner_ref, local_ref, picked_ref, s_pick_ref, state_ref = refs[:9]
    state_out_ref, base_ref = refs[9:]
    state = state_ref[...] + DAMPING * corrected(links, arrived_refs, hot_ref, n_ref, weight_ref, mask_ref, local_ref)
    state_out_ref[...] = state
    base_ref[...] = picked_ref[...].astype(F32) - times((state * inner_ref[:1]).astype(BF16), s_pick_ref[...])


def last_update_kernel(trips, links, *refs):
    arrived_refs, refs = refs[:trips], refs[trips:]
    hot_ref, n_ref, weight_ref, mask_ref, local_ref, state_ref, state_out_ref = refs
    update = corrected(links, arrived_refs, hot_ref, n_ref, weight_ref, mask_ref, local_ref)
    state_out_ref[...] = (state_ref[...] + DAMPING * update).T


def residual_kernel(trips, links, *refs):
    arrived_refs, refs = refs[:trips], refs[trips:]
    hot_ref, s_ref, turned_ref, weight_ref, mask_ref, inner_ref, n_pick_ref, state_ref = refs[:8]
    state_out_ref, local_ref, base_ref = refs[8:]
    state = state_ref[...] + DAMPING * times_t(gather(links, arrived_refs), hot_ref[...])
    state_out_ref[...] = state
    local = mask_ref[:1] * (turned_ref[...].astype(F32) - times(state.astype(BF16), s_ref[0]))
    local_ref[...] = local
    base_ref[...] = times_t((weight_ref[...] * local * inner_ref[:1]).astype(BF16), n_pick_ref[...])


def close_kernel(trips, links, *refs):
    arrived_refs, (hot_ref, state_ref, out_ref, piece_ref, sems) = refs[:trips], refs[trips:]
    arrived = gather(links, arrived_refs)
    rows = state_ref.shape[0] // PIECES
    copies = []
    for k in range(PIECES):
        part = pl.ds(k * rows, rows)
        piece_ref[part, :] = state_ref[part, :] + DAMPING * times_t(hot_ref[part, :], arrived)
        copies.append(pltpu.make_async_copy(piece_ref.at[part, :], out_ref.at[0, part, :], sems.at[k]))
        copies[k].start()
    for copy in copies:
        copy.wait()


def run(kernel, operands, results, flops, spaces=(), outputs=pltpu.VMEM, scratch=()):
    spaces = [dict(spaces).get(k, pltpu.VMEM) for k in range(len(operands))]
    moved = sum(a.size * a.dtype.itemsize for a in (*operands, *results))
    operands = [
        pltpu.with_memory_space_constraint(a, space) if space is pltpu.HBM else a for a, space in zip(operands, spaces)
    ]
    return pl.pallas_call(
        kernel,
        out_shape=results,
        in_specs=[pl.BlockSpec(memory_space=space) for space in spaces],
        out_specs=[pl.BlockSpec(memory_space=outputs)] * len(results),
        scratch_shapes=scratch,
        compiler_params=pltpu.CompilerParams(vmem_limit_bytes=LIMIT),
        cost_estimate=pl.CostEstimate(flops=flops, bytes_accessed=moved, transcendentals=0),
    )(*operands)


def body(right_side, schur, neumann, weights, neighbours, counts, shared_rows):
    width, leads = right_side.shape[1:]
    share = shared_rows.shape[2]
    subs = lax.axis_size("sub")
    routes = swaps(subs)
    trips = len(routes)
    links = len(slots_of(0, subs))
    total = links * share

    def array(rows, columns, kind=F32):
        return jax.ShapeDtypeStruct((rows, columns), kind)

    def same_as(a):
        return jax.ShapeDtypeStruct(a.shape, a.dtype)

    messages = [array(leads, share, BF16)] * trips
    full, some = array(leads, width), array(leads, total)
    small = array(total, total, BF16)
    row = array(8, width)
    picks = 2 * leads * total * width
    whole = 2 * leads * width * width
    path = 4 * leads * total * total

    def exchange(parts):
        return [lax.ppermute(part, "sub", route) for part, route in zip(parts, routes)]

    def bound(kernel, *settings):
        return functools.partial(kernel, trips, links, *settings)

    hot, turned, picked, listed, weight, n_mat, *sent = run(
        bound(open_kernel, subs),
        [shared_rows, neighbours, right_side, weights, neumann],
        [
            array(width, total, BF16),
            array(leads, width, BF16),
            array(leads, total, BF16),
            array(8, total),
            same_as(weights),
            same_as(neumann),
            *messages,
        ],
        picks,
        spaces={k: pltpu.HBM for k in range(5)},
        scratch=[
            pltpu.VMEM(shared_rows.shape, jnp.int32),
            pltpu.VMEM(neighbours.shape, jnp.int32),
            pltpu.VMEM(right_side.shape, BF16),
            pltpu.SemaphoreType.DMA((5,)),
        ],
    )
    arrived = exchange(sent)
    hot_t, n_pick, n_small, same, inner, mask, local, base, rows, s_mat = run(
        bound(pick_n_kernel),
        [hot, turned, listed, n_mat, weight, counts, schur],
        [
            array(total, width, BF16),
            array(total, width, BF16),
            small,
            array(trips * share, total, BF16),
            row,
            row,
            full,
            some,
            array(8, total),
            same_as(schur),
        ],
        2 * total * width * width + 2 * total * total * width + picks,
        spaces={5: pltpu.SMEM, 6: pltpu.HBM},
        scratch=[pltpu.SemaphoreType.DMA],
    )
    near = picked
    near_state = None
    for step in range(ITERS):
        came, last = arrived, step == ITERS - 1
        operands = [*came, same, n_small, rows, near, base]
        if step and not last:
            operands.append(near_state)
        kernel = bound(update_path_kernel, step, last)
        if last:
            sent = run(kernel, operands, messages, path)
            arrived = exchange(sent)
            (state,) = run(
                bound(last_update_kernel),
                [*came, hot, n_mat, weight, mask, local, state],
                [array(width, leads)],
                whole + picks,
            )
            break
        near_state, *sent = run(kernel, operands, [some, *messages], path)
        arrived = exchange(sent)
        if step == 0:
            state, base, s_pick, s_small = run(
                bound(first_update_kernel),
                [*came, hot, hot_t, n_mat, s_mat, weight, mask, inner, local, picked],
                [full, some, array(width, total, BF16), small],
                whole + 2 * picks + 2 * total * width * (width + total),
            )
        else:
            state, base = run(
                bound(update_kernel),
                [*came, hot, n_mat, weight, mask, inner, local, picked, s_pick, state],
                [full, some],
                whole + 2 * picks,
            )
        came = arrived
        ends = step == ITERS - 2
        near, *sent = run(
            bound(residual_path_kernel, ends),
            [*came, same, s_small, rows, base, near_state],
            [some, *([] if ends else [some]), *messages],
            path,
        )
        if not ends:
            near_state, *sent = sent
        arrived = exchange(sent)
        state, local, base = run(
            bound(residual_kernel),
            [*came, hot, s_mat, turned, weight, mask, inner, n_pick, state],
            [full, full, some],
            whole + 2 * picks,
        )
    (out,) = run(
        bound(close_kernel),
        [*arrived, hot, state],
        [jax.ShapeDtypeStruct((1, width, leads), F32)],
        picks,
        outputs=pltpu.HBM,
        scratch=[pltpu.VMEM((width, leads), F32), pltpu.SemaphoreType.DMA((PIECES,))],
    )
    return out


def solution(mesh):
    in_specs = (
        P("sub", None, None),
        P("sub", None, None),
        P("sub", None, None),
        P("sub", None),
        P("sub", None),
        P("sub"),
        P("sub", None, None),
    )
    out_specs = P("sub", None, None)
    return jax.shard_map(body, mesh=mesh, in_specs=in_specs, out_specs=out_specs, check_vma=False)
```

```python
import functools

import jax
import jax.numpy as jnp
from jax import lax
from jax.experimental import pallas as pl
from jax.experimental.pallas import tpu as pltpu
from jax.sharding import PartitionSpec as P

ITERS = 4
FAR = 16
DAMPING = 0.7
LIMIT = 16 * 2**20
PIECES = 4
F32 = jnp.float32
BF16 = jnp.bfloat16


PLANS = (
    (
        (1, 1, 2, 1, 1, 1, 1, 0, 0, 0, 0, 0, 2, 1, 1, 1),
        (0, 0, 2, 1, 1, 1, 0, 2, 0, 0, 0, 1, 1, 1, 2),
        (((0, 5), (6, 15), (12, 16)), ((2, 18),), ((3, 7), (4, 13), (14, 31), (17, 19))),
    ),
    (
        (1, 1, 1, 2, 2, 1, 1, 0, 0, 0, 2, 0, 1, 1, 1, 1),
        (0, 1, 0, 1, 1, 2, 2, 2, 2, 1, 2, 1, 1, 2, 2),
        (((0, 4), (3, 10), (22, 26)), ((11, 27),), ((2, 5), (23, 31))),
    ),
    (
        (0, 0, 0, 0, 0, 2, 1, 1, 1, 0, 0, 1, 1, 0, 0, 0),
        (1, 1, 0, 0, 1, 0, 2, 1, 1, 1, 0, 0, 1, 0, 2),
        ((), ((0, 5), (13, 14), (21, 29)), ((4, 12), (15, 20), (28, 31))),
    ),
)


def turns(count, plan):
    far_turns, odd_turns, _ = PLANS[plan]
    far = [far_turns[i % FAR] for i in range(count)]
    odd = [odd_turns[(i - 1) // 2] if 0 < i < count - 1 else -1 for i in range(count)]
    return far, odd


def mixed(count):
    return count == 2 * FAR


def swaps(count, plan):
    blocks = count // FAR
    near = [i ^ 1 for i in range(count)]
    far = [i ^ FAR for i in range(count)]
    odd = [(((i + 1) ^ 1) - 1) % count for i in range(count)]
    if mixed(count):
        far_turns, odd_turns = turns(count, plan)
        pairings = []
        for turn, fill in enumerate(PLANS[plan][2]):
            pairing = list(near)
            for i, j in fill:
                pairing[i], pairing[j] = j, i
            for i in range(count):
                if far_turns[i] == turn:
                    pairing[i] = far[i]
                elif odd_turns[i] == turn:
                    pairing[i] = odd[i]
            pairings.append(pairing)
        pairings.append(near)
    else:
        again = [(((i // FAR + 1) ^ 1) - 1) % blocks * FAR + i % FAR for i in range(count)]
        pairings = ([far] if blocks > 1 else []) + ([again] if blocks > 2 else []) + [odd, near]
    for pairing in pairings:
        assert all(pairing[j] == i != j for i, j in enumerate(pairing))
    return [list(enumerate(pairing)) for pairing in pairings]


def is_turn(own_turns, turn):
    bits = sum(1 << i for i, own in enumerate(own_turns) if own == turn)
    bits = bits - (1 << 32) if bits >> 31 else bits
    return lax.shift_right_logical(jnp.int32(bits), lax.axis_index("sub")) & 1 == 1


def slots_of(index, count):
    odd = lax.rem(index, 2)
    block = lax.rem(lax.div(index, FAR), 2)
    blocks = count // FAR
    far = [2 + block] if blocks > 1 else []
    again = [3 - block] if blocks > 2 else []
    return [*far, *again, 1 - odd, odd]


def times(a, b):
    return jnp.dot(a, b, preferred_element_type=F32)


def times_t(a, b):
    return lax.dot_general(a, b, (((1,), (1,)), ((), ())), preferred_element_type=F32)


def gather(links, plan, refs):
    parts = [ref[...] for ref in refs]
    if len(parts) > links:
        values = [part.astype(F32) for part in parts[:3]]
        picked = []
        for own in turns(2 * FAR, plan):
            later = jnp.where(is_turn(own, 1), values[1], values[2])
            picked.append(jnp.where(is_turn(own, 0), values[0], later).astype(BF16))
        parts = [*picked, parts[3]]
    return jnp.concatenate(parts, 1)


def scatter(links, plan, refs, block):
    share = refs[0].shape[1]
    parts = [block[:, k * share : (k + 1) * share].astype(F32) for k in range(links)]
    if len(refs) > links:
        far, odd, near = parts
        own, _ = turns(2 * FAR, plan)
        parts = [*(jnp.where(is_turn(own, turn), far, odd) for turn in range(3)), near]
    for ref, part in zip(refs, parts):
        ref[...] = part.astype(BF16)


def open_kernel(
    trips,
    links,
    plan_out,
    subs,
    rows_in,
    near_in,
    rhs_in,
    weight_in,
    n_in,
    hot_ref,
    turned_ref,
    picked_ref,
    list_ref,
    weight_ref,
    n_ref,
    *refs,
):
    out_refs, (rows_ref, near_ref, rhs_ref, sems) = refs[:trips], refs[trips:]
    pairs = [
        (rows_in, rows_ref),
        (near_in, near_ref),
        (rhs_in, rhs_ref),
        (weight_in, weight_ref),
        (n_in, n_ref),
    ]
    copies = [pltpu.make_async_copy(source, target, sems.at[k]) for k, (source, target) in enumerate(pairs)]
    for copy in copies:
        copy.start()
    width, share = rhs_ref.shape[1], rows_ref.shape[2]
    slots = slots_of(lax.axis_index("sub"), subs)
    place = lax.broadcasted_iota(jnp.int32, (width, share), 0)
    copies[0].wait()
    copies[1].wait()
    near = near_ref[...].astype(F32)
    lane = lax.broadcasted_iota(jnp.int32, near.shape, 1)
    for k, slot in enumerate(slots):
        partner = jnp.sum(jnp.where(lane == slot, near, 0.0), 1, keepdims=True)
        row = jnp.where(partner >= 0.0, rows_ref[0, pl.ds(slot, 1), :], -1)
        list_ref[:, pl.ds(k * share, share)] = jnp.broadcast_to(row.astype(F32), (list_ref.shape[0], share))
        hot_ref[:, pl.ds(k * share, share)] = jnp.where(place == row, 1.0, 0.0).astype(BF16)
    copies[2].wait()
    turned = rhs_ref[0].T
    turned_ref[...] = turned
    picked = times(turned, hot_ref[...]).astype(BF16)
    picked_ref[...] = picked
    scatter(links, plan_out, out_refs, picked)
    for copy in copies[3:]:
        copy.wait()


def pick_n_kernel(
    hot_ref,
    turned_ref,
    list_ref,
    n_ref,
    weight_ref,
    count_ref,
    s_in,
    hot_t_ref,
    n_pick_ref,
    n_small_ref,
    same_ref,
    inner_ref,
    mask_ref,
    local_ref,
    base_ref,
    row_ref,
    s_ref,
    sem,
):
    copy = pltpu.make_async_copy(s_in, s_ref, sem)
    copy.start()
    hot = hot_ref[...]
    width, total = hot.shape
    weight = weight_ref[...]
    side = 128
    listed = list_ref[:1]
    lane = lax.broadcasted_iota(jnp.int32, (side, side), 1).astype(F32)
    hits = [jnp.zeros((1, side), F32)] * (width // side)
    same = []
    for k in range(0, total, side):
        down = jnp.broadcast_to(listed[:, k : k + side], (side, side)).T
        for m in range(width // side):
            block = jnp.where(down == lane + float(m * side), 1.0, 0.0)
            hits[m] = hits[m] + jnp.sum(block, 0, keepdims=True)
            hot_t_ref[k : k + side, m * side : (m + 1) * side] = block.astype(BF16)
        wide = jnp.concatenate([down] * (total // side), 1)
        same.append(jnp.where((wide == listed) & (wide >= 0.0), 1.0, 0.0))
    same = jnp.concatenate(same, 0)
    same_ref[...] = same.astype(BF16)
    inner = jnp.where(jnp.concatenate(hits, 1) > 0.0, 0.0, 1.0)
    inner_ref[...] = jnp.broadcast_to(inner, inner_ref.shape)
    n_pick = times(hot_t_ref[...], n_ref[0]).astype(BF16)
    n_pick_ref[...] = n_pick
    n_small_ref[...] = times(n_pick, hot).astype(BF16)
    earlier = lax.broadcasted_iota(jnp.int32, same.shape, 0) < lax.broadcasted_iota(jnp.int32, same.shape, 1)
    repeats = jnp.sum(jnp.where(earlier, same, 0.0), 0, keepdims=True)
    first = jnp.where(repeats > 0.0, 0.0, 1.0)
    high = weight.astype(BF16).astype(F32)
    middle = (weight - high).astype(BF16).astype(F32)
    low = weight - high - middle
    level = lax.broadcasted_iota(jnp.int32, (8, width), 0)
    pieces = jnp.where(level == 0, high, jnp.where(level == 1, middle, jnp.where(level == 2, low, 0.0)))
    pieces = times(pieces.astype(BF16), hot)
    chosen = (pieces[0:1] + pieces[1:2]) + pieces[2:3]
    row_ref[0:1] = chosen
    row_ref[1:2] = chosen * first
    row_ref[2:3] = first
    row_ref[3:8] = jnp.zeros((5, total), F32)
    mask = jnp.where(lax.broadcasted_iota(jnp.int32, mask_ref.shape, 1) < count_ref[0], 1.0, 0.0)
    mask_ref[...] = mask
    local = mask[:1] * turned_ref[...].astype(F32)
    local_ref[...] = local
    base_ref[...] = times_t((weight * local * inner).astype(BF16), n_pick)
    copy.wait()


def update_path_kernel(trips, links, plan, plan_out, step, last, *refs):
    arrived_refs, refs = refs[:trips], refs[trips:]
    same_ref, n_small_ref, row_ref, local_ref, base_ref = refs[:5]
    refs = refs[5:]
    residual = local_ref[...].astype(F32) + times(gather(links, plan, arrived_refs), same_ref[...])
    scaled = (row_ref[1:2] * residual).astype(BF16)
    sent = row_ref[0:1] * (base_ref[...] + times_t(scaled, n_small_ref[...]))
    if last:
        scatter(links, plan_out, refs, sent)
    elif step == 0:
        scatter(links, plan_out, refs[1:], sent)
        refs[0][...] = DAMPING * sent
    else:
        scatter(links, plan_out, refs[2:], sent)
        refs[1][...] = refs[0][...] + DAMPING * sent


def residual_path_kernel(trips, links, plan, plan_out, last, *refs):
    arrived_refs, refs = refs[:trips], refs[trips:]
    same_ref, s_small_ref, row_ref, base_ref, state_ref, local_ref = refs[:6]
    state = state_ref[...] + DAMPING * times(gather(links, plan, arrived_refs), same_ref[...])
    if last:
        refs = refs[6:]
    else:
        refs[6][...] = state
        refs = refs[7:]
    local = base_ref[...] - times((state * row_ref[2:3]).astype(BF16), s_small_ref[...])
    local_ref[...] = local
    scatter(links, plan_out, refs, local)


def corrected(links, plan, arrived_refs, hot_ref, n_ref, weight_ref, mask_ref, local_ref):
    weight = weight_ref[...]
    residual = local_ref[...] + times_t(gather(links, plan, arrived_refs), hot_ref[...])
    scaled = (weight * residual).astype(BF16)
    return mask_ref[:1] * weight * times_t(scaled, n_ref[0])


def first_update_kernel(trips, links, plan, *refs):
    arrived_refs, refs = refs[:trips], refs[trips:]
    hot_ref, hot_t_ref, n_ref, s_ref, weight_ref, mask_ref, inner_ref, local_ref, picked_ref = refs[:9]
    state_out_ref, base_ref, s_pick_ref, s_small_ref = refs[9:]
    state = DAMPING * corrected(links, plan, arrived_refs, hot_ref, n_ref, weight_ref, mask_ref, local_ref)
    state_out_ref[...] = state
    s_pick = times(s_ref[0], hot_ref[...]).astype(BF16)
    s_pick_ref[...] = s_pick
    s_small_ref[...] = times(hot_t_ref[...], s_pick).astype(BF16)
    base_ref[...] = picked_ref[...].astype(F32) - times((state * inner_ref[:1]).astype(BF16), s_pick)


def update_kernel(trips, links, plan, *refs):
    arrived_refs, refs = refs[:trips], refs[trips:]
    hot_ref, n_ref, weight_ref, mask_ref, inner_ref, local_ref, picked_ref, s_pick_ref, state_ref = refs[:9]
    state_out_ref, base_ref = refs[9:]
    state = state_ref[...] + DAMPING * corrected(links, plan, arrived_refs, hot_ref, n_ref, weight_ref, mask_ref, local_ref)
    state_out_ref[...] = state
    base_ref[...] = picked_ref[...].astype(F32) - times((state * inner_ref[:1]).astype(BF16), s_pick_ref[...])


def last_update_kernel(trips, links, plan, *refs):
    arrived_refs, refs = refs[:trips], refs[trips:]
    hot_ref, n_ref, weight_ref, mask_ref, local_ref, state_ref, state_out_ref = refs
    update = corrected(links, plan, arrived_refs, hot_ref, n_ref, weight_ref, mask_ref, local_ref)
    state_out_ref[...] = (state_ref[...] + DAMPING * update).T


def residual_kernel(trips, links, plan, *refs):
    arrived_refs, refs = refs[:trips], refs[trips:]
    hot_ref, s_ref, turned_ref, weight_ref, mask_ref, inner_ref, n_pick_ref, state_ref = refs[:8]
    state_out_ref, local_ref, base_ref = refs[8:]
    state = state_ref[...] + DAMPING * times_t(gather(links, plan, arrived_refs), hot_ref[...])
    state_out_ref[...] = state
    local = mask_ref[:1] * (turned_ref[...].astype(F32) - times(state.astype(BF16), s_ref[0]))
    local_ref[...] = local
    base_ref[...] = times_t((weight_ref[...] * local * inner_ref[:1]).astype(BF16), n_pick_ref[...])


def close_kernel(trips, links, plan, *refs):
    arrived_refs, (hot_ref, state_ref, out_ref, piece_ref, sems) = refs[:trips], refs[trips:]
    arrived = gather(links, plan, arrived_refs)
    rows = state_ref.shape[0] // PIECES
    copies = []
    for k in range(PIECES):
        part = pl.ds(k * rows, rows)
        piece_ref[part, :] = state_ref[part, :] + DAMPING * times_t(hot_ref[part, :], arrived)
        copies.append(pltpu.make_async_copy(piece_ref.at[part, :], out_ref.at[0, part, :], sems.at[k]))
        copies[k].start()
    for copy in copies:
        copy.wait()


def run(kernel, operands, results, flops, spaces=(), outputs=pltpu.VMEM, scratch=()):
    spaces = [dict(spaces).get(k, pltpu.VMEM) for k in range(len(operands))]
    moved = sum(a.size * a.dtype.itemsize for a in (*operands, *results))
    operands = [
        pltpu.with_memory_space_constraint(a, space) if space is pltpu.HBM else a for a, space in zip(operands, spaces)
    ]
    return pl.pallas_call(
        kernel,
        out_shape=results,
        in_specs=[pl.BlockSpec(memory_space=space) for space in spaces],
        out_specs=[pl.BlockSpec(memory_space=outputs)] * len(results),
        scratch_shapes=scratch,
        compiler_params=pltpu.CompilerParams(vmem_limit_bytes=LIMIT),
        cost_estimate=pl.CostEstimate(flops=flops, bytes_accessed=moved, transcendentals=0),
    )(*operands)


def body(right_side, schur, neumann, weights, neighbours, counts, shared_rows):
    width, leads = right_side.shape[1:]
    share = shared_rows.shape[2]
    subs = lax.axis_size("sub")
    plans = [min(k, len(PLANS) - 1) for k in range(2 * ITERS)]
    trips = len(swaps(subs, plans[0]))
    links = len(slots_of(0, subs))
    total = links * share

    def array(rows, columns, kind=F32):
        return jax.ShapeDtypeStruct((rows, columns), kind)

    def same_as(a):
        return jax.ShapeDtypeStruct(a.shape, a.dtype)

    messages = [array(leads, share, BF16)] * trips
    full, some = array(leads, width), array(leads, total)
    small = array(total, total, BF16)
    row = array(8, width)
    picks = 2 * leads * total * width
    whole = 2 * leads * width * width
    path = 4 * leads * total * total

    def exchange(parts, plan):
        return [lax.ppermute(part, "sub", route) for part, route in zip(parts, swaps(subs, plan))]

    def bound(kernel, *settings):
        return functools.partial(kernel, trips, links, *settings)

    hot, turned, picked, listed, weight, n_mat, *sent = run(
        bound(open_kernel, plans[0], subs),
        [shared_rows, neighbours, right_side, weights, neumann],
        [
            array(width, total, BF16),
            array(leads, width, BF16),
            array(leads, total, BF16),
            array(8, total),
            same_as(weights),
            same_as(neumann),
            *messages,
        ],
        picks,
        spaces={k: pltpu.HBM for k in range(5)},
        scratch=[
            pltpu.VMEM(shared_rows.shape, jnp.int32),
            pltpu.VMEM(neighbours.shape, jnp.int32),
            pltpu.VMEM(right_side.shape, BF16),
            pltpu.SemaphoreType.DMA((5,)),
        ],
    )
    arrived = exchange(sent, plans[0])
    hot_t, n_pick, n_small, same, inner, mask, local, base, rows, s_mat = run(
        pick_n_kernel,
        [hot, turned, listed, n_mat, weight, counts, schur],
        [
            array(total, width, BF16),
            array(total, width, BF16),
            small,
            small,
            row,
            row,
            full,
            some,
            array(8, total),
            same_as(schur),
        ],
        2 * total * width * width + 2 * total * total * width + picks,
        spaces={5: pltpu.SMEM, 6: pltpu.HBM},
        scratch=[pltpu.SemaphoreType.DMA],
    )
    near = picked
    near_state = None
    for step in range(ITERS):
        came, last = arrived, step == ITERS - 1
        plan, next_plan, after = (*plans[2 * step :], None)[:3]
        operands = [*came, same, n_small, rows, near, base]
        if step and not last:
            operands.append(near_state)
        kernel = bound(update_path_kernel, plan, next_plan, step, last)
        if last:
            sent = run(kernel, operands, messages, path)
            arrived = exchange(sent, next_plan)
            (state,) = run(
                bound(last_update_kernel, plan),
                [*came, hot, n_mat, weight, mask, local, state],
                [array(width, leads)],
                whole + picks,
            )
            break
        near_state, *sent = run(kernel, operands, [some, *messages], path)
        arrived = exchange(sent, next_plan)
        if step == 0:
            state, base, s_pick, s_small = run(
                bound(first_update_kernel, plan),
                [*came, hot, hot_t, n_mat, s_mat, weight, mask, inner, local, picked],
                [full, some, array(width, total, BF16), small],
                whole + 2 * picks + 2 * total * width * (width + total),
            )
        else:
            state, base = run(
                bound(update_kernel, plan),
                [*came, hot, n_mat, weight, mask, inner, local, picked, s_pick, state],
                [full, some],
                whole + 2 * picks,
            )
        came = arrived
        ends = step == ITERS - 2
        near, *sent = run(
            bound(residual_path_kernel, next_plan, after, ends),
            [*came, same, s_small, rows, base, near_state],
            [some, *([] if ends else [some]), *messages],
            path,
        )
        if not ends:
            near_state, *sent = sent
        arrived = exchange(sent, after)
        state, local, base = run(
            bound(residual_kernel, next_plan),
            [*came, hot, s_mat, turned, weight, mask, inner, n_pick, state],
            [full, full, some],
            whole + 2 * picks,
        )
    (out,) = run(
        bound(close_kernel, plans[-1]),
        [*arrived, hot, state],
        [jax.ShapeDtypeStruct((1, width, leads), F32)],
        picks,
        outputs=pltpu.HBM,
        scratch=[pltpu.VMEM((width, leads), F32), pltpu.SemaphoreType.DMA((PIECES,))],
    )
    return out


def solution(mesh):
    in_specs = (
        P("sub", None, None),
        P("sub", None, None),
        P("sub", None, None),
        P("sub", None),
        P("sub", None),
        P("sub"),
        P("sub", None, None),
    )
    out_specs = P("sub", None, None)
    return jax.shard_map(body, mesh=mesh, in_specs=in_specs, out_specs=out_specs, check_vma=False)
```

```python
import functools

import jax
import jax.numpy as jnp
from jax import lax
from jax.experimental import pallas as pl
from jax.experimental.pallas import tpu as pltpu
from jax.sharding import PartitionSpec as P

ITERS = 4
FAR = 16
DAMPING = 0.7
LIMIT = 16 * 2**20
PIECES = 4
F32 = jnp.float32
BF16 = jnp.bfloat16


PLANS = (
    (
        (0, 1, 2, 0, 2, 2, 2, 0, 0, 0, 0, 1, 2, 2, 2, 2),
        (0, 1, 1, 1, 1, 0, 0, 1, 0, 1, 1, 1, 2, 0, 1),
        (((6, 15), (22, 29)), ((0, 2), (14, 18), (25, 26), (28, 31)), ((3, 7), (19, 23), (24, 27))),
    ),
    (
        (0, 1, 1, 0, 0, 0, 0, 1, 1, 1, 1, 0, 0, 0, 0, 0),
        (0, 2, 1, 0, 0, 1, 2, 1, 0, 1, 1, 0, 0, 1, 1),
        ((), ((0, 3), (4, 13), (14, 31)), ((2, 5), (12, 15))),
    ),
)


def turns(count, plan):
    far_turns, odd_turns, _ = PLANS[plan]
    far = [far_turns[i % FAR] for i in range(count)]
    odd = [odd_turns[(i - 1) // 2] if 0 < i < count - 1 else -1 for i in range(count)]
    return far, odd


def mixed(count):
    return count == 2 * FAR


def swaps(count, plan):
    blocks = count // FAR
    near = [i ^ 1 for i in range(count)]
    far = [i ^ FAR for i in range(count)]
    odd = [(((i + 1) ^ 1) - 1) % count for i in range(count)]
    if mixed(count):
        far_turns, odd_turns = turns(count, plan)
        pairings = []
        for turn, fill in enumerate(PLANS[plan][2]):
            pairing = list(near)
            for i, j in fill:
                pairing[i], pairing[j] = j, i
            for i in range(count):
                if far_turns[i] == turn:
                    pairing[i] = far[i]
                elif odd_turns[i] == turn:
                    pairing[i] = odd[i]
            pairings.append(pairing)
        pairings.append(near)
    else:
        again = [(((i // FAR + 1) ^ 1) - 1) % blocks * FAR + i % FAR for i in range(count)]
        pairings = ([far] if blocks > 1 else []) + ([again] if blocks > 2 else []) + [odd, near]
    for pairing in pairings:
        assert all(pairing[j] == i != j for i, j in enumerate(pairing))
    return [list(enumerate(pairing)) for pairing in pairings]


def is_turn(own_turns, turn):
    bits = sum(1 << i for i, own in enumerate(own_turns) if own == turn)
    bits = bits - (1 << 32) if bits >> 31 else bits
    return lax.shift_right_logical(jnp.int32(bits), lax.axis_index("sub")) & 1 == 1


def slots_of(index, count):
    odd = lax.rem(index, 2)
    block = lax.rem(lax.div(index, FAR), 2)
    blocks = count // FAR
    far = [2 + block] if blocks > 1 else []
    again = [3 - block] if blocks > 2 else []
    return [*far, *again, 1 - odd, odd]


def times(a, b):
    return jnp.dot(a, b, preferred_element_type=F32)


def times_t(a, b):
    return lax.dot_general(a, b, (((1,), (1,)), ((), ())), preferred_element_type=F32)


def gather(links, plan, refs):
    parts = [ref[...] for ref in refs]
    if len(parts) > links:
        values = [part.astype(F32) for part in parts[:3]]
        picked = []
        for own in turns(2 * FAR, plan):
            later = jnp.where(is_turn(own, 1), values[1], values[2])
            picked.append(jnp.where(is_turn(own, 0), values[0], later).astype(BF16))
        parts = [*picked, parts[3]]
    return jnp.concatenate(parts, 1)


def scatter(links, plan, refs, block):
    share = refs[0].shape[1]
    parts = [block[:, k * share : (k + 1) * share].astype(F32) for k in range(links)]
    if len(refs) > links:
        far, odd, near = parts
        own, _ = turns(2 * FAR, plan)
        parts = [*(jnp.where(is_turn(own, turn), far, odd) for turn in range(3)), near]
    for ref, part in zip(refs, parts):
        ref[...] = part.astype(BF16)


def open_kernel(
    trips,
    links,
    plan_out,
    subs,
    rows_in,
    near_in,
    rhs_in,
    weight_in,
    n_in,
    hot_ref,
    turned_ref,
    picked_ref,
    list_ref,
    weight_ref,
    n_ref,
    *refs,
):
    out_refs, (rows_ref, near_ref, rhs_ref, sems) = refs[:trips], refs[trips:]
    pairs = [
        (rows_in, rows_ref),
        (near_in, near_ref),
        (rhs_in, rhs_ref),
        (weight_in, weight_ref),
        (n_in, n_ref),
    ]
    copies = [pltpu.make_async_copy(source, target, sems.at[k]) for k, (source, target) in enumerate(pairs)]
    for copy in copies:
        copy.start()
    width, share = rhs_ref.shape[1], rows_ref.shape[2]
    slots = slots_of(lax.axis_index("sub"), subs)
    place = lax.broadcasted_iota(jnp.int32, (width, share), 0)
    copies[0].wait()
    copies[1].wait()
    near = near_ref[...].astype(F32)
    lane = lax.broadcasted_iota(jnp.int32, near.shape, 1)
    for k, slot in enumerate(slots):
        partner = jnp.sum(jnp.where(lane == slot, near, 0.0), 1, keepdims=True)
        row = jnp.where(partner >= 0.0, rows_ref[0, pl.ds(slot, 1), :], -1)
        list_ref[:, pl.ds(k * share, share)] = jnp.broadcast_to(row.astype(F32), (list_ref.shape[0], share))
        hot_ref[:, pl.ds(k * share, share)] = jnp.where(place == row, 1.0, 0.0).astype(BF16)
    copies[2].wait()
    turned = rhs_ref[0].T
    turned_ref[...] = turned
    picked = times(turned, hot_ref[...]).astype(BF16)
    picked_ref[...] = picked
    scatter(links, plan_out, out_refs, picked)
    for copy in copies[3:]:
        copy.wait()


def pick_n_kernel(
    hot_ref,
    turned_ref,
    list_ref,
    n_ref,
    weight_ref,
    count_ref,
    s_in,
    hot_t_ref,
    n_pick_ref,
    n_small_ref,
    same_ref,
    inner_ref,
    mask_ref,
    local_ref,
    base_ref,
    row_ref,
    s_ref,
    sem,
):
    copy = pltpu.make_async_copy(s_in, s_ref, sem)
    copy.start()
    hot = hot_ref[...]
    width, total = hot.shape
    weight = weight_ref[...]
    side = 128
    listed = list_ref[:1]
    lane = lax.broadcasted_iota(jnp.int32, (side, side), 1).astype(F32)
    hits = [jnp.zeros((1, side), F32)] * (width // side)
    same = []
    for k in range(0, total, side):
        down = jnp.broadcast_to(listed[:, k : k + side], (side, side)).T
        for m in range(width // side):
            block = jnp.where(down == lane + float(m * side), 1.0, 0.0)
            hits[m] = hits[m] + jnp.sum(block, 0, keepdims=True)
            hot_t_ref[k : k + side, m * side : (m + 1) * side] = block.astype(BF16)
        wide = jnp.concatenate([down] * (total // side), 1)
        same.append(jnp.where((wide == listed) & (wide >= 0.0), 1.0, 0.0))
    same = jnp.concatenate(same, 0)
    same_ref[...] = same.astype(BF16)
    inner = jnp.where(jnp.concatenate(hits, 1) > 0.0, 0.0, 1.0)
    inner_ref[...] = jnp.broadcast_to(inner, inner_ref.shape)
    n_pick = times(hot_t_ref[...], n_ref[0]).astype(BF16)
    n_pick_ref[...] = n_pick
    n_small_ref[...] = times(n_pick, hot).astype(BF16)
    earlier = lax.broadcasted_iota(jnp.int32, same.shape, 0) < lax.broadcasted_iota(jnp.int32, same.shape, 1)
    repeats = jnp.sum(jnp.where(earlier, same, 0.0), 0, keepdims=True)
    first = jnp.where(repeats > 0.0, 0.0, 1.0)
    high = weight.astype(BF16).astype(F32)
    middle = (weight - high).astype(BF16).astype(F32)
    low = weight - high - middle
    level = lax.broadcasted_iota(jnp.int32, (8, width), 0)
    pieces = jnp.where(level == 0, high, jnp.where(level == 1, middle, jnp.where(level == 2, low, 0.0)))
    pieces = times(pieces.astype(BF16), hot)
    chosen = (pieces[0:1] + pieces[1:2]) + pieces[2:3]
    row_ref[0:1] = chosen
    row_ref[1:2] = chosen * first
    row_ref[2:3] = first
    row_ref[3:8] = jnp.zeros((5, total), F32)
    mask = jnp.where(lax.broadcasted_iota(jnp.int32, mask_ref.shape, 1) < count_ref[0], 1.0, 0.0)
    mask_ref[...] = mask
    local = mask[:1] * turned_ref[...].astype(F32)
    local_ref[...] = local
    base_ref[...] = times_t((weight * local * inner).astype(BF16), n_pick)
    copy.wait()


def update_path_kernel(trips, links, plan, plan_out, step, last, *refs):
    arrived_refs, refs = refs[:trips], refs[trips:]
    same_ref, n_small_ref, row_ref, local_ref, base_ref = refs[:5]
    refs = refs[5:]
    residual = local_ref[...].astype(F32) + times(gather(links, plan, arrived_refs), same_ref[...])
    scaled = (row_ref[1:2] * residual).astype(BF16)
    sent = row_ref[0:1] * (base_ref[...] + times_t(scaled, n_small_ref[...]))
    if last:
        scatter(links, plan_out, refs, sent)
    elif step == 0:
        scatter(links, plan_out, refs[1:], sent)
        refs[0][...] = DAMPING * sent
    else:
        scatter(links, plan_out, refs[2:], sent)
        refs[1][...] = refs[0][...] + DAMPING * sent


def residual_path_kernel(trips, links, plan, plan_out, last, *refs):
    arrived_refs, refs = refs[:trips], refs[trips:]
    same_ref, s_small_ref, row_ref, base_ref, state_ref, local_ref = refs[:6]
    state = state_ref[...] + DAMPING * times(gather(links, plan, arrived_refs), same_ref[...])
    if last:
        refs = refs[6:]
    else:
        refs[6][...] = state
        refs = refs[7:]
    local = base_ref[...] - times((state * row_ref[2:3]).astype(BF16), s_small_ref[...])
    local_ref[...] = local
    scatter(links, plan_out, refs, local)


def corrected(links, plan, arrived_refs, hot_ref, n_ref, weight_ref, mask_ref, local_ref):
    weight = weight_ref[...]
    residual = local_ref[...] + times_t(gather(links, plan, arrived_refs), hot_ref[...])
    scaled = (weight * residual).astype(BF16)
    return mask_ref[:1] * weight * times_t(scaled, n_ref[0])


def first_update_kernel(trips, links, plan, *refs):
    arrived_refs, refs = refs[:trips], refs[trips:]
    hot_ref, hot_t_ref, n_ref, s_ref, weight_ref, mask_ref, inner_ref, local_ref, picked_ref = refs[:9]
    state_out_ref, base_ref, s_pick_ref, s_small_ref = refs[9:]
    state = DAMPING * corrected(links, plan, arrived_refs, hot_ref, n_ref, weight_ref, mask_ref, local_ref)
    state_out_ref[...] = state
    s_pick = times(s_ref[0], hot_ref[...]).astype(BF16)
    s_pick_ref[...] = s_pick
    s_small_ref[...] = times(hot_t_ref[...], s_pick).astype(BF16)
    base_ref[...] = picked_ref[...].astype(F32) - times((state * inner_ref[:1]).astype(BF16), s_pick)


def update_kernel(trips, links, plan, *refs):
    arrived_refs, refs = refs[:trips], refs[trips:]
    hot_ref, n_ref, weight_ref, mask_ref, inner_ref, local_ref, picked_ref, s_pick_ref, state_ref = refs[:9]
    state_out_ref, base_ref = refs[9:]
    state = state_ref[...] + DAMPING * corrected(links, plan, arrived_refs, hot_ref, n_ref, weight_ref, mask_ref, local_ref)
    state_out_ref[...] = state
    base_ref[...] = picked_ref[...].astype(F32) - times((state * inner_ref[:1]).astype(BF16), s_pick_ref[...])


def last_update_kernel(trips, links, plan, *refs):
    arrived_refs, refs = refs[:trips], refs[trips:]
    hot_ref, n_ref, weight_ref, mask_ref, local_ref, state_ref, state_out_ref = refs
    update = corrected(links, plan, arrived_refs, hot_ref, n_ref, weight_ref, mask_ref, local_ref)
    state_out_ref[...] = (state_ref[...] + DAMPING * update).T


def residual_kernel(trips, links, plan, *refs):
    arrived_refs, refs = refs[:trips], refs[trips:]
    hot_ref, s_ref, turned_ref, weight_ref, mask_ref, inner_ref, n_pick_ref, state_ref = refs[:8]
    state_out_ref, local_ref, base_ref = refs[8:]
    state = state_ref[...] + DAMPING * times_t(gather(links, plan, arrived_refs), hot_ref[...])
    state_out_ref[...] = state
    local = mask_ref[:1] * (turned_ref[...].astype(F32) - times(state.astype(BF16), s_ref[0]))
    local_ref[...] = local
    base_ref[...] = times_t((weight_ref[...] * local * inner_ref[:1]).astype(BF16), n_pick_ref[...])


def close_kernel(trips, links, plan, *refs):
    arrived_refs, (hot_ref, state_ref, out_ref, piece_ref, sems) = refs[:trips], refs[trips:]
    arrived = gather(links, plan, arrived_refs)
    rows = state_ref.shape[0] // PIECES
    copies = []
    for k in range(PIECES):
        part = pl.ds(k * rows, rows)
        piece_ref[part, :] = state_ref[part, :] + DAMPING * times_t(hot_ref[part, :], arrived)
        copies.append(pltpu.make_async_copy(piece_ref.at[part, :], out_ref.at[0, part, :], sems.at[k]))
        copies[k].start()
    for copy in copies:
        copy.wait()


def run(kernel, operands, results, flops, spaces=(), outputs=pltpu.VMEM, scratch=()):
    spaces = [dict(spaces).get(k, pltpu.VMEM) for k in range(len(operands))]
    moved = sum(a.size * a.dtype.itemsize for a in (*operands, *results))
    operands = [
        pltpu.with_memory_space_constraint(a, space) if space is pltpu.HBM else a for a, space in zip(operands, spaces)
    ]
    return pl.pallas_call(
        kernel,
        out_shape=results,
        in_specs=[pl.BlockSpec(memory_space=space) for space in spaces],
        out_specs=[pl.BlockSpec(memory_space=outputs)] * len(results),
        scratch_shapes=scratch,
        compiler_params=pltpu.CompilerParams(vmem_limit_bytes=LIMIT),
        cost_estimate=pl.CostEstimate(flops=flops, bytes_accessed=moved, transcendentals=0),
    )(*operands)


def body(right_side, schur, neumann, weights, neighbours, counts, shared_rows):
    width, leads = right_side.shape[1:]
    share = shared_rows.shape[2]
    subs = lax.axis_size("sub")
    plans = [min(k // 2, len(PLANS) - 1) for k in range(2 * ITERS)]
    trips = len(swaps(subs, plans[0]))
    links = len(slots_of(0, subs))
    total = links * share

    def array(rows, columns, kind=F32):
        return jax.ShapeDtypeStruct((rows, columns), kind)

    def same_as(a):
        return jax.ShapeDtypeStruct(a.shape, a.dtype)

    messages = [array(leads, share, BF16)] * trips
    full, some = array(leads, width), array(leads, total)
    small = array(total, total, BF16)
    row = array(8, width)
    picks = 2 * leads * total * width
    whole = 2 * leads * width * width
    path = 4 * leads * total * total

    def exchange(parts, plan):
        return [lax.ppermute(part, "sub", route) for part, route in zip(parts, swaps(subs, plan))]

    def bound(kernel, *settings):
        return functools.partial(kernel, trips, links, *settings)

    hot, turned, picked, listed, weight, n_mat, *sent = run(
        bound(open_kernel, plans[0], subs),
        [shared_rows, neighbours, right_side, weights, neumann],
        [
            array(width, total, BF16),
            array(leads, width, BF16),
            array(leads, total, BF16),
            array(8, total),
            same_as(weights),
            same_as(neumann),
            *messages,
        ],
        picks,
        spaces={k: pltpu.HBM for k in range(5)},
        scratch=[
            pltpu.VMEM(shared_rows.shape, jnp.int32),
            pltpu.VMEM(neighbours.shape, jnp.int32),
            pltpu.VMEM(right_side.shape, BF16),
            pltpu.SemaphoreType.DMA((5,)),
        ],
    )
    arrived = exchange(sent, plans[0])
    hot_t, n_pick, n_small, same, inner, mask, local, base, rows, s_mat = run(
        pick_n_kernel,
        [hot, turned, listed, n_mat, weight, counts, schur],
        [
            array(total, width, BF16),
            array(total, width, BF16),
            small,
            small,
            row,
            row,
            full,
            some,
            array(8, total),
            same_as(schur),
        ],
        2 * total * width * width + 2 * total * total * width + picks,
        spaces={5: pltpu.SMEM, 6: pltpu.HBM},
        scratch=[pltpu.SemaphoreType.DMA],
    )
    near = picked
    near_state = None
    for step in range(ITERS):
        came, last = arrived, step == ITERS - 1
        plan, next_plan, after = (*plans[2 * step :], None)[:3]
        operands = [*came, same, n_small, rows, near, base]
        if step and not last:
            operands.append(near_state)
        kernel = bound(update_path_kernel, plan, next_plan, step, last)
        if last:
            sent = run(kernel, operands, messages, path)
            arrived = exchange(sent, next_plan)
            (state,) = run(
                bound(last_update_kernel, plan),
                [*came, hot, n_mat, weight, mask, local, state],
                [array(width, leads)],
                whole + picks,
            )
            break
        near_state, *sent = run(kernel, operands, [some, *messages], path)
        arrived = exchange(sent, next_plan)
        if step == 0:
            state, base, s_pick, s_small = run(
                bound(first_update_kernel, plan),
                [*came, hot, hot_t, n_mat, s_mat, weight, mask, inner, local, picked],
                [full, some, array(width, total, BF16), small],
                whole + 2 * picks + 2 * total * width * (width + total),
            )
        else:
            state, base = run(
                bound(update_kernel, plan),
                [*came, hot, n_mat, weight, mask, inner, local, picked, s_pick, state],
                [full, some],
                whole + 2 * picks,
            )
        came = arrived
        ends = step == ITERS - 2
        near, *sent = run(
            bound(residual_path_kernel, next_plan, after, ends),
            [*came, same, s_small, rows, base, near_state],
            [some, *([] if ends else [some]), *messages],
            path,
        )
        if not ends:
            near_state, *sent = sent
        arrived = exchange(sent, after)
        state, local, base = run(
            bound(residual_kernel, next_plan),
            [*came, hot, s_mat, turned, weight, mask, inner, n_pick, state],
            [full, full, some],
            whole + 2 * picks,
        )
    (out,) = run(
        bound(close_kernel, plans[-1]),
        [*arrived, hot, state],
        [jax.ShapeDtypeStruct((1, width, leads), F32)],
        picks,
        outputs=pltpu.HBM,
        scratch=[pltpu.VMEM((width, leads), F32), pltpu.SemaphoreType.DMA((PIECES,))],
    )
    return out


def solution(mesh):
    in_specs = (
        P("sub", None, None),
        P("sub", None, None),
        P("sub", None, None),
        P("sub", None),
        P("sub", None),
        P("sub"),
        P("sub", None, None),
    )
    out_specs = P("sub", None, None)
    return jax.shard_map(body, mesh=mesh, in_specs=in_specs, out_specs=out_specs, check_vma=False)
```

```python
import functools

import jax
import jax.numpy as jnp
from jax import lax
from jax.experimental import pallas as pl
from jax.experimental.pallas import tpu as pltpu
from jax.sharding import PartitionSpec as P

ITERS = 4
FAR = 16
DAMPING = 0.7
LIMIT = 16 * 2**20
PIECES = 4
F32 = jnp.float32
BF16 = jnp.bfloat16


FAR_TURNS = (0, 0, 0, 0, 0, 2, 1, 1, 1, 0, 0, 0, 0, 0, 1, 2)
ODD_TURNS = (1, 1, 0, 0, 1, 1, 2, 1, 1, 1, 0, 0, 1, 1, 2)
FILL = ((), ((0, 5), (13, 21), (29, 31)), ((4, 12), (20, 28)))


def turns(count):
    far = [FAR_TURNS[i % FAR] for i in range(count)]
    odd = [ODD_TURNS[(i - 1) // 2] if 0 < i < count - 1 else -1 for i in range(count)]
    return far, odd


def mixed(count):
    return count == 2 * FAR


def swaps(count):
    blocks = count // FAR
    near = [i ^ 1 for i in range(count)]
    far = [i ^ FAR for i in range(count)]
    odd = [(((i + 1) ^ 1) - 1) % count for i in range(count)]
    if mixed(count):
        far_turns, odd_turns = turns(count)
        pairings = []
        for turn, fill in enumerate(FILL):
            pairing = list(near)
            for i, j in fill:
                pairing[i], pairing[j] = j, i
            for i in range(count):
                if far_turns[i] == turn:
                    pairing[i] = far[i]
                elif odd_turns[i] == turn:
                    pairing[i] = odd[i]
            pairings.append(pairing)
        pairings.append(near)
    else:
        again = [(((i // FAR + 1) ^ 1) - 1) % blocks * FAR + i % FAR for i in range(count)]
        pairings = ([far] if blocks > 1 else []) + ([again] if blocks > 2 else []) + [odd, near]
    for pairing in pairings:
        assert all(pairing[j] == i != j for i, j in enumerate(pairing))
    return [list(enumerate(pairing)) for pairing in pairings]


def is_turn(own_turns, turn):
    bits = sum(1 << i for i, own in enumerate(own_turns) if own == turn)
    bits = bits - (1 << 32) if bits >> 31 else bits
    return lax.shift_right_logical(jnp.int32(bits), lax.axis_index("sub")) & 1 == 1


def slots_of(index, count):
    odd = lax.rem(index, 2)
    block = lax.rem(lax.div(index, FAR), 2)
    blocks = count // FAR
    far = [2 + block] if blocks > 1 else []
    again = [3 - block] if blocks > 2 else []
    return [*far, *again, 1 - odd, odd]


def times(a, b):
    return jnp.dot(a, b, preferred_element_type=F32)


def times_t(a, b):
    return lax.dot_general(a, b, (((1,), (1,)), ((), ())), preferred_element_type=F32)


def gather(links, refs):
    parts = [ref[...] for ref in refs]
    if len(parts) > links:
        values = [part.astype(F32) for part in parts[:3]]
        picked = []
        for own in turns(2 * FAR):
            later = jnp.where(is_turn(own, 1), values[1], values[2])
            picked.append(jnp.where(is_turn(own, 0), values[0], later).astype(BF16))
        parts = [*picked, parts[3]]
    return jnp.concatenate(parts, 1)


def scatter(links, refs, block):
    share = refs[0].shape[1]
    parts = [block[:, k * share : (k + 1) * share].astype(F32) for k in range(links)]
    if len(refs) > links:
        far, odd, near = parts
        own, _ = turns(2 * FAR)
        parts = [*(jnp.where(is_turn(own, turn), far, odd) for turn in range(3)), near]
    for ref, part in zip(refs, parts):
        ref[...] = part.astype(BF16)


def open_kernel(
    trips,
    links,
    subs,
    rows_in,
    near_in,
    rhs_in,
    weight_in,
    n_in,
    hot_ref,
    turned_ref,
    picked_ref,
    list_ref,
    weight_ref,
    n_ref,
    *refs,
):
    out_refs, (rows_ref, near_ref, rhs_ref, sems) = refs[:trips], refs[trips:]
    pairs = [
        (rows_in, rows_ref),
        (near_in, near_ref),
        (rhs_in, rhs_ref),
        (weight_in, weight_ref),
        (n_in.at[0, :, pl.ds(0, n_ref.shape[1])], n_ref),
    ]
    copies = [pltpu.make_async_copy(source, target, sems.at[k]) for k, (source, target) in enumerate(pairs)]
    for copy in copies:
        copy.start()
    width, share = rhs_ref.shape[1], rows_ref.shape[2]
    slots = slots_of(lax.axis_index("sub"), subs)
    place = lax.broadcasted_iota(jnp.int32, (width, share), 0)
    copies[0].wait()
    copies[1].wait()
    near = near_ref[...].astype(F32)
    lane = lax.broadcasted_iota(jnp.int32, near.shape, 1)
    for k, slot in enumerate(slots):
        partner = jnp.sum(jnp.where(lane == slot, near, 0.0), 1, keepdims=True)
        row = jnp.where(partner >= 0.0, rows_ref[0, pl.ds(slot, 1), :], -1)
        list_ref[:, pl.ds(k * share, share)] = jnp.broadcast_to(row.astype(F32), (list_ref.shape[0], share))
        hot_ref[:, pl.ds(k * share, share)] = jnp.where(place == row, 1.0, 0.0).astype(BF16)
    copies[2].wait()
    turned = rhs_ref[0].T
    turned_ref[...] = turned
    picked = times(turned, hot_ref[...]).astype(BF16)
    picked_ref[...] = picked
    scatter(links, out_refs, picked)
    for copy in copies[3:]:
        copy.wait()


def pick_n_kernel(
    hot_ref,
    turned_ref,
    list_ref,
    n_ref,
    weight_ref,
    count_ref,
    n_in,
    s_in,
    hot_t_ref,
    n_pick_ref,
    n_small_ref,
    same_ref,
    inner_ref,
    mask_ref,
    local_ref,
    base_ref,
    row_ref,
    n_rest_ref,
    s_ref,
    sems,
):
    half = n_rest_ref.shape[1]
    rest_copy = pltpu.make_async_copy(n_in.at[0, :, pl.ds(half, half)], n_rest_ref, sems.at[0])
    s_copy = pltpu.make_async_copy(s_in, s_ref, sems.at[1])
    rest_copy.start()
    s_copy.start()
    hot = hot_ref[...]
    width, total = hot.shape
    weight = weight_ref[...]
    side = 128
    listed = list_ref[:1]
    lane = lax.broadcasted_iota(jnp.int32, (side, side), 1).astype(F32)
    hits = [jnp.zeros((1, side), F32)] * (width // side)
    same = []
    for k in range(0, total, side):
        down = jnp.broadcast_to(listed[:, k : k + side], (side, side)).T
        for m in range(width // side):
            block = jnp.where(down == lane + float(m * side), 1.0, 0.0)
            hits[m] = hits[m] + jnp.sum(block, 0, keepdims=True)
            hot_t_ref[k : k + side, m * side : (m + 1) * side] = block.astype(BF16)
        wide = jnp.concatenate([down] * (total // side), 1)
        same.append(jnp.where((wide == listed) & (wide >= 0.0), 1.0, 0.0))
    same = jnp.concatenate(same, 0)
    same_ref[...] = same.astype(BF16)
    inner = jnp.where(jnp.concatenate(hits, 1) > 0.0, 0.0, 1.0)
    inner_ref[...] = jnp.broadcast_to(inner, inner_ref.shape)
    n_pick_ref[:, :half] = times(hot_t_ref[...], n_ref[...]).astype(BF16)
    earlier = lax.broadcasted_iota(jnp.int32, same.shape, 0) < lax.broadcasted_iota(jnp.int32, same.shape, 1)
    repeats = jnp.sum(jnp.where(earlier, same, 0.0), 0, keepdims=True)
    first = jnp.where(repeats > 0.0, 0.0, 1.0)
    high = weight.astype(BF16).astype(F32)
    middle = (weight - high).astype(BF16).astype(F32)
    low = weight - high - middle
    level = lax.broadcasted_iota(jnp.int32, (8, width), 0)
    pieces = jnp.where(level == 0, high, jnp.where(level == 1, middle, jnp.where(level == 2, low, 0.0)))
    pieces = times(pieces.astype(BF16), hot)
    chosen = (pieces[0:1] + pieces[1:2]) + pieces[2:3]
    row_ref[0:1] = chosen
    row_ref[1:2] = chosen * first
    row_ref[2:3] = first
    row_ref[3:8] = jnp.zeros((5, total), F32)
    rest_copy.wait()
    n_pick_ref[:, half:] = times(hot_t_ref[...], n_rest_ref[...]).astype(BF16)
    n_pick = n_pick_ref[...]
    n_small_ref[...] = times(n_pick, hot).astype(BF16)
    mask = jnp.where(lax.broadcasted_iota(jnp.int32, mask_ref.shape, 1) < count_ref[0], 1.0, 0.0)
    mask_ref[...] = mask
    local = mask[:1] * turned_ref[...].astype(F32)
    local_ref[...] = local
    base_ref[...] = times_t((weight * local * inner).astype(BF16), n_pick)
    s_copy.wait()


def update_path_kernel(trips, links, step, last, *refs):
    arrived_refs, refs = refs[:trips], refs[trips:]
    same_ref, n_small_ref, row_ref, local_ref, base_ref = refs[:5]
    refs = refs[5:]
    residual = local_ref[...].astype(F32) + times(gather(links, arrived_refs), same_ref[...])
    scaled = (row_ref[1:2] * residual).astype(BF16)
    sent = row_ref[0:1] * (base_ref[...] + times_t(scaled, n_small_ref[...]))
    if last:
        scatter(links, refs, sent)
    elif step == 0:
        scatter(links, refs[1:], sent)
        refs[0][...] = DAMPING * sent
    else:
        scatter(links, refs[2:], sent)
        refs[1][...] = refs[0][...] + DAMPING * sent


def residual_path_kernel(trips, links, last, *refs):
    arrived_refs, refs = refs[:trips], refs[trips:]
    same_ref, s_small_ref, row_ref, base_ref, state_ref, local_ref = refs[:6]
    state = state_ref[...] + DAMPING * times(gather(links, arrived_refs), same_ref[...])
    if last:
        refs = refs[6:]
    else:
        refs[6][...] = state
        refs = refs[7:]
    local = base_ref[...] - times((state * row_ref[2:3]).astype(BF16), s_small_ref[...])
    local_ref[...] = local
    scatter(links, refs, local)


def corrected(links, arrived_refs, hot_ref, n_ref, n_rest_ref, weight_ref, mask_ref, local_ref):
    weight = weight_ref[...]
    residual = local_ref[...] + times_t(gather(links, arrived_refs), hot_ref[...])
    scaled = (weight * residual).astype(BF16)
    half = n_ref.shape[1]
    product = times_t(scaled[:, :half], n_ref[...]) + times_t(scaled[:, half:], n_rest_ref[...])
    return mask_ref[:1] * weight * product


def first_update_kernel(trips, links, *refs):
    arrived_refs, refs = refs[:trips], refs[trips:]
    hot_ref, hot_t_ref, n_ref, n_rest_ref, s_ref, weight_ref, mask_ref, inner_ref, local_ref, picked_ref = refs[:10]
    state_out_ref, base_ref, s_pick_ref, s_small_ref = refs[10:]
    state = DAMPING * corrected(links, arrived_refs, hot_ref, n_ref, n_rest_ref, weight_ref, mask_ref, local_ref)
    state_out_ref[...] = state
    s_pick = times(s_ref[0], hot_ref[...]).astype(BF16)
    s_pick_ref[...] = s_pick
    s_small_ref[...] = times(hot_t_ref[...], s_pick).astype(BF16)
    base_ref[...] = picked_ref[...].astype(F32) - times((state * inner_ref[:1]).astype(BF16), s_pick)


def update_kernel(trips, links, *refs):
    arrived_refs, refs = refs[:trips], refs[trips:]
    hot_ref, n_ref, n_rest_ref, weight_ref, mask_ref, inner_ref, local_ref, picked_ref, s_pick_ref, state_ref = refs[:10]
    state_out_ref, base_ref = refs[10:]
    state = state_ref[...] + DAMPING * corrected(links, arrived_refs, hot_ref, n_ref, n_rest_ref, weight_ref, mask_ref, local_ref)
    state_out_ref[...] = state
    base_ref[...] = picked_ref[...].astype(F32) - times((state * inner_ref[:1]).astype(BF16), s_pick_ref[...])


def last_update_kernel(trips, links, *refs):
    arrived_refs, refs = refs[:trips], refs[trips:]
    hot_ref, n_ref, n_rest_ref, weight_ref, mask_ref, local_ref, state_ref, state_out_ref = refs
    update = corrected(links, arrived_refs, hot_ref, n_ref, n_rest_ref, weight_ref, mask_ref, local_ref)
    state_out_ref[...] = (state_ref[...] + DAMPING * update).T


def residual_kernel(trips, links, *refs):
    arrived_refs, refs = refs[:trips], refs[trips:]
    hot_ref, s_ref, turned_ref, weight_ref, mask_ref, inner_ref, n_pick_ref, state_ref = refs[:8]
    state_out_ref, local_ref, base_ref = refs[8:]
    state = state_ref[...] + DAMPING * times_t(gather(links, arrived_refs), hot_ref[...])
    state_out_ref[...] = state
    local = mask_ref[:1] * (turned_ref[...].astype(F32) - times(state.astype(BF16), s_ref[0]))
    local_ref[...] = local
    base_ref[...] = times_t((weight_ref[...] * local * inner_ref[:1]).astype(BF16), n_pick_ref[...])


def close_kernel(trips, links, *refs):
    arrived_refs, (hot_ref, state_ref, out_ref, piece_ref, sems) = refs[:trips], refs[trips:]
    arrived = gather(links, arrived_refs)
    rows = state_ref.shape[0] // PIECES
    copies = []
    for k in range(PIECES):
        part = pl.ds(k * rows, rows)
        piece_ref[part, :] = state_ref[part, :] + DAMPING * times_t(hot_ref[part, :], arrived)
        copies.append(pltpu.make_async_copy(piece_ref.at[part, :], out_ref.at[0, part, :], sems.at[k]))
        copies[k].start()
    for copy in copies:
        copy.wait()


def run(kernel, operands, results, flops, spaces=(), outputs=pltpu.VMEM, scratch=()):
    spaces = [dict(spaces).get(k, pltpu.VMEM) for k in range(len(operands))]
    moved = sum(a.size * a.dtype.itemsize for a in (*operands, *results))
    operands = [
        pltpu.with_memory_space_constraint(a, space) if space is pltpu.HBM else a for a, space in zip(operands, spaces)
    ]
    return pl.pallas_call(
        kernel,
        out_shape=results,
        in_specs=[pl.BlockSpec(memory_space=space) for space in spaces],
        out_specs=[pl.BlockSpec(memory_space=outputs)] * len(results),
        scratch_shapes=scratch,
        compiler_params=pltpu.CompilerParams(vmem_limit_bytes=LIMIT),
        cost_estimate=pl.CostEstimate(flops=flops, bytes_accessed=moved, transcendentals=0),
    )(*operands)


def body(right_side, schur, neumann, weights, neighbours, counts, shared_rows):
    width, leads = right_side.shape[1:]
    share = shared_rows.shape[2]
    subs = lax.axis_size("sub")
    routes = swaps(subs)
    trips = len(routes)
    links = len(slots_of(0, subs))
    total = links * share

    def array(rows, columns, kind=F32):
        return jax.ShapeDtypeStruct((rows, columns), kind)

    def same_as(a):
        return jax.ShapeDtypeStruct(a.shape, a.dtype)

    messages = [array(leads, share, BF16)] * trips
    full, some = array(leads, width), array(leads, total)
    small = array(total, total, BF16)
    row = array(8, width)
    half = array(width, width // 2, BF16)
    picks = 2 * leads * total * width
    whole = 2 * leads * width * width
    path = 4 * leads * total * total

    def exchange(parts):
        return [lax.ppermute(part, "sub", route) for part, route in zip(parts, routes)]

    def bound(kernel, *settings):
        return functools.partial(kernel, trips, links, *settings)

    hot, turned, picked, listed, weight, n_mat, *sent = run(
        bound(open_kernel, subs),
        [shared_rows, neighbours, right_side, weights, neumann],
        [
            array(width, total, BF16),
            array(leads, width, BF16),
            array(leads, total, BF16),
            array(8, total),
            same_as(weights),
            half,
            *messages,
        ],
        picks,
        spaces={k: pltpu.HBM for k in range(5)},
        scratch=[
            pltpu.VMEM(shared_rows.shape, jnp.int32),
            pltpu.VMEM(neighbours.shape, jnp.int32),
            pltpu.VMEM(right_side.shape, BF16),
            pltpu.SemaphoreType.DMA((5,)),
        ],
    )
    arrived = exchange(sent)
    hot_t, n_pick, n_small, same, inner, mask, local, base, rows, n_rest, s_mat = run(
        pick_n_kernel,
        [hot, turned, listed, n_mat, weight, counts, neumann, schur],
        [
            array(total, width, BF16),
            array(total, width, BF16),
            small,
            small,
            row,
            row,
            full,
            some,
            array(8, total),
            half,
            same_as(schur),
        ],
        2 * total * width * width + 2 * total * total * width + picks,
        spaces={5: pltpu.SMEM, 6: pltpu.HBM, 7: pltpu.HBM},
        scratch=[pltpu.SemaphoreType.DMA((2,))],
    )
    near = picked
    near_state = None
    for step in range(ITERS):
        came, last = arrived, step == ITERS - 1
        operands = [*came, same, n_small, rows, near, base]
        if step and not last:
            operands.append(near_state)
        kernel = bound(update_path_kernel, step, last)
        if last:
            sent = run(kernel, operands, messages, path)
            arrived = exchange(sent)
            (state,) = run(
                bound(last_update_kernel),
                [*came, hot, n_mat, n_rest, weight, mask, local, state],
                [array(width, leads)],
                whole + picks,
            )
            break
        near_state, *sent = run(kernel, operands, [some, *messages], path)
        arrived = exchange(sent)
        if step == 0:
            state, base, s_pick, s_small = run(
                bound(first_update_kernel),
                [*came, hot, hot_t, n_mat, n_rest, s_mat, weight, mask, inner, local, picked],
                [full, some, array(width, total, BF16), small],
                whole + 2 * picks + 2 * total * width * (width + total),
            )
        else:
            state, base = run(
                bound(update_kernel),
                [*came, hot, n_mat, n_rest, weight, mask, inner, local, picked, s_pick, state],
                [full, some],
                whole + 2 * picks,
            )
        came = arrived
        ends = step == ITERS - 2
        near, *sent = run(
            bound(residual_path_kernel, ends),
            [*came, same, s_small, rows, base, near_state],
            [some, *([] if ends else [some]), *messages],
            path,
        )
        if not ends:
            near_state, *sent = sent
        arrived = exchange(sent)
        state, local, base = run(
            bound(residual_kernel),
            [*came, hot, s_mat, turned, weight, mask, inner, n_pick, state],
            [full, full, some],
            whole + 2 * picks,
        )
    (out,) = run(
        bound(close_kernel),
        [*arrived, hot, state],
        [jax.ShapeDtypeStruct((1, width, leads), F32)],
        picks,
        outputs=pltpu.HBM,
        scratch=[pltpu.VMEM((width, leads), F32), pltpu.SemaphoreType.DMA((PIECES,))],
    )
    return out


def solution(mesh):
    in_specs = (
        P("sub", None, None),
        P("sub", None, None),
        P("sub", None, None),
        P("sub", None),
        P("sub", None),
        P("sub"),
        P("sub", None, None),
    )
    out_specs = P("sub", None, None)
    return jax.shard_map(body, mesh=mesh, in_specs=in_specs, out_specs=out_specs, check_vma=False)
```

```python
import functools

import jax
import jax.numpy as jnp
from jax import lax
from jax.experimental import pallas as pl
from jax.experimental.pallas import tpu as pltpu
from jax.sharding import PartitionSpec as P

ITERS = 4
FAR = 16
DAMPING = 0.7
LIMIT = 16 * 2**20
PIECES = 4
F32 = jnp.float32
BF16 = jnp.bfloat16


PLANS = (
    (
        (0, 1, 2, 0, 2, 2, 2, 0, 0, 0, 0, 1, 2, 2, 2, 2),
        (0, 1, 1, 1, 1, 0, 0, 1, 0, 1, 1, 1, 2, 0, 1),
        (((6, 15), (22, 29)), ((0, 2), (14, 18), (25, 26), (28, 31)), ((3, 7), (19, 23), (24, 27))),
    ),
    (
        (0, 1, 1, 0, 0, 0, 0, 1, 1, 1, 1, 0, 0, 0, 0, 0),
        (0, 2, 1, 0, 0, 1, 2, 1, 0, 1, 1, 0, 0, 1, 1),
        ((), ((0, 3), (4, 13), (14, 31)), ((2, 5), (12, 15))),
    ),
)


def turns(count, plan):
    far_turns, odd_turns, _ = PLANS[plan]
    far = [far_turns[i % FAR] for i in range(count)]
    odd = [odd_turns[(i - 1) // 2] if 0 < i < count - 1 else -1 for i in range(count)]
    return far, odd


def mixed(count):
    return count == 2 * FAR


def swaps(count, plan):
    blocks = count // FAR
    near = [i ^ 1 for i in range(count)]
    far = [i ^ FAR for i in range(count)]
    odd = [(((i + 1) ^ 1) - 1) % count for i in range(count)]
    if mixed(count):
        far_turns, odd_turns = turns(count, plan)
        pairings = []
        for turn, fill in enumerate(PLANS[plan][2]):
            pairing = list(near)
            for i, j in fill:
                pairing[i], pairing[j] = j, i
            for i in range(count):
                if far_turns[i] == turn:
                    pairing[i] = far[i]
                elif odd_turns[i] == turn:
                    pairing[i] = odd[i]
            pairings.append(pairing)
        pairings.append(near)
    else:
        again = [(((i // FAR + 1) ^ 1) - 1) % blocks * FAR + i % FAR for i in range(count)]
        pairings = ([far] if blocks > 1 else []) + ([again] if blocks > 2 else []) + [odd, near]
    for pairing in pairings:
        assert all(pairing[j] == i != j for i, j in enumerate(pairing))
    return [list(enumerate(pairing)) for pairing in pairings]


def is_turn(own_turns, turn):
    bits = sum(1 << i for i, own in enumerate(own_turns) if own == turn)
    bits = bits - (1 << 32) if bits >> 31 else bits
    return lax.shift_right_logical(jnp.int32(bits), lax.axis_index("sub")) & 1 == 1


def slots_of(index, count):
    odd = lax.rem(index, 2)
    block = lax.rem(lax.div(index, FAR), 2)
    blocks = count // FAR
    far = [2 + block] if blocks > 1 else []
    again = [3 - block] if blocks > 2 else []
    return [*far, *again, 1 - odd, odd]


def times(a, b):
    return jnp.dot(a, b, preferred_element_type=F32)


def times_t(a, b):
    return lax.dot_general(a, b, (((1,), (1,)), ((), ())), preferred_element_type=F32)


def gather(links, plan, refs):
    parts = [ref[...] for ref in refs]
    if len(parts) > links:
        values = [part.astype(F32) for part in parts[:3]]
        picked = []
        for own in turns(2 * FAR, plan):
            later = jnp.where(is_turn(own, 1), values[1], values[2])
            picked.append(jnp.where(is_turn(own, 0), values[0], later).astype(BF16))
        parts = [*picked, parts[3]]
    return jnp.concatenate(parts, 1)


def scatter(links, plan, refs, block):
    share = refs[0].shape[1]
    parts = [block[:, k * share : (k + 1) * share].astype(F32) for k in range(links)]
    if len(refs) > links:
        far, odd, near = parts
        own, _ = turns(2 * FAR, plan)
        parts = [*(jnp.where(is_turn(own, turn), far, odd) for turn in range(3)), near]
    for ref, part in zip(refs, parts):
        ref[...] = part.astype(BF16)


def open_kernel(
    trips,
    links,
    plan_out,
    subs,
    rows_in,
    near_in,
    rhs_in,
    weight_in,
    n_in,
    hot_ref,
    turned_ref,
    picked_ref,
    list_ref,
    chosen_ref,
    weight_ref,
    n_ref,
    *refs,
):
    out_refs, (rows_ref, near_ref, rhs_ref, sems) = refs[:trips], refs[trips:]
    pairs = [
        (rows_in, rows_ref),
        (near_in, near_ref),
        (rhs_in, rhs_ref),
        (weight_in, weight_ref),
        (n_in, n_ref),
    ]
    copies = [pltpu.make_async_copy(source, target, sems.at[k]) for k, (source, target) in enumerate(pairs)]
    for copy in copies:
        copy.start()
    width, share = rhs_ref.shape[1], rows_ref.shape[2]
    slots = slots_of(lax.axis_index("sub"), subs)
    place = lax.broadcasted_iota(jnp.int32, (width, share), 0)
    copies[0].wait()
    copies[1].wait()
    near = near_ref[...].astype(F32)
    lane = lax.broadcasted_iota(jnp.int32, near.shape, 1)
    for k, slot in enumerate(slots):
        partner = jnp.sum(jnp.where(lane == slot, near, 0.0), 1, keepdims=True)
        row = jnp.where(partner >= 0.0, rows_ref[0, pl.ds(slot, 1), :], -1)
        list_ref[:, pl.ds(k * share, share)] = jnp.broadcast_to(row.astype(F32), (list_ref.shape[0], share))
        hot_ref[:, pl.ds(k * share, share)] = jnp.where(place == row, 1.0, 0.0).astype(BF16)
    copies[2].wait()
    turned = rhs_ref[0].T
    turned_ref[...] = turned
    copies[3].wait()
    weight = weight_ref[...]
    high = weight.astype(BF16).astype(F32)
    middle = (weight - high).astype(BF16).astype(F32)
    low = weight - high - middle
    level = lax.broadcasted_iota(jnp.int32, (16, width), 0)
    pieces = jnp.where(level == 0, high, jnp.where(level == 1, middle, jnp.where(level == 2, low, 0.0)))
    rest = jnp.zeros((turned.shape[0] - 16, width), BF16)
    product = times(jnp.concatenate([turned, pieces.astype(BF16), rest], 0), hot_ref[...])
    leads = turned.shape[0]
    picked = product[:leads].astype(BF16)
    pieces = product[leads : leads + 8]
    chosen_ref[...] = jnp.broadcast_to((pieces[0:1] + pieces[1:2]) + pieces[2:3], chosen_ref.shape)
    picked_ref[...] = picked
    scatter(links, plan_out, out_refs, picked)
    copies[4].wait()


def pick_n_kernel(
    hot_ref,
    turned_ref,
    list_ref,
    chosen_ref,
    n_ref,
    weight_ref,
    count_ref,
    s_in,
    hot_t_ref,
    n_pick_ref,
    n_small_ref,
    same_ref,
    inner_ref,
    mask_ref,
    local_ref,
    base_ref,
    row_ref,
    s_ref,
    sem,
):
    copy = pltpu.make_async_copy(s_in, s_ref, sem)
    copy.start()
    hot = hot_ref[...]
    width, total = hot.shape
    weight = weight_ref[...]
    side = 128
    listed = list_ref[:1]
    lane = lax.broadcasted_iota(jnp.int32, (side, side), 1).astype(F32)
    hits = [jnp.zeros((1, side), F32)] * (width // side)
    same = []
    for k in range(0, total, side):
        down = jnp.broadcast_to(listed[:, k : k + side], (side, side)).T
        for m in range(width // side):
            block = jnp.where(down == lane + float(m * side), 1.0, 0.0)
            hits[m] = hits[m] + jnp.sum(block, 0, keepdims=True)
            hot_t_ref[k : k + side, m * side : (m + 1) * side] = block.astype(BF16)
        wide = jnp.concatenate([down] * (total // side), 1)
        same.append(jnp.where((wide == listed) & (wide >= 0.0), 1.0, 0.0))
    same = jnp.concatenate(same, 0)
    same_ref[...] = same.astype(BF16)
    inner = jnp.where(jnp.concatenate(hits, 1) > 0.0, 0.0, 1.0)
    inner_ref[...] = jnp.broadcast_to(inner, inner_ref.shape)
    n_pick = times(hot_t_ref[...], n_ref[0]).astype(BF16)
    n_pick_ref[...] = n_pick
    n_small_ref[...] = times(n_pick, hot).astype(BF16)
    earlier = lax.broadcasted_iota(jnp.int32, same.shape, 0) < lax.broadcasted_iota(jnp.int32, same.shape, 1)
    repeats = jnp.sum(jnp.where(earlier, same, 0.0), 0, keepdims=True)
    first = jnp.where(repeats > 0.0, 0.0, 1.0)
    chosen = chosen_ref[:1]
    row_ref[0:1] = chosen
    row_ref[1:2] = chosen * first
    row_ref[2:3] = first
    row_ref[3:8] = jnp.zeros((5, total), F32)
    mask = jnp.where(lax.broadcasted_iota(jnp.int32, mask_ref.shape, 1) < count_ref[0], 1.0, 0.0)
    mask_ref[...] = mask
    local = mask[:1] * turned_ref[...].astype(F32)
    local_ref[...] = local
    base_ref[...] = times_t((weight * local * inner).astype(BF16), n_pick)
    copy.wait()


def update_path_kernel(trips, links, plan, plan_out, step, last, *refs):
    arrived_refs, refs = refs[:trips], refs[trips:]
    same_ref, n_small_ref, row_ref, local_ref, base_ref = refs[:5]
    refs = refs[5:]
    residual = local_ref[...].astype(F32) + times(gather(links, plan, arrived_refs), same_ref[...])
    scaled = (row_ref[1:2] * residual).astype(BF16)
    sent = row_ref[0:1] * (base_ref[...] + times_t(scaled, n_small_ref[...]))
    if last:
        scatter(links, plan_out, refs, sent)
    elif step == 0:
        scatter(links, plan_out, refs[1:], sent)
        refs[0][...] = DAMPING * sent
    else:
        scatter(links, plan_out, refs[2:], sent)
        refs[1][...] = refs[0][...] + DAMPING * sent


def residual_path_kernel(trips, links, plan, plan_out, last, *refs):
    arrived_refs, refs = refs[:trips], refs[trips:]
    same_ref, s_small_ref, row_ref, base_ref, state_ref, local_ref = refs[:6]
    state = state_ref[...] + DAMPING * times(gather(links, plan, arrived_refs), same_ref[...])
    if last:
        refs = refs[6:]
    else:
        refs[6][...] = state
        refs = refs[7:]
    local = base_ref[...] - times((state * row_ref[2:3]).astype(BF16), s_small_ref[...])
    local_ref[...] = local
    scatter(links, plan_out, refs, local)


def corrected(links, plan, arrived_refs, hot_ref, n_ref, weight_ref, mask_ref, local_ref):
    weight = weight_ref[...]
    residual = local_ref[...] + times_t(gather(links, plan, arrived_refs), hot_ref[...])
    scaled = (weight * residual).astype(BF16)
    return mask_ref[:1] * weight * times_t(scaled, n_ref[0])


def first_update_kernel(trips, links, plan, *refs):
    arrived_refs, refs = refs[:trips], refs[trips:]
    hot_ref, hot_t_ref, n_ref, s_ref, weight_ref, mask_ref, inner_ref, local_ref, picked_ref = refs[:9]
    state_out_ref, base_ref, s_pick_ref, s_small_ref = refs[9:]
    state = DAMPING * corrected(links, plan, arrived_refs, hot_ref, n_ref, weight_ref, mask_ref, local_ref)
    state_out_ref[...] = state
    s_pick = times(s_ref[0], hot_ref[...]).astype(BF16)
    s_pick_ref[...] = s_pick
    s_small_ref[...] = times(hot_t_ref[...], s_pick).astype(BF16)
    base_ref[...] = picked_ref[...].astype(F32) - times((state * inner_ref[:1]).astype(BF16), s_pick)


def update_kernel(trips, links, plan, *refs):
    arrived_refs, refs = refs[:trips], refs[trips:]
    hot_ref, n_ref, weight_ref, mask_ref, inner_ref, local_ref, picked_ref, s_pick_ref, state_ref = refs[:9]
    state_out_ref, base_ref = refs[9:]
    state = state_ref[...] + DAMPING * corrected(links, plan, arrived_refs, hot_ref, n_ref, weight_ref, mask_ref, local_ref)
    state_out_ref[...] = state
    base_ref[...] = picked_ref[...].astype(F32) - times((state * inner_ref[:1]).astype(BF16), s_pick_ref[...])


def last_update_kernel(trips, links, plan, *refs):
    arrived_refs, refs = refs[:trips], refs[trips:]
    hot_ref, n_ref, weight_ref, mask_ref, local_ref, state_ref, state_out_ref = refs
    update = corrected(links, plan, arrived_refs, hot_ref, n_ref, weight_ref, mask_ref, local_ref)
    state_out_ref[...] = (state_ref[...] + DAMPING * update).T


def residual_kernel(trips, links, plan, *refs):
    arrived_refs, refs = refs[:trips], refs[trips:]
    hot_ref, s_ref, turned_ref, weight_ref, mask_ref, inner_ref, n_pick_ref, state_ref = refs[:8]
    state_out_ref, local_ref, base_ref = refs[8:]
    state = state_ref[...] + DAMPING * times_t(gather(links, plan, arrived_refs), hot_ref[...])
    state_out_ref[...] = state
    local = mask_ref[:1] * (turned_ref[...].astype(F32) - times(state.astype(BF16), s_ref[0]))
    local_ref[...] = local
    base_ref[...] = times_t((weight_ref[...] * local * inner_ref[:1]).astype(BF16), n_pick_ref[...])


def close_kernel(trips, links, plan, *refs):
    arrived_refs, (hot_ref, state_ref, out_ref, piece_ref, sems) = refs[:trips], refs[trips:]
    arrived = gather(links, plan, arrived_refs)
    rows = state_ref.shape[0] // PIECES
    copies = []
    for k in range(PIECES):
        part = pl.ds(k * rows, rows)
        piece_ref[part, :] = state_ref[part, :] + DAMPING * times_t(hot_ref[part, :], arrived)
        copies.append(pltpu.make_async_copy(piece_ref.at[part, :], out_ref.at[0, part, :], sems.at[k]))
        copies[k].start()
    for copy in copies:
        copy.wait()


def run(kernel, operands, results, flops, spaces=(), outputs=pltpu.VMEM, scratch=()):
    spaces = [dict(spaces).get(k, pltpu.VMEM) for k in range(len(operands))]
    moved = sum(a.size * a.dtype.itemsize for a in (*operands, *results))
    operands = [
        pltpu.with_memory_space_constraint(a, space) if space is pltpu.HBM else a for a, space in zip(operands, spaces)
    ]
    return pl.pallas_call(
        kernel,
        out_shape=results,
        in_specs=[pl.BlockSpec(memory_space=space) for space in spaces],
        out_specs=[pl.BlockSpec(memory_space=outputs)] * len(results),
        scratch_shapes=scratch,
        compiler_params=pltpu.CompilerParams(vmem_limit_bytes=LIMIT),
        cost_estimate=pl.CostEstimate(flops=flops, bytes_accessed=moved, transcendentals=0),
    )(*operands)


def body(right_side, schur, neumann, weights, neighbours, counts, shared_rows):
    width, leads = right_side.shape[1:]
    share = shared_rows.shape[2]
    subs = lax.axis_size("sub")
    plans = [min(k // 2, len(PLANS) - 1) for k in range(2 * ITERS)]
    trips = len(swaps(subs, plans[0]))
    links = len(slots_of(0, subs))
    total = links * share

    def array(rows, columns, kind=F32):
        return jax.ShapeDtypeStruct((rows, columns), kind)

    def same_as(a):
        return jax.ShapeDtypeStruct(a.shape, a.dtype)

    messages = [array(leads, share, BF16)] * trips
    full, some = array(leads, width), array(leads, total)
    small = array(total, total, BF16)
    row = array(8, width)
    picks = 2 * leads * total * width
    whole = 2 * leads * width * width
    path = 4 * leads * total * total

    def exchange(parts, plan):
        return [lax.ppermute(part, "sub", route) for part, route in zip(parts, swaps(subs, plan))]

    def bound(kernel, *settings):
        return functools.partial(kernel, trips, links, *settings)

    hot, turned, picked, listed, chosen, weight, n_mat, *sent = run(
        bound(open_kernel, plans[0], subs),
        [shared_rows, neighbours, right_side, weights, neumann],
        [
            array(width, total, BF16),
            array(leads, width, BF16),
            array(leads, total, BF16),
            array(8, total),
            array(8, total),
            same_as(weights),
            same_as(neumann),
            *messages,
        ],
        picks,
        spaces={k: pltpu.HBM for k in range(5)},
        scratch=[
            pltpu.VMEM(shared_rows.shape, jnp.int32),
            pltpu.VMEM(neighbours.shape, jnp.int32),
            pltpu.VMEM(right_side.shape, BF16),
            pltpu.SemaphoreType.DMA((5,)),
        ],
    )
    arrived = exchange(sent, plans[0])
    hot_t, n_pick, n_small, same, inner, mask, local, base, rows, s_mat = run(
        pick_n_kernel,
        [hot, turned, listed, chosen, n_mat, weight, counts, schur],
        [
            array(total, width, BF16),
            array(total, width, BF16),
            small,
            small,
            row,
            row,
            full,
            some,
            array(8, total),
            same_as(schur),
        ],
        2 * total * width * width + 2 * total * total * width + picks,
        spaces={6: pltpu.SMEM, 7: pltpu.HBM},
        scratch=[pltpu.SemaphoreType.DMA],
    )
    near = picked
    near_state = None
    for step in range(ITERS):
        came, last = arrived, step == ITERS - 1
        plan, next_plan, after = (*plans[2 * step :], None)[:3]
        operands = [*came, same, n_small, rows, near, base]
        if step and not last:
            operands.append(near_state)
        kernel = bound(update_path_kernel, plan, next_plan, step, last)
        if last:
            sent = run(kernel, operands, messages, path)
            arrived = exchange(sent, next_plan)
            (state,) = run(
                bound(last_update_kernel, plan),
                [*came, hot, n_mat, weight, mask, local, state],
                [array(width, leads)],
                whole + picks,
            )
            break
        near_state, *sent = run(kernel, operands, [some, *messages], path)
        arrived = exchange(sent, next_plan)
        if step == 0:
            state, base, s_pick, s_small = run(
                bound(first_update_kernel, plan),
                [*came, hot, hot_t, n_mat, s_mat, weight, mask, inner, local, picked],
                [full, some, array(width, total, BF16), small],
                whole + 2 * picks + 2 * total * width * (width + total),
            )
        else:
            state, base = run(
                bound(update_kernel, plan),
                [*came, hot, n_mat, weight, mask, inner, local, picked, s_pick, state],
                [full, some],
                whole + 2 * picks,
            )
        came = arrived
        ends = step == ITERS - 2
        near, *sent = run(
            bound(residual_path_kernel, next_plan, after, ends),
            [*came, same, s_small, rows, base, near_state],
            [some, *([] if ends else [some]), *messages],
            path,
        )
        if not ends:
            near_state, *sent = sent
        arrived = exchange(sent, after)
        state, local, base = run(
            bound(residual_kernel, next_plan),
            [*came, hot, s_mat, turned, weight, mask, inner, n_pick, state],
            [full, full, some],
            whole + 2 * picks,
        )
    (out,) = run(
        bound(close_kernel, plans[-1]),
        [*arrived, hot, state],
        [jax.ShapeDtypeStruct((1, width, leads), F32)],
        picks,
        outputs=pltpu.HBM,
        scratch=[pltpu.VMEM((width, leads), F32), pltpu.SemaphoreType.DMA((PIECES,))],
    )
    return out


def solution(mesh):
    in_specs = (
        P("sub", None, None),
        P("sub", None, None),
        P("sub", None, None),
        P("sub", None),
        P("sub", None),
        P("sub"),
        P("sub", None, None),
    )
    out_specs = P("sub", None, None)
    return jax.shard_map(body, mesh=mesh, in_specs=in_specs, out_specs=out_specs, check_vma=False)
```

```python
import functools

import jax
import jax.numpy as jnp
from jax import lax
from jax.experimental import pallas as pl
from jax.experimental.pallas import tpu as pltpu
from jax.sharding import PartitionSpec as P

ITERS = 4
FAR = 16
DAMPING = 0.7
LIMIT = 16 * 2**20
PIECES = 4
F32 = jnp.float32
BF16 = jnp.bfloat16


PLANS = (
    (
        (0, 1, 2, 0, 2, 2, 2, 0, 0, 0, 0, 1, 2, 2, 2, 2),
        (0, 1, 1, 1, 1, 0, 0, 1, 0, 1, 1, 1, 2, 0, 1),
        (((6, 15), (22, 29)), ((0, 2), (14, 18), (25, 26), (28, 31)), ((3, 7), (19, 23), (24, 27))),
    ),
    (
        (0, 1, 1, 0, 0, 0, 0, 1, 1, 1, 1, 0, 0, 0, 0, 0),
        (0, 2, 1, 0, 0, 1, 2, 1, 0, 1, 1, 0, 0, 1, 1),
        ((), ((0, 3), (4, 13), (14, 31)), ((2, 5), (12, 15))),
    ),
)


def turns(count, plan):
    far_turns, odd_turns, _ = PLANS[plan]
    far = [far_turns[i % FAR] for i in range(count)]
    odd = [odd_turns[(i - 1) // 2] if 0 < i < count - 1 else -1 for i in range(count)]
    return far, odd


def mixed(count):
    return count == 2 * FAR


def swaps(count, plan):
    blocks = count // FAR
    near = [i ^ 1 for i in range(count)]
    far = [i ^ FAR for i in range(count)]
    odd = [(((i + 1) ^ 1) - 1) % count for i in range(count)]
    if mixed(count):
        far_turns, odd_turns = turns(count, plan)
        pairings = []
        for turn, fill in enumerate(PLANS[plan][2]):
            pairing = list(near)
            for i, j in fill:
                pairing[i], pairing[j] = j, i
            for i in range(count):
                if far_turns[i] == turn:
                    pairing[i] = far[i]
                elif odd_turns[i] == turn:
                    pairing[i] = odd[i]
            pairings.append(pairing)
        pairings.append(near)
    else:
        again = [(((i // FAR + 1) ^ 1) - 1) % blocks * FAR + i % FAR for i in range(count)]
        pairings = ([far] if blocks > 1 else []) + ([again] if blocks > 2 else []) + [odd, near]
    for pairing in pairings:
        assert all(pairing[j] == i != j for i, j in enumerate(pairing))
    return [list(enumerate(pairing)) for pairing in pairings]


def is_turn(own_turns, turn):
    bits = sum(1 << i for i, own in enumerate(own_turns) if own == turn)
    bits = bits - (1 << 32) if bits >> 31 else bits
    return lax.shift_right_logical(jnp.int32(bits), lax.axis_index("sub")) & 1 == 1


def slots_of(index, count):
    odd = lax.rem(index, 2)
    block = lax.rem(lax.div(index, FAR), 2)
    blocks = count // FAR
    far = [2 + block] if blocks > 1 else []
    again = [3 - block] if blocks > 2 else []
    return [*far, *again, 1 - odd, odd]


def times(a, b):
    return jnp.dot(a, b, preferred_element_type=F32)


def times_t(a, b):
    return lax.dot_general(a, b, (((1,), (1,)), ((), ())), preferred_element_type=F32)


def gather(links, plan, refs):
    parts = [ref[...] for ref in refs]
    if len(parts) > links:
        values = [part.astype(F32) for part in parts[:3]]
        picked = []
        for own in turns(2 * FAR, plan):
            later = jnp.where(is_turn(own, 1), values[1], values[2])
            picked.append(jnp.where(is_turn(own, 0), values[0], later).astype(BF16))
        parts = [*picked, parts[3]]
    return jnp.concatenate(parts, 1)


def scatter(links, plan, refs, block):
    share = refs[0].shape[1]
    parts = [block[:, k * share : (k + 1) * share].astype(F32) for k in range(links)]
    if len(refs) > links:
        far, odd, near = parts
        own, _ = turns(2 * FAR, plan)
        parts = [*(jnp.where(is_turn(own, turn), far, odd) for turn in range(3)), near]
    for ref, part in zip(refs, parts):
        ref[...] = part.astype(BF16)


def open_kernel(
    trips,
    links,
    plan_out,
    subs,
    rows_in,
    near_in,
    rhs_in,
    weight_in,
    n_in,
    hot_ref,
    turned_ref,
    picked_ref,
    list_ref,
    chosen_ref,
    weight_ref,
    n_ref,
    *refs,
):
    out_refs, (rows_ref, near_ref, rhs_ref, sems) = refs[:trips], refs[trips:]
    pairs = [
        (rows_in, rows_ref),
        (near_in, near_ref),
        (rhs_in, rhs_ref),
        (weight_in, weight_ref),
        (n_in, n_ref),
    ]
    copies = [pltpu.make_async_copy(source, target, sems.at[k]) for k, (source, target) in enumerate(pairs)]
    for copy in copies:
        copy.start()
    width, share = rhs_ref.shape[1], rows_ref.shape[2]
    slots = slots_of(lax.axis_index("sub"), subs)
    place = lax.broadcasted_iota(jnp.int32, (width, share), 0)
    copies[0].wait()
    copies[1].wait()
    near = near_ref[...].astype(F32)
    lane = lax.broadcasted_iota(jnp.int32, near.shape, 1)
    for k, slot in enumerate(slots):
        partner = jnp.sum(jnp.where(lane == slot, near, 0.0), 1, keepdims=True)
        row = jnp.where(partner >= 0.0, rows_ref[0, pl.ds(slot, 1), :], -1)
        list_ref[:, pl.ds(k * share, share)] = jnp.broadcast_to(row.astype(F32), (list_ref.shape[0], share))
        hot_ref[:, pl.ds(k * share, share)] = jnp.where(place == row, 1.0, 0.0).astype(BF16)
    copies[2].wait()
    turned = rhs_ref[0].T
    turned_ref[...] = turned
    copies[3].wait()
    weight = weight_ref[...]
    high = weight.astype(BF16).astype(F32)
    middle = (weight - high).astype(BF16).astype(F32)
    low = weight - high - middle
    level = lax.broadcasted_iota(jnp.int32, (16, width), 0)
    pieces = jnp.where(level == 0, high, jnp.where(level == 1, middle, jnp.where(level == 2, low, 0.0)))
    rest = jnp.zeros((turned.shape[0] - 16, width), BF16)
    product = times(jnp.concatenate([turned, pieces.astype(BF16), rest], 0), hot_ref[...])
    leads = turned.shape[0]
    picked = product[:leads].astype(BF16)
    pieces = product[leads : leads + 8]
    chosen_ref[...] = jnp.broadcast_to((pieces[0:1] + pieces[1:2]) + pieces[2:3], chosen_ref.shape)
    picked_ref[...] = picked
    scatter(links, plan_out, out_refs, picked)
    copies[4].wait()


def pick_n_kernel(
    hot_ref,
    turned_ref,
    list_ref,
    chosen_ref,
    n_ref,
    weight_ref,
    count_ref,
    s_in,
    hot_t_ref,
    n_pick_ref,
    n_small_ref,
    same_ref,
    inner_ref,
    mask_ref,
    local_ref,
    base_ref,
    row_ref,
    s_ref,
    sem,
):
    copy = pltpu.make_async_copy(s_in, s_ref, sem)
    copy.start()
    width, total = hot_ref.shape
    weight = weight_ref[...]
    side = 128
    listed = list_ref[:1]
    lane = lax.broadcasted_iota(jnp.int32, (side, side), 1).astype(F32)
    hits = [jnp.zeros((1, side), F32)] * (width // side)
    same = []
    for k in range(0, total, side):
        down = jnp.broadcast_to(listed[:, k : k + side], (side, side)).T
        for m in range(width // side):
            block = jnp.where(down == lane + float(m * side), 1.0, 0.0)
            hits[m] = hits[m] + jnp.sum(block, 0, keepdims=True)
            hot_t_ref[k : k + side, m * side : (m + 1) * side] = block.astype(BF16)
        wide = jnp.concatenate([down] * (total // side), 1)
        same.append(jnp.where((wide == listed) & (wide >= 0.0), 1.0, 0.0))
    same = jnp.concatenate(same, 0)
    same_ref[...] = same.astype(BF16)
    inner = jnp.where(jnp.concatenate(hits, 1) > 0.0, 0.0, 1.0)
    inner_ref[...] = jnp.broadcast_to(inner, inner_ref.shape)
    n_pick_ref[...] = times(hot_t_ref[...], n_ref[0]).astype(BF16)
    earlier = lax.broadcasted_iota(jnp.int32, same.shape, 0) < lax.broadcasted_iota(jnp.int32, same.shape, 1)
    repeats = jnp.sum(jnp.where(earlier, same, 0.0), 0, keepdims=True)
    first = jnp.where(repeats > 0.0, 0.0, 1.0)
    chosen = chosen_ref[:1]
    row_ref[0:1] = chosen
    row_ref[1:2] = chosen * first
    row_ref[2:3] = first
    row_ref[3:8] = jnp.zeros((5, total), F32)
    mask = jnp.where(lax.broadcasted_iota(jnp.int32, mask_ref.shape, 1) < count_ref[0], 1.0, 0.0)
    mask_ref[...] = mask
    local = mask[:1] * turned_ref[...].astype(F32)
    local_ref[...] = local
    base_ref[...] = times_t((weight * local * inner).astype(BF16), n_pick_ref[...])
    n_small_ref[...] = times(n_pick_ref[...], hot_ref[...]).astype(BF16)
    copy.wait()


def update_path_kernel(trips, links, plan, plan_out, step, last, *refs):
    arrived_refs, refs = refs[:trips], refs[trips:]
    same_ref, n_small_ref, row_ref, local_ref, base_ref = refs[:5]
    refs = refs[5:]
    residual = local_ref[...].astype(F32) + times(gather(links, plan, arrived_refs), same_ref[...])
    scaled = (row_ref[1:2] * residual).astype(BF16)
    sent = row_ref[0:1] * (base_ref[...] + times_t(scaled, n_small_ref[...]))
    if last:
        scatter(links, plan_out, refs, sent)
    elif step == 0:
        scatter(links, plan_out, refs[1:], sent)
        refs[0][...] = DAMPING * sent
    else:
        scatter(links, plan_out, refs[2:], sent)
        refs[1][...] = refs[0][...] + DAMPING * sent


def residual_path_kernel(trips, links, plan, plan_out, last, *refs):
    arrived_refs, refs = refs[:trips], refs[trips:]
    same_ref, s_small_ref, row_ref, base_ref, state_ref, local_ref = refs[:6]
    state = state_ref[...] + DAMPING * times(gather(links, plan, arrived_refs), same_ref[...])
    if last:
        refs = refs[6:]
    else:
        refs[6][...] = state
        refs = refs[7:]
    local = base_ref[...] - times((state * row_ref[2:3]).astype(BF16), s_small_ref[...])
    local_ref[...] = local
    scatter(links, plan_out, refs, local)


def corrected(links, plan, arrived_refs, hot_ref, n_ref, weight_ref, mask_ref, local_ref):
    weight = weight_ref[...]
    residual = local_ref[...] + times_t(gather(links, plan, arrived_refs), hot_ref[...])
    scaled = (weight * residual).astype(BF16)
    return mask_ref[:1] * weight * times_t(scaled, n_ref[0])


def first_update_kernel(trips, links, plan, *refs):
    arrived_refs, refs = refs[:trips], refs[trips:]
    hot_ref, hot_t_ref, n_ref, s_ref, weight_ref, mask_ref, inner_ref, local_ref, picked_ref = refs[:9]
    state_out_ref, base_ref, s_pick_ref, s_small_ref = refs[9:]
    state = DAMPING * corrected(links, plan, arrived_refs, hot_ref, n_ref, weight_ref, mask_ref, local_ref)
    state_out_ref[...] = state
    s_pick = times(s_ref[0], hot_ref[...]).astype(BF16)
    s_pick_ref[...] = s_pick
    s_small_ref[...] = times(hot_t_ref[...], s_pick).astype(BF16)
    base_ref[...] = picked_ref[...].astype(F32) - times((state * inner_ref[:1]).astype(BF16), s_pick)


def update_kernel(trips, links, plan, *refs):
    arrived_refs, refs = refs[:trips], refs[trips:]
    hot_ref, n_ref, weight_ref, mask_ref, inner_ref, local_ref, picked_ref, s_pick_ref, state_ref = refs[:9]
    state_out_ref, base_ref = refs[9:]
    state = state_ref[...] + DAMPING * corrected(links, plan, arrived_refs, hot_ref, n_ref, weight_ref, mask_ref, local_ref)
    state_out_ref[...] = state
    base_ref[...] = picked_ref[...].astype(F32) - times((state * inner_ref[:1]).astype(BF16), s_pick_ref[...])


def last_update_kernel(trips, links, plan, *refs):
    arrived_refs, refs = refs[:trips], refs[trips:]
    hot_ref, n_ref, weight_ref, mask_ref, local_ref, state_ref, state_out_ref = refs
    update = corrected(links, plan, arrived_refs, hot_ref, n_ref, weight_ref, mask_ref, local_ref)
    state_out_ref[...] = (state_ref[...] + DAMPING * update).T


def residual_kernel(trips, links, plan, *refs):
    arrived_refs, refs = refs[:trips], refs[trips:]
    hot_ref, s_ref, turned_ref, weight_ref, mask_ref, inner_ref, n_pick_ref, state_ref = refs[:8]
    state_out_ref, local_ref, base_ref = refs[8:]
    state = state_ref[...] + DAMPING * times_t(gather(links, plan, arrived_refs), hot_ref[...])
    state_out_ref[...] = state
    local = mask_ref[:1] * (turned_ref[...].astype(F32) - times(state.astype(BF16), s_ref[0]))
    local_ref[...] = local
    base_ref[...] = times_t((weight_ref[...] * local * inner_ref[:1]).astype(BF16), n_pick_ref[...])


def close_kernel(trips, links, plan, *refs):
    arrived_refs, (hot_ref, state_ref, out_ref, piece_ref, sems) = refs[:trips], refs[trips:]
    arrived = gather(links, plan, arrived_refs)
    rows = state_ref.shape[0] // PIECES
    copies = []
    for k in range(PIECES):
        part = pl.ds(k * rows, rows)
        piece_ref[part, :] = state_ref[part, :] + DAMPING * times_t(hot_ref[part, :], arrived)
        copies.append(pltpu.make_async_copy(piece_ref.at[part, :], out_ref.at[0, part, :], sems.at[k]))
        copies[k].start()
    for copy in copies:
        copy.wait()


def run(kernel, operands, results, flops, spaces=(), outputs=pltpu.VMEM, scratch=()):
    spaces = [dict(spaces).get(k, pltpu.VMEM) for k in range(len(operands))]
    moved = sum(a.size * a.dtype.itemsize for a in (*operands, *results))
    operands = [
        pltpu.with_memory_space_constraint(a, space) if space is pltpu.HBM else a for a, space in zip(operands, spaces)
    ]
    return pl.pallas_call(
        kernel,
        out_shape=results,
        in_specs=[pl.BlockSpec(memory_space=space) for space in spaces],
        out_specs=[pl.BlockSpec(memory_space=outputs)] * len(results),
        scratch_shapes=scratch,
        compiler_params=pltpu.CompilerParams(vmem_limit_bytes=LIMIT),
        cost_estimate=pl.CostEstimate(flops=flops, bytes_accessed=moved, transcendentals=0),
    )(*operands)


def body(right_side, schur, neumann, weights, neighbours, counts, shared_rows):
    width, leads = right_side.shape[1:]
    share = shared_rows.shape[2]
    subs = lax.axis_size("sub")
    plans = [min(k // 2, len(PLANS) - 1) for k in range(2 * ITERS)]
    trips = len(swaps(subs, plans[0]))
    links = len(slots_of(0, subs))
    total = links * share

    def array(rows, columns, kind=F32):
        return jax.ShapeDtypeStruct((rows, columns), kind)

    def same_as(a):
        return jax.ShapeDtypeStruct(a.shape, a.dtype)

    messages = [array(leads, share, BF16)] * trips
    full, some = array(leads, width), array(leads, total)
    small = array(total, total, BF16)
    row = array(8, width)
    picks = 2 * leads * total * width
    whole = 2 * leads * width * width
    path = 4 * leads * total * total

    def exchange(parts, plan):
        return [lax.ppermute(part, "sub", route) for part, route in zip(parts, swaps(subs, plan))]

    def bound(kernel, *settings):
        return functools.partial(kernel, trips, links, *settings)

    hot, turned, picked, listed, chosen, weight, n_mat, *sent = run(
        bound(open_kernel, plans[0], subs),
        [shared_rows, neighbours, right_side, weights, neumann],
        [
            array(width, total, BF16),
            array(leads, width, BF16),
            array(leads, total, BF16),
            array(8, total),
            array(8, total),
            same_as(weights),
            same_as(neumann),
            *messages,
        ],
        picks,
        spaces={k: pltpu.HBM for k in range(5)},
        scratch=[
            pltpu.VMEM(shared_rows.shape, jnp.int32),
            pltpu.VMEM(neighbours.shape, jnp.int32),
            pltpu.VMEM(right_side.shape, BF16),
            pltpu.SemaphoreType.DMA((5,)),
        ],
    )
    arrived = exchange(sent, plans[0])
    hot_t, n_pick, n_small, same, inner, mask, local, base, rows, s_mat = run(
        pick_n_kernel,
        [hot, turned, listed, chosen, n_mat, weight, counts, schur],
        [
            array(total, width, BF16),
            array(total, width, BF16),
            small,
            small,
            row,
            row,
            full,
            some,
            array(8, total),
            same_as(schur),
        ],
        2 * total * width * width + 2 * total * total * width + picks,
        spaces={6: pltpu.SMEM, 7: pltpu.HBM},
        scratch=[pltpu.SemaphoreType.DMA],
    )
    near = picked
    near_state = None
    for step in range(ITERS):
        came, last = arrived, step == ITERS - 1
        plan, next_plan, after = (*plans[2 * step :], None)[:3]
        operands = [*came, same, n_small, rows, near, base]
        if step and not last:
            operands.append(near_state)
        kernel = bound(update_path_kernel, plan, next_plan, step, last)
        if last:
            sent = run(kernel, operands, messages, path)
            arrived = exchange(sent, next_plan)
            (state,) = run(
                bound(last_update_kernel, plan),
                [*came, hot, n_mat, weight, mask, local, state],
                [array(width, leads)],
                whole + picks,
            )
            break
        near_state, *sent = run(kernel, operands, [some, *messages], path)
        arrived = exchange(sent, next_plan)
        if step == 0:
            state, base, s_pick, s_small = run(
                bound(first_update_kernel, plan),
                [*came, hot, hot_t, n_mat, s_mat, weight, mask, inner, local, picked],
                [full, some, array(width, total, BF16), small],
                whole + 2 * picks + 2 * total * width * (width + total),
            )
        else:
            state, base = run(
                bound(update_kernel, plan),
                [*came, hot, n_mat, weight, mask, inner, local, picked, s_pick, state],
                [full, some],
                whole + 2 * picks,
            )
        came = arrived
        ends = step == ITERS - 2
        near, *sent = run(
            bound(residual_path_kernel, next_plan, after, ends),
            [*came, same, s_small, rows, base, near_state],
            [some, *([] if ends else [some]), *messages],
            path,
        )
        if not ends:
            near_state, *sent = sent
        arrived = exchange(sent, after)
        state, local, base = run(
            bound(residual_kernel, next_plan),
            [*came, hot, s_mat, turned, weight, mask, inner, n_pick, state],
            [full, full, some],
            whole + 2 * picks,
        )
    (out,) = run(
        bound(close_kernel, plans[-1]),
        [*arrived, hot, state],
        [jax.ShapeDtypeStruct((1, width, leads), F32)],
        picks,
        outputs=pltpu.HBM,
        scratch=[pltpu.VMEM((width, leads), F32), pltpu.SemaphoreType.DMA((PIECES,))],
    )
    return out


def solution(mesh):
    in_specs = (
        P("sub", None, None),
        P("sub", None, None),
        P("sub", None, None),
        P("sub", None),
        P("sub", None),
        P("sub"),
        P("sub", None, None),
    )
    out_specs = P("sub", None, None)
    return jax.shard_map(body, mesh=mesh, in_specs=in_specs, out_specs=out_specs, check_vma=False)
```

```python
import functools

import jax
import jax.numpy as jnp
from jax import lax
from jax.experimental import pallas as pl
from jax.experimental.pallas import tpu as pltpu
from jax.sharding import PartitionSpec as P

ITERS = 4
FAR = 16
DAMPING = 0.7
LIMIT = 16 * 2**20
PIECES = 4
F32 = jnp.float32
BF16 = jnp.bfloat16


PLANS = (
    (
        (0, 1, 2, 0, 2, 2, 2, 0, 0, 0, 0, 1, 2, 2, 2, 2),
        (0, 1, 1, 1, 1, 0, 0, 1, 0, 1, 1, 1, 2, 0, 1),
        (((6, 15), (22, 29)), ((0, 2), (14, 18), (25, 26), (28, 31)), ((3, 7), (19, 23), (24, 27))),
    ),
    (
        (0, 1, 1, 0, 0, 0, 0, 1, 1, 1, 1, 0, 0, 0, 0, 0),
        (0, 2, 1, 0, 0, 1, 2, 1, 0, 1, 1, 0, 0, 1, 1),
        ((), ((0, 3), (4, 13), (14, 31)), ((2, 5), (12, 15))),
    ),
)


def turns(count, plan):
    far_turns, odd_turns, _ = PLANS[plan]
    far = [far_turns[i % FAR] for i in range(count)]
    odd = [odd_turns[(i - 1) // 2] if 0 < i < count - 1 else -1 for i in range(count)]
    return far, odd


def mixed(count):
    return count == 2 * FAR


def swaps(count, plan):
    blocks = count // FAR
    near = [i ^ 1 for i in range(count)]
    far = [i ^ FAR for i in range(count)]
    odd = [(((i + 1) ^ 1) - 1) % count for i in range(count)]
    if mixed(count):
        far_turns, odd_turns = turns(count, plan)
        pairings = []
        for turn, fill in enumerate(PLANS[plan][2]):
            pairing = list(near)
            for i, j in fill:
                pairing[i], pairing[j] = j, i
            for i in range(count):
                if far_turns[i] == turn:
                    pairing[i] = far[i]
                elif odd_turns[i] == turn:
                    pairing[i] = odd[i]
            pairings.append(pairing)
        pairings.append(near)
    else:
        again = [(((i // FAR + 1) ^ 1) - 1) % blocks * FAR + i % FAR for i in range(count)]
        pairings = ([far] if blocks > 1 else []) + ([again] if blocks > 2 else []) + [odd, near]
    for pairing in pairings:
        assert all(pairing[j] == i != j for i, j in enumerate(pairing))
    return [list(enumerate(pairing)) for pairing in pairings]


def is_turn(own_turns, turn):
    bits = sum(1 << i for i, own in enumerate(own_turns) if own == turn)
    bits = bits - (1 << 32) if bits >> 31 else bits
    return lax.shift_right_logical(jnp.int32(bits), lax.axis_index("sub")) & 1 == 1


def slots_of(index, count):
    odd = lax.rem(index, 2)
    block = lax.rem(lax.div(index, FAR), 2)
    blocks = count // FAR
    far = [2 + block] if blocks > 1 else []
    again = [3 - block] if blocks > 2 else []
    return [*far, *again, 1 - odd, odd]


def times(a, b):
    return jnp.dot(a, b, preferred_element_type=F32)


def times_t(a, b):
    return lax.dot_general(a, b, (((1,), (1,)), ((), ())), preferred_element_type=F32)


def gather(links, plan, refs):
    parts = [ref[...] for ref in refs]
    if len(parts) > links:
        values = [part.astype(F32) for part in parts[:3]]
        picked = []
        for own in turns(2 * FAR, plan):
            later = jnp.where(is_turn(own, 1), values[1], values[2])
            picked.append(jnp.where(is_turn(own, 0), values[0], later).astype(BF16))
        parts = [*picked, parts[3]]
    return jnp.concatenate(parts, 1)


def scatter(links, plan, refs, block):
    share = refs[0].shape[1]
    parts = [block[:, k * share : (k + 1) * share].astype(F32) for k in range(links)]
    if len(refs) > links:
        far, odd, near = parts
        own, _ = turns(2 * FAR, plan)
        parts = [*(jnp.where(is_turn(own, turn), far, odd) for turn in range(3)), near]
    for ref, part in zip(refs, parts):
        ref[...] = part.astype(BF16)


def open_kernel(
    trips,
    links,
    plan_out,
    subs,
    rows_in,
    near_in,
    rhs_in,
    weight_in,
    n_in,
    hot_ref,
    turned_ref,
    picked_ref,
    list_ref,
    chosen_ref,
    weight_ref,
    n_ref,
    *refs,
):
    out_refs, (rows_ref, near_ref, rhs_ref, sems) = refs[:trips], refs[trips:]
    pairs = [
        (rows_in, rows_ref),
        (near_in, near_ref),
        (rhs_in, rhs_ref),
        (weight_in, weight_ref),
        (n_in, n_ref),
    ]
    copies = [pltpu.make_async_copy(source, target, sems.at[k]) for k, (source, target) in enumerate(pairs)]
    for copy in copies:
        copy.start()
    width, share = rhs_ref.shape[1], rows_ref.shape[2]
    slots = slots_of(lax.axis_index("sub"), subs)
    place = lax.broadcasted_iota(jnp.int32, (width, share), 0)
    copies[0].wait()
    copies[1].wait()
    near = near_ref[...].astype(F32)
    lane = lax.broadcasted_iota(jnp.int32, near.shape, 1)
    for k, slot in enumerate(slots):
        partner = jnp.sum(jnp.where(lane == slot, near, 0.0), 1, keepdims=True)
        row = jnp.where(partner >= 0.0, rows_ref[0, pl.ds(slot, 1), :], -1)
        list_ref[:, pl.ds(k * share, share)] = jnp.broadcast_to(row.astype(F32), (list_ref.shape[0], share))
        hot_ref[:, pl.ds(k * share, share)] = jnp.where(place == row, 1.0, 0.0).astype(BF16)
    copies[2].wait()
    turned = rhs_ref[0].T
    turned_ref[...] = turned
    copies[3].wait()
    weight = weight_ref[...]
    high = weight.astype(BF16).astype(F32)
    middle = (weight - high).astype(BF16).astype(F32)
    low = weight - high - middle
    level = lax.broadcasted_iota(jnp.int32, (16, width), 0)
    pieces = jnp.where(level == 0, high, jnp.where(level == 1, middle, jnp.where(level == 2, low, 0.0)))
    rest = jnp.zeros((turned.shape[0] - 16, width), BF16)
    product = times(jnp.concatenate([turned, pieces.astype(BF16), rest], 0), hot_ref[...])
    leads = turned.shape[0]
    picked = product[:leads].astype(BF16)
    pieces = product[leads : leads + 8]
    chosen_ref[...] = jnp.broadcast_to((pieces[0:1] + pieces[1:2]) + pieces[2:3], chosen_ref.shape)
    picked_ref[...] = picked
    scatter(links, plan_out, out_refs, picked)
    copies[4].wait()


def pick_n_kernel(
    hot_ref,
    turned_ref,
    list_ref,
    chosen_ref,
    n_ref,
    weight_ref,
    count_ref,
    s_in,
    hot_t_ref,
    n_pick_ref,
    n_small_ref,
    same_ref,
    inner_ref,
    mask_ref,
    local_ref,
    base_ref,
    row_ref,
    s_ref,
    sem,
):
    copy = pltpu.make_async_copy(s_in, s_ref, sem)
    copy.start()
    width, total = hot_ref.shape
    weight = weight_ref[...]
    side = 128
    listed = list_ref[:1]
    lane = lax.broadcasted_iota(jnp.int32, (side, side), 1).astype(F32)
    hits = [jnp.zeros((1, side), F32)] * (width // side)
    same = []
    for k in range(0, total, side):
        down = jnp.broadcast_to(listed[:, k : k + side], (side, side)).T
        for m in range(width // side):
            block = jnp.where(down == lane + float(m * side), 1.0, 0.0)
            hits[m] = hits[m] + jnp.sum(block, 0, keepdims=True)
            hot_t_ref[k : k + side, m * side : (m + 1) * side] = block.astype(BF16)
        wide = jnp.concatenate([down] * (total // side), 1)
        same.append(jnp.where((wide == listed) & (wide >= 0.0), 1.0, 0.0))
    same = jnp.concatenate(same, 0)
    same_ref[...] = same.astype(BF16)
    inner = jnp.where(jnp.concatenate(hits, 1) > 0.0, 0.0, 1.0)
    inner_ref[...] = jnp.broadcast_to(inner, inner_ref.shape)
    n_pick_ref[...] = times(hot_t_ref[...], n_ref[0]).astype(BF16)
    earlier = lax.broadcasted_iota(jnp.int32, same.shape, 0) < lax.broadcasted_iota(jnp.int32, same.shape, 1)
    repeats = jnp.sum(jnp.where(earlier, same, 0.0), 0, keepdims=True)
    first = jnp.where(repeats > 0.0, 0.0, 1.0)
    chosen = chosen_ref[:1]
    row_ref[0:1] = chosen
    row_ref[1:2] = chosen * first
    row_ref[2:3] = first
    row_ref[3:8] = jnp.zeros((5, total), F32)
    mask = jnp.where(lax.broadcasted_iota(jnp.int32, mask_ref.shape, 1) < count_ref[0], 1.0, 0.0)
    mask_ref[...] = mask
    local = mask[:1] * turned_ref[...].astype(F32)
    local_ref[...] = local
    base_ref[...] = times_t((weight * local * inner).astype(BF16), n_pick_ref[...])
    n_small_ref[...] = times(n_pick_ref[...], hot_ref[...]).astype(BF16)
    copy.wait()


def update_path_kernel(trips, links, plan, plan_out, step, last, *refs):
    arrived_refs, refs = refs[:trips], refs[trips:]
    same_ref, n_small_ref, row_ref, local_ref, base_ref = refs[:5]
    refs = refs[5:]
    residual = local_ref[...].astype(F32) + times(gather(links, plan, arrived_refs), same_ref[...])
    scaled = (row_ref[1:2] * residual).astype(BF16)
    sent = row_ref[0:1] * (base_ref[...] + times_t(scaled, n_small_ref[...]))
    if last:
        scatter(links, plan_out, refs, sent)
    elif step == 0:
        scatter(links, plan_out, refs[1:], sent)
        refs[0][...] = DAMPING * sent
    else:
        scatter(links, plan_out, refs[2:], sent)
        refs[1][...] = refs[0][...] + DAMPING * sent


def residual_path_kernel(trips, links, plan, plan_out, last, *refs):
    arrived_refs, refs = refs[:trips], refs[trips:]
    same_ref, s_small_ref, row_ref, base_ref, state_ref, local_ref = refs[:6]
    state = state_ref[...] + DAMPING * times(gather(links, plan, arrived_refs), same_ref[...])
    if last:
        refs = refs[6:]
    else:
        refs[6][...] = state
        refs = refs[7:]
    local = base_ref[...] - times((state * row_ref[2:3]).astype(BF16), s_small_ref[...])
    local_ref[...] = local
    scatter(links, plan_out, refs, local)


def corrected(links, plan, arrived_refs, hot_ref, n_ref, weight_ref, mask_ref, local_ref):
    weight = weight_ref[...]
    residual = local_ref[...] + times_t(gather(links, plan, arrived_refs), hot_ref[...])
    scaled = (weight * residual).astype(BF16)
    return mask_ref[:1] * weight * times_t(scaled, n_ref[0])


def first_update_kernel(trips, links, plan, *refs):
    arrived_refs, refs = refs[:trips], refs[trips:]
    hot_ref, hot_t_ref, n_ref, s_ref, weight_ref, mask_ref, inner_ref, local_ref, picked_ref = refs[:9]
    state_out_ref, base_ref, s_pick_ref, s_small_ref = refs[9:]
    s_pick_ref[...] = times(s_ref[0], hot_ref[...]).astype(BF16)
    s_small_ref[...] = times(hot_t_ref[...], s_pick_ref[...]).astype(BF16)
    state_out_ref[...] = DAMPING * corrected(links, plan, arrived_refs, hot_ref, n_ref, weight_ref, mask_ref, local_ref)
    inside = (state_out_ref[...] * inner_ref[:1]).astype(BF16)
    base_ref[...] = picked_ref[...].astype(F32) - times(inside, s_pick_ref[...])


def update_kernel(trips, links, plan, *refs):
    arrived_refs, refs = refs[:trips], refs[trips:]
    hot_ref, n_ref, weight_ref, mask_ref, inner_ref, local_ref, picked_ref, s_pick_ref, state_ref = refs[:9]
    state_out_ref, base_ref = refs[9:]
    state = state_ref[...] + DAMPING * corrected(links, plan, arrived_refs, hot_ref, n_ref, weight_ref, mask_ref, local_ref)
    state_out_ref[...] = state
    base_ref[...] = picked_ref[...].astype(F32) - times((state * inner_ref[:1]).astype(BF16), s_pick_ref[...])


def last_update_kernel(trips, links, plan, *refs):
    arrived_refs, refs = refs[:trips], refs[trips:]
    hot_ref, n_ref, weight_ref, mask_ref, local_ref, state_ref, state_out_ref = refs
    update = corrected(links, plan, arrived_refs, hot_ref, n_ref, weight_ref, mask_ref, local_ref)
    state_out_ref[...] = (state_ref[...] + DAMPING * update).T


def residual_kernel(trips, links, plan, *refs):
    arrived_refs, refs = refs[:trips], refs[trips:]
    hot_ref, s_ref, turned_ref, weight_ref, mask_ref, inner_ref, n_pick_ref, state_ref = refs[:8]
    state_out_ref, local_ref, base_ref = refs[8:]
    state = state_ref[...] + DAMPING * times_t(gather(links, plan, arrived_refs), hot_ref[...])
    state_out_ref[...] = state
    local = mask_ref[:1] * (turned_ref[...].astype(F32) - times(state.astype(BF16), s_ref[0]))
    local_ref[...] = local
    base_ref[...] = times_t((weight_ref[...] * local * inner_ref[:1]).astype(BF16), n_pick_ref[...])


def close_kernel(trips, links, plan, *refs):
    arrived_refs, (hot_ref, state_ref, out_ref, piece_ref, sems) = refs[:trips], refs[trips:]
    arrived = gather(links, plan, arrived_refs)
    rows = state_ref.shape[0] // PIECES
    copies = []
    for k in range(PIECES):
        part = pl.ds(k * rows, rows)
        piece_ref[part, :] = state_ref[part, :] + DAMPING * times_t(hot_ref[part, :], arrived)
        copies.append(pltpu.make_async_copy(piece_ref.at[part, :], out_ref.at[0, part, :], sems.at[k]))
        copies[k].start()
    for copy in copies:
        copy.wait()


def run(kernel, operands, results, flops, spaces=(), outputs=pltpu.VMEM, scratch=()):
    spaces = [dict(spaces).get(k, pltpu.VMEM) for k in range(len(operands))]
    moved = sum(a.size * a.dtype.itemsize for a in (*operands, *results))
    operands = [
        pltpu.with_memory_space_constraint(a, space) if space is pltpu.HBM else a for a, space in zip(operands, spaces)
    ]
    return pl.pallas_call(
        kernel,
        out_shape=results,
        in_specs=[pl.BlockSpec(memory_space=space) for space in spaces],
        out_specs=[pl.BlockSpec(memory_space=outputs)] * len(results),
        scratch_shapes=scratch,
        compiler_params=pltpu.CompilerParams(vmem_limit_bytes=LIMIT),
        cost_estimate=pl.CostEstimate(flops=flops, bytes_accessed=moved, transcendentals=0),
    )(*operands)


def body(right_side, schur, neumann, weights, neighbours, counts, shared_rows):
    width, leads = right_side.shape[1:]
    share = shared_rows.shape[2]
    subs = lax.axis_size("sub")
    plans = [min(k // 2, len(PLANS) - 1) for k in range(2 * ITERS)]
    trips = len(swaps(subs, plans[0]))
    links = len(slots_of(0, subs))
    total = links * share

    def array(rows, columns, kind=F32):
        return jax.ShapeDtypeStruct((rows, columns), kind)

    def same_as(a):
        return jax.ShapeDtypeStruct(a.shape, a.dtype)

    messages = [array(leads, share, BF16)] * trips
    full, some = array(leads, width), array(leads, total)
    small = array(total, total, BF16)
    row = array(8, width)
    picks = 2 * leads * total * width
    whole = 2 * leads * width * width
    path = 4 * leads * total * total

    def exchange(parts, plan):
        return [lax.ppermute(part, "sub", route) for part, route in zip(parts, swaps(subs, plan))]

    def bound(kernel, *settings):
        return functools.partial(kernel, trips, links, *settings)

    hot, turned, picked, listed, chosen, weight, n_mat, *sent = run(
        bound(open_kernel, plans[0], subs),
        [shared_rows, neighbours, right_side, weights, neumann],
        [
            array(width, total, BF16),
            array(leads, width, BF16),
            array(leads, total, BF16),
            array(8, total),
            array(8, total),
            same_as(weights),
            same_as(neumann),
            *messages,
        ],
        picks,
        spaces={k: pltpu.HBM for k in range(5)},
        scratch=[
            pltpu.VMEM(shared_rows.shape, jnp.int32),
            pltpu.VMEM(neighbours.shape, jnp.int32),
            pltpu.VMEM(right_side.shape, BF16),
            pltpu.SemaphoreType.DMA((5,)),
        ],
    )
    arrived = exchange(sent, plans[0])
    hot_t, n_pick, n_small, same, inner, mask, local, base, rows, s_mat = run(
        pick_n_kernel,
        [hot, turned, listed, chosen, n_mat, weight, counts, schur],
        [
            array(total, width, BF16),
            array(total, width, BF16),
            small,
            small,
            row,
            row,
            full,
            some,
            array(8, total),
            same_as(schur),
        ],
        2 * total * width * width + 2 * total * total * width + picks,
        spaces={6: pltpu.SMEM, 7: pltpu.HBM},
        scratch=[pltpu.SemaphoreType.DMA],
    )
    near = picked
    near_state = None
    for step in range(ITERS):
        came, last = arrived, step == ITERS - 1
        plan, next_plan, after = (*plans[2 * step :], None)[:3]
        operands = [*came, same, n_small, rows, near, base]
        if step and not last:
            operands.append(near_state)
        kernel = bound(update_path_kernel, plan, next_plan, step, last)
        if last:
            sent = run(kernel, operands, messages, path)
            arrived = exchange(sent, next_plan)
            (state,) = run(
                bound(last_update_kernel, plan),
                [*came, hot, n_mat, weight, mask, local, state],
                [array(width, leads)],
                whole + picks,
            )
            break
        near_state, *sent = run(kernel, operands, [some, *messages], path)
        arrived = exchange(sent, next_plan)
        if step == 0:
            state, base, s_pick, s_small = run(
                bound(first_update_kernel, plan),
                [*came, hot, hot_t, n_mat, s_mat, weight, mask, inner, local, picked],
                [full, some, array(width, total, BF16), small],
                whole + 2 * picks + 2 * total * width * (width + total),
            )
        else:
            state, base = run(
                bound(update_kernel, plan),
                [*came, hot, n_mat, weight, mask, inner, local, picked, s_pick, state],
                [full, some],
                whole + 2 * picks,
            )
        came = arrived
        ends = step == ITERS - 2
        near, *sent = run(
            bound(residual_path_kernel, next_plan, after, ends),
            [*came, same, s_small, rows, base, near_state],
            [some, *([] if ends else [some]), *messages],
            path,
        )
        if not ends:
            near_state, *sent = sent
        arrived = exchange(sent, after)
        state, local, base = run(
            bound(residual_kernel, next_plan),
            [*came, hot, s_mat, turned, weight, mask, inner, n_pick, state],
            [full, full, some],
            whole + 2 * picks,
        )
    (out,) = run(
        bound(close_kernel, plans[-1]),
        [*arrived, hot, state],
        [jax.ShapeDtypeStruct((1, width, leads), F32)],
        picks,
        outputs=pltpu.HBM,
        scratch=[pltpu.VMEM((width, leads), F32), pltpu.SemaphoreType.DMA((PIECES,))],
    )
    return out


def solution(mesh):
    in_specs = (
        P("sub", None, None),
        P("sub", None, None),
        P("sub", None, None),
        P("sub", None),
        P("sub", None),
        P("sub"),
        P("sub", None, None),
    )
    out_specs = P("sub", None, None)
    return jax.shard_map(body, mesh=mesh, in_specs=in_specs, out_specs=out_specs, check_vma=False)
```

```python
import functools

import jax
import jax.numpy as jnp
from jax import lax
from jax.experimental import pallas as pl
from jax.experimental.pallas import tpu as pltpu
from jax.sharding import PartitionSpec as P

ITERS = 4
FAR = 16
DAMPING = 0.7
LIMIT = 16 * 2**20
PIECES = 4
F32 = jnp.float32
BF16 = jnp.bfloat16


PLANS = (
    (
        (0, 1, 2, 0, 2, 2, 2, 0, 0, 0, 0, 1, 2, 2, 2, 2),
        (0, 1, 1, 1, 1, 0, 0, 1, 0, 1, 1, 1, 2, 0, 1),
        (((6, 15), (22, 29)), ((0, 2), (14, 18), (25, 26), (28, 31)), ((3, 7), (19, 23), (24, 27))),
    ),
    (
        (0, 1, 1, 0, 0, 0, 0, 1, 1, 1, 1, 0, 0, 0, 0, 0),
        (0, 2, 1, 0, 0, 1, 2, 1, 0, 1, 1, 0, 0, 1, 1),
        ((), ((0, 3), (4, 13), (14, 31)), ((2, 5), (12, 15))),
    ),
)


def turns(count, plan):
    far_turns, odd_turns, _ = PLANS[plan]
    far = [far_turns[i % FAR] for i in range(count)]
    odd = [odd_turns[(i - 1) // 2] if 0 < i < count - 1 else -1 for i in range(count)]
    return far, odd


def mixed(count):
    return count == 2 * FAR


def swaps(count, plan):
    blocks = count // FAR
    near = [i ^ 1 for i in range(count)]
    far = [i ^ FAR for i in range(count)]
    odd = [(((i + 1) ^ 1) - 1) % count for i in range(count)]
    if mixed(count):
        far_turns, odd_turns = turns(count, plan)
        pairings = []
        for turn, fill in enumerate(PLANS[plan][2]):
            pairing = list(near)
            for i, j in fill:
                pairing[i], pairing[j] = j, i
            for i in range(count):
                if far_turns[i] == turn:
                    pairing[i] = far[i]
                elif odd_turns[i] == turn:
                    pairing[i] = odd[i]
            pairings.append(pairing)
        pairings.append(near)
    else:
        again = [(((i // FAR + 1) ^ 1) - 1) % blocks * FAR + i % FAR for i in range(count)]
        pairings = ([far] if blocks > 1 else []) + ([again] if blocks > 2 else []) + [odd, near]
    for pairing in pairings:
        assert all(pairing[j] == i != j for i, j in enumerate(pairing))
    return [list(enumerate(pairing)) for pairing in pairings]


def is_turn(own_turns, turn):
    bits = sum(1 << i for i, own in enumerate(own_turns) if own == turn)
    bits = bits - (1 << 32) if bits >> 31 else bits
    return lax.shift_right_logical(jnp.int32(bits), lax.axis_index("sub")) & 1 == 1


def slots_of(index, count):
    odd = lax.rem(index, 2)
    block = lax.rem(lax.div(index, FAR), 2)
    blocks = count // FAR
    far = [2 + block] if blocks > 1 else []
    again = [3 - block] if blocks > 2 else []
    return [*far, *again, 1 - odd, odd]


def times(a, b):
    return jnp.dot(a, b, preferred_element_type=F32)


def times_t(a, b):
    return lax.dot_general(a, b, (((1,), (1,)), ((), ())), preferred_element_type=F32)


def gather(links, plan, refs):
    parts = [ref[...] for ref in refs]
    if len(parts) > links:
        values = [part.astype(F32) for part in parts[:3]]
        picked = []
        for own in turns(2 * FAR, plan):
            later = jnp.where(is_turn(own, 1), values[1], values[2])
            picked.append(jnp.where(is_turn(own, 0), values[0], later).astype(BF16))
        parts = [*picked, parts[3]]
    return jnp.concatenate(parts, 1)


def scatter(links, plan, refs, block):
    share = refs[0].shape[1]
    parts = [block[:, k * share : (k + 1) * share].astype(F32) for k in range(links)]
    if len(refs) > links:
        far, odd, near = parts
        own, _ = turns(2 * FAR, plan)
        parts = [*(jnp.where(is_turn(own, turn), far, odd) for turn in range(3)), near]
    for ref, part in zip(refs, parts):
        ref[...] = part.astype(BF16)


def open_kernel(
    trips,
    links,
    plan_out,
    subs,
    rows_in,
    near_in,
    rhs_in,
    weight_in,
    n_in,
    hot_ref,
    turned_ref,
    picked_ref,
    list_ref,
    chosen_ref,
    weight_ref,
    n_ref,
    *refs,
):
    out_refs, (rows_ref, near_ref, rhs_ref, sems) = refs[:trips], refs[trips:]
    pairs = [
        (rows_in, rows_ref),
        (near_in, near_ref),
        (rhs_in, rhs_ref),
        (weight_in, weight_ref),
        (n_in.at[0, :, pl.ds(0, n_ref.shape[1])], n_ref),
    ]
    copies = [pltpu.make_async_copy(source, target, sems.at[k]) for k, (source, target) in enumerate(pairs)]
    for copy in copies:
        copy.start()
    width, share = rhs_ref.shape[1], rows_ref.shape[2]
    slots = slots_of(lax.axis_index("sub"), subs)
    place = lax.broadcasted_iota(jnp.int32, (width, share), 0)
    copies[0].wait()
    copies[1].wait()
    near = near_ref[...].astype(F32)
    lane = lax.broadcasted_iota(jnp.int32, near.shape, 1)
    for k, slot in enumerate(slots):
        partner = jnp.sum(jnp.where(lane == slot, near, 0.0), 1, keepdims=True)
        row = jnp.where(partner >= 0.0, rows_ref[0, pl.ds(slot, 1), :], -1)
        list_ref[:, pl.ds(k * share, share)] = jnp.broadcast_to(row.astype(F32), (list_ref.shape[0], share))
        hot_ref[:, pl.ds(k * share, share)] = jnp.where(place == row, 1.0, 0.0).astype(BF16)
    copies[2].wait()
    turned = rhs_ref[0].T
    turned_ref[...] = turned
    copies[3].wait()
    weight = weight_ref[...]
    high = weight.astype(BF16).astype(F32)
    middle = (weight - high).astype(BF16).astype(F32)
    low = weight - high - middle
    level = lax.broadcasted_iota(jnp.int32, (16, width), 0)
    pieces = jnp.where(level == 0, high, jnp.where(level == 1, middle, jnp.where(level == 2, low, 0.0)))
    rest = jnp.zeros((turned.shape[0] - 16, width), BF16)
    product = times(jnp.concatenate([turned, pieces.astype(BF16), rest], 0), hot_ref[...])
    leads = turned.shape[0]
    picked = product[:leads].astype(BF16)
    pieces = product[leads : leads + 8]
    chosen_ref[...] = jnp.broadcast_to((pieces[0:1] + pieces[1:2]) + pieces[2:3], chosen_ref.shape)
    picked_ref[...] = picked
    scatter(links, plan_out, out_refs, picked)
    copies[4].wait()


def pick_n_kernel(
    hot_ref,
    turned_ref,
    list_ref,
    chosen_ref,
    n_ref,
    weight_ref,
    count_ref,
    n_in,
    s_in,
    hot_t_ref,
    n_pick_ref,
    n_small_ref,
    same_ref,
    inner_ref,
    mask_ref,
    local_ref,
    base_ref,
    row_ref,
    n_rest_ref,
    s_ref,
    sems,
):
    half = n_rest_ref.shape[1]
    rest_copy = pltpu.make_async_copy(n_in.at[0, :, pl.ds(half, half)], n_rest_ref, sems.at[0])
    s_copy = pltpu.make_async_copy(s_in, s_ref, sems.at[1])
    rest_copy.start()
    s_copy.start()
    width, total = hot_ref.shape
    weight = weight_ref[...]
    side = 128
    listed = list_ref[:1]
    lane = lax.broadcasted_iota(jnp.int32, (side, side), 1).astype(F32)
    hits = [jnp.zeros((1, side), F32)] * (width // side)
    same = []
    for k in range(0, total, side):
        down = jnp.broadcast_to(listed[:, k : k + side], (side, side)).T
        for m in range(width // side):
            block = jnp.where(down == lane + float(m * side), 1.0, 0.0)
            hits[m] = hits[m] + jnp.sum(block, 0, keepdims=True)
            hot_t_ref[k : k + side, m * side : (m + 1) * side] = block.astype(BF16)
        wide = jnp.concatenate([down] * (total // side), 1)
        same.append(jnp.where((wide == listed) & (wide >= 0.0), 1.0, 0.0))
    same = jnp.concatenate(same, 0)
    same_ref[...] = same.astype(BF16)
    inner = jnp.where(jnp.concatenate(hits, 1) > 0.0, 0.0, 1.0)
    inner_ref[...] = jnp.broadcast_to(inner, inner_ref.shape)
    n_pick_ref[:, :half] = times(hot_t_ref[...], n_ref[...]).astype(BF16)
    earlier = lax.broadcasted_iota(jnp.int32, same.shape, 0) < lax.broadcasted_iota(jnp.int32, same.shape, 1)
    repeats = jnp.sum(jnp.where(earlier, same, 0.0), 0, keepdims=True)
    first = jnp.where(repeats > 0.0, 0.0, 1.0)
    chosen = chosen_ref[:1]
    row_ref[0:1] = chosen
    row_ref[1:2] = chosen * first
    row_ref[2:3] = first
    row_ref[3:8] = jnp.zeros((5, total), F32)
    mask = jnp.where(lax.broadcasted_iota(jnp.int32, mask_ref.shape, 1) < count_ref[0], 1.0, 0.0)
    mask_ref[...] = mask
    local = mask[:1] * turned_ref[...].astype(F32)
    local_ref[...] = local
    rest_copy.wait()
    n_pick_ref[:, half:] = times(hot_t_ref[...], n_rest_ref[...]).astype(BF16)
    base_ref[...] = times_t((weight * local * inner).astype(BF16), n_pick_ref[...])
    n_small_ref[...] = times(n_pick_ref[...], hot_ref[...]).astype(BF16)
    s_copy.wait()


def update_path_kernel(trips, links, plan, plan_out, step, last, *refs):
    arrived_refs, refs = refs[:trips], refs[trips:]
    same_ref, n_small_ref, row_ref, local_ref, base_ref = refs[:5]
    refs = refs[5:]
    residual = local_ref[...].astype(F32) + times(gather(links, plan, arrived_refs), same_ref[...])
    scaled = (row_ref[1:2] * residual).astype(BF16)
    sent = row_ref[0:1] * (base_ref[...] + times_t(scaled, n_small_ref[...]))
    if last:
        scatter(links, plan_out, refs, sent)
    elif step == 0:
        scatter(links, plan_out, refs[1:], sent)
        refs[0][...] = DAMPING * sent
    else:
        scatter(links, plan_out, refs[2:], sent)
        refs[1][...] = refs[0][...] + DAMPING * sent


def residual_path_kernel(trips, links, plan, plan_out, last, *refs):
    arrived_refs, refs = refs[:trips], refs[trips:]
    same_ref, s_small_ref, row_ref, base_ref, state_ref, local_ref = refs[:6]
    state = state_ref[...] + DAMPING * times(gather(links, plan, arrived_refs), same_ref[...])
    if last:
        refs = refs[6:]
    else:
        refs[6][...] = state
        refs = refs[7:]
    local = base_ref[...] - times((state * row_ref[2:3]).astype(BF16), s_small_ref[...])
    local_ref[...] = local
    scatter(links, plan_out, refs, local)


def corrected(links, plan, arrived_refs, hot_ref, n_ref, n_rest_ref, weight_ref, mask_ref, local_ref):
    weight = weight_ref[...]
    residual = local_ref[...] + times_t(gather(links, plan, arrived_refs), hot_ref[...])
    scaled = (weight * residual).astype(BF16)
    half = n_ref.shape[1]
    product = times_t(scaled[:, :half], n_ref[...]) + times_t(scaled[:, half:], n_rest_ref[...])
    return mask_ref[:1] * weight * product


def first_update_kernel(trips, links, plan, *refs):
    arrived_refs, refs = refs[:trips], refs[trips:]
    hot_ref, hot_t_ref, n_ref, n_rest_ref, s_ref, weight_ref, mask_ref, inner_ref, local_ref, picked_ref = refs[:10]
    state_out_ref, base_ref, s_pick_ref, s_small_ref = refs[10:]
    state = DAMPING * corrected(links, plan, arrived_refs, hot_ref, n_ref, n_rest_ref, weight_ref, mask_ref, local_ref)
    state_out_ref[...] = state
    s_pick = times(s_ref[0], hot_ref[...]).astype(BF16)
    s_pick_ref[...] = s_pick
    s_small_ref[...] = times(hot_t_ref[...], s_pick).astype(BF16)
    base_ref[...] = picked_ref[...].astype(F32) - times((state * inner_ref[:1]).astype(BF16), s_pick)


def update_kernel(trips, links, plan, *refs):
    arrived_refs, refs = refs[:trips], refs[trips:]
    hot_ref, n_ref, n_rest_ref, weight_ref, mask_ref, inner_ref, local_ref, picked_ref, s_pick_ref, state_ref = refs[:10]
    state_out_ref, base_ref = refs[10:]
    state = state_ref[...] + DAMPING * corrected(links, plan, arrived_refs, hot_ref, n_ref, n_rest_ref, weight_ref, mask_ref, local_ref)
    state_out_ref[...] = state
    base_ref[...] = picked_ref[...].astype(F32) - times((state * inner_ref[:1]).astype(BF16), s_pick_ref[...])


def last_update_kernel(trips, links, plan, *refs):
    arrived_refs, refs = refs[:trips], refs[trips:]
    hot_ref, n_ref, n_rest_ref, weight_ref, mask_ref, local_ref, state_ref, state_out_ref = refs
    update = corrected(links, plan, arrived_refs, hot_ref, n_ref, n_rest_ref, weight_ref, mask_ref, local_ref)
    state_out_ref[...] = (state_ref[...] + DAMPING * update).T


def residual_kernel(trips, links, plan, *refs):
    arrived_refs, refs = refs[:trips], refs[trips:]
    hot_ref, s_ref, turned_ref, weight_ref, mask_ref, inner_ref, n_pick_ref, state_ref = refs[:8]
    state_out_ref, local_ref, base_ref = refs[8:]
    state = state_ref[...] + DAMPING * times_t(gather(links, plan, arrived_refs), hot_ref[...])
    state_out_ref[...] = state
    local = mask_ref[:1] * (turned_ref[...].astype(F32) - times(state.astype(BF16), s_ref[0]))
    local_ref[...] = local
    base_ref[...] = times_t((weight_ref[...] * local * inner_ref[:1]).astype(BF16), n_pick_ref[...])


def close_kernel(trips, links, plan, *refs):
    arrived_refs, (hot_ref, state_ref, out_ref, piece_ref, sems) = refs[:trips], refs[trips:]
    arrived = gather(links, plan, arrived_refs)
    rows = state_ref.shape[0] // PIECES
    copies = []
    for k in range(PIECES):
        part = pl.ds(k * rows, rows)
        piece_ref[part, :] = state_ref[part, :] + DAMPING * times_t(hot_ref[part, :], arrived)
        copies.append(pltpu.make_async_copy(piece_ref.at[part, :], out_ref.at[0, part, :], sems.at[k]))
        copies[k].start()
    for copy in copies:
        copy.wait()


def run(kernel, operands, results, flops, spaces=(), outputs=pltpu.VMEM, scratch=()):
    spaces = [dict(spaces).get(k, pltpu.VMEM) for k in range(len(operands))]
    moved = sum(a.size * a.dtype.itemsize for a in (*operands, *results))
    operands = [
        pltpu.with_memory_space_constraint(a, space) if space is pltpu.HBM else a for a, space in zip(operands, spaces)
    ]
    return pl.pallas_call(
        kernel,
        out_shape=results,
        in_specs=[pl.BlockSpec(memory_space=space) for space in spaces],
        out_specs=[pl.BlockSpec(memory_space=outputs)] * len(results),
        scratch_shapes=scratch,
        compiler_params=pltpu.CompilerParams(vmem_limit_bytes=LIMIT),
        cost_estimate=pl.CostEstimate(flops=flops, bytes_accessed=moved, transcendentals=0),
    )(*operands)


def body(right_side, schur, neumann, weights, neighbours, counts, shared_rows):
    width, leads = right_side.shape[1:]
    share = shared_rows.shape[2]
    subs = lax.axis_size("sub")
    plans = [min(k // 2, len(PLANS) - 1) for k in range(2 * ITERS)]
    trips = len(swaps(subs, plans[0]))
    links = len(slots_of(0, subs))
    total = links * share

    def array(rows, columns, kind=F32):
        return jax.ShapeDtypeStruct((rows, columns), kind)

    def same_as(a):
        return jax.ShapeDtypeStruct(a.shape, a.dtype)

    messages = [array(leads, share, BF16)] * trips
    full, some = array(leads, width), array(leads, total)
    small = array(total, total, BF16)
    row = array(8, width)
    half = array(width, width // 2, BF16)
    picks = 2 * leads * total * width
    whole = 2 * leads * width * width
    path = 4 * leads * total * total

    def exchange(parts, plan):
        return [lax.ppermute(part, "sub", route) for part, route in zip(parts, swaps(subs, plan))]

    def bound(kernel, *settings):
        return functools.partial(kernel, trips, links, *settings)

    hot, turned, picked, listed, chosen, weight, n_mat, *sent = run(
        bound(open_kernel, plans[0], subs),
        [shared_rows, neighbours, right_side, weights, neumann],
        [
            array(width, total, BF16),
            array(leads, width, BF16),
            array(leads, total, BF16),
            array(8, total),
            array(8, total),
            same_as(weights),
            half,
            *messages,
        ],
        picks,
        spaces={k: pltpu.HBM for k in range(5)},
        scratch=[
            pltpu.VMEM(shared_rows.shape, jnp.int32),
            pltpu.VMEM(neighbours.shape, jnp.int32),
            pltpu.VMEM(right_side.shape, BF16),
            pltpu.SemaphoreType.DMA((5,)),
        ],
    )
    arrived = exchange(sent, plans[0])
    hot_t, n_pick, n_small, same, inner, mask, local, base, rows, n_rest, s_mat = run(
        pick_n_kernel,
        [hot, turned, listed, chosen, n_mat, weight, counts, neumann, schur],
        [
            array(total, width, BF16),
            array(total, width, BF16),
            small,
            small,
            row,
            row,
            full,
            some,
            array(8, total),
            half,
            same_as(schur),
        ],
        2 * total * width * width + 2 * total * total * width + picks,
        spaces={6: pltpu.SMEM, 7: pltpu.HBM, 8: pltpu.HBM},
        scratch=[pltpu.SemaphoreType.DMA((2,))],
    )
    near = picked
    near_state = None
    for step in range(ITERS):
        came, last = arrived, step == ITERS - 1
        plan, next_plan, after = (*plans[2 * step :], None)[:3]
        operands = [*came, same, n_small, rows, near, base]
        if step and not last:
            operands.append(near_state)
        kernel = bound(update_path_kernel, plan, next_plan, step, last)
        if last:
            sent = run(kernel, operands, messages, path)
            arrived = exchange(sent, next_plan)
            (state,) = run(
                bound(last_update_kernel, plan),
                [*came, hot, n_mat, n_rest, weight, mask, local, state],
                [array(width, leads)],
                whole + picks,
            )
            break
        near_state, *sent = run(kernel, operands, [some, *messages], path)
        arrived = exchange(sent, next_plan)
        if step == 0:
            state, base, s_pick, s_small = run(
                bound(first_update_kernel, plan),
                [*came, hot, hot_t, n_mat, n_rest, s_mat, weight, mask, inner, local, picked],
                [full, some, array(width, total, BF16), small],
                whole + 2 * picks + 2 * total * width * (width + total),
            )
        else:
            state, base = run(
                bound(update_kernel, plan),
                [*came, hot, n_mat, n_rest, weight, mask, inner, local, picked, s_pick, state],
                [full, some],
                whole + 2 * picks,
            )
        came = arrived
        ends = step == ITERS - 2
        near, *sent = run(
            bound(residual_path_kernel, next_plan, after, ends),
            [*came, same, s_small, rows, base, near_state],
            [some, *([] if ends else [some]), *messages],
            path,
        )
        if not ends:
            near_state, *sent = sent
        arrived = exchange(sent, after)
        state, local, base = run(
            bound(residual_kernel, next_plan),
            [*came, hot, s_mat, turned, weight, mask, inner, n_pick, state],
            [full, full, some],
            whole + 2 * picks,
        )
    (out,) = run(
        bound(close_kernel, plans[-1]),
        [*arrived, hot, state],
        [jax.ShapeDtypeStruct((1, width, leads), F32)],
        picks,
        outputs=pltpu.HBM,
        scratch=[pltpu.VMEM((width, leads), F32), pltpu.SemaphoreType.DMA((PIECES,))],
    )
    return out


def solution(mesh):
    in_specs = (
        P("sub", None, None),
        P("sub", None, None),
        P("sub", None, None),
        P("sub", None),
        P("sub", None),
        P("sub"),
        P("sub", None, None),
    )
    out_specs = P("sub", None, None)
    return jax.shard_map(body, mesh=mesh, in_specs=in_specs, out_specs=out_specs, check_vma=False)
```

```python
import functools

import jax
import jax.numpy as jnp
from jax import lax
from jax.experimental import pallas as pl
from jax.experimental.pallas import tpu as pltpu
from jax.sharding import PartitionSpec as P

ITERS = 4
FAR = 16
DAMPING = 0.7
LIMIT = 16 * 2**20
PIECES = 4
F32 = jnp.float32
BF16 = jnp.bfloat16


PLANS = (
    (
        (0, 1, 2, 0, 2, 2, 2, 0, 0, 0, 0, 1, 2, 2, 2, 2),
        (0, 1, 1, 1, 1, 0, 0, 1, 0, 1, 1, 1, 2, 0, 1),
        (((6, 15), (22, 29)), ((0, 2), (14, 18), (25, 26), (28, 31)), ((3, 7), (19, 23), (24, 27))),
    ),
    (
        (0, 1, 1, 0, 0, 0, 0, 1, 1, 1, 1, 0, 0, 0, 0, 0),
        (0, 2, 1, 0, 0, 1, 2, 1, 0, 1, 1, 0, 0, 1, 1),
        ((), ((0, 3), (4, 13), (14, 31)), ((2, 5), (12, 15))),
    ),
)


def turns(count, plan):
    far_turns, odd_turns, _ = PLANS[plan]
    far = [far_turns[i % FAR] for i in range(count)]
    odd = [odd_turns[(i - 1) // 2] if 0 < i < count - 1 else -1 for i in range(count)]
    return far, odd


def mixed(count):
    return count == 2 * FAR


def swaps(count, plan):
    blocks = count // FAR
    near = [i ^ 1 for i in range(count)]
    far = [i ^ FAR for i in range(count)]
    odd = [(((i + 1) ^ 1) - 1) % count for i in range(count)]
    if mixed(count):
        far_turns, odd_turns = turns(count, plan)
        pairings = []
        for turn, fill in enumerate(PLANS[plan][2]):
            pairing = list(near)
            for i, j in fill:
                pairing[i], pairing[j] = j, i
            for i in range(count):
                if far_turns[i] == turn:
                    pairing[i] = far[i]
                elif odd_turns[i] == turn:
                    pairing[i] = odd[i]
            pairings.append(pairing)
        pairings.append(near)
    else:
        again = [(((i // FAR + 1) ^ 1) - 1) % blocks * FAR + i % FAR for i in range(count)]
        pairings = ([far] if blocks > 1 else []) + ([again] if blocks > 2 else []) + [odd, near]
    for pairing in pairings:
        assert all(pairing[j] == i != j for i, j in enumerate(pairing))
    return [list(enumerate(pairing)) for pairing in pairings]


def is_turn(own_turns, turn):
    bits = sum(1 << i for i, own in enumerate(own_turns) if own == turn)
    bits = bits - (1 << 32) if bits >> 31 else bits
    return lax.shift_right_logical(jnp.int32(bits), lax.axis_index("sub")) & 1 == 1


def slots_of(index, count):
    odd = lax.rem(index, 2)
    block = lax.rem(lax.div(index, FAR), 2)
    blocks = count // FAR
    far = [2 + block] if blocks > 1 else []
    again = [3 - block] if blocks > 2 else []
    return [*far, *again, 1 - odd, odd]


def times(a, b):
    return jnp.dot(a, b, preferred_element_type=F32)


def times_t(a, b):
    return lax.dot_general(a, b, (((1,), (1,)), ((), ())), preferred_element_type=F32)


def gather(links, plan, refs):
    parts = [ref[...] for ref in refs]
    if len(parts) > links:
        values = [part.astype(F32) for part in parts[:3]]
        picked = []
        for own in turns(2 * FAR, plan):
            later = jnp.where(is_turn(own, 1), values[1], values[2])
            picked.append(jnp.where(is_turn(own, 0), values[0], later).astype(BF16))
        parts = [*picked, parts[3]]
    return jnp.concatenate(parts, 1)


def early_part(links, plan, third, near):
    if links > 3:
        return jnp.concatenate([*[jnp.zeros_like(third)] * (links - 2), third, near], 1)
    value, none = third.astype(F32), jnp.zeros(third.shape, F32)
    parts = [jnp.where(is_turn(own, 2), value, none).astype(BF16) for own in turns(2 * FAR, plan)]
    return jnp.concatenate([*parts, near], 1)


def late_product(links, plan, first, second, same_ref):
    parts = [first, second]
    if links == 3:
        values = [first.astype(F32), second.astype(F32)]
        none = jnp.zeros(first.shape, F32)
        parts = []
        for own in turns(2 * FAR, plan):
            other = jnp.where(is_turn(own, 1), values[1], none)
            parts.append(jnp.where(is_turn(own, 0), values[0], other).astype(BF16))
    return times(jnp.concatenate(parts, 1), same_ref[: 2 * first.shape[1], :])


def early_kernel(links, plan, scale, third_ref, near_ref, same_ref, state_ref, out_ref):
    arrived = early_part(links, plan, third_ref[...], near_ref[...])
    out_ref[...] = state_ref[...].astype(F32) + scale * times(arrived, same_ref[...])


def scatter(links, plan, refs, block):
    share = refs[0].shape[1]
    parts = [block[:, k * share : (k + 1) * share].astype(F32) for k in range(links)]
    if len(refs) > links:
        far, odd, near = parts
        own, _ = turns(2 * FAR, plan)
        parts = [*(jnp.where(is_turn(own, turn), far, odd) for turn in range(3)), near]
    for ref, part in zip(refs, parts):
        ref[...] = part.astype(BF16)


def open_kernel(
    trips,
    links,
    plan_out,
    subs,
    rows_in,
    near_in,
    rhs_in,
    weight_in,
    n_in,
    hot_ref,
    turned_ref,
    picked_ref,
    list_ref,
    weight_ref,
    n_ref,
    *refs,
):
    out_refs, (rows_ref, near_ref, rhs_ref, sems) = refs[:trips], refs[trips:]
    pairs = [
        (rows_in, rows_ref),
        (near_in, near_ref),
        (rhs_in, rhs_ref),
        (weight_in, weight_ref),
        (n_in, n_ref),
    ]
    copies = [pltpu.make_async_copy(source, target, sems.at[k]) for k, (source, target) in enumerate(pairs)]
    for copy in copies:
        copy.start()
    width, share = rhs_ref.shape[1], rows_ref.shape[2]
    slots = slots_of(lax.axis_index("sub"), subs)
    place = lax.broadcasted_iota(jnp.int32, (width, share), 0)
    copies[0].wait()
    copies[1].wait()
    near = near_ref[...].astype(F32)
    lane = lax.broadcasted_iota(jnp.int32, near.shape, 1)
    for k, slot in enumerate(slots):
        partner = jnp.sum(jnp.where(lane == slot, near, 0.0), 1, keepdims=True)
        row = jnp.where(partner >= 0.0, rows_ref[0, pl.ds(slot, 1), :], -1)
        list_ref[:, pl.ds(k * share, share)] = jnp.broadcast_to(row.astype(F32), (list_ref.shape[0], share))
        hot_ref[:, pl.ds(k * share, share)] = jnp.where(place == row, 1.0, 0.0).astype(BF16)
    copies[2].wait()
    turned = rhs_ref[0].T
    turned_ref[...] = turned
    picked = times(turned, hot_ref[...]).astype(BF16)
    picked_ref[...] = picked
    scatter(links, plan_out, out_refs, picked)
    for copy in copies[3:]:
        copy.wait()


def pick_n_kernel(
    hot_ref,
    turned_ref,
    list_ref,
    n_ref,
    weight_ref,
    count_ref,
    s_in,
    hot_t_ref,
    n_pick_ref,
    n_small_ref,
    same_ref,
    inner_ref,
    mask_ref,
    local_ref,
    base_ref,
    row_ref,
    s_ref,
    sem,
):
    copy = pltpu.make_async_copy(s_in, s_ref, sem)
    copy.start()
    hot = hot_ref[...]
    width, total = hot.shape
    weight = weight_ref[...]
    side = 128
    listed = list_ref[:1]
    lane = lax.broadcasted_iota(jnp.int32, (side, side), 1).astype(F32)
    hits = [jnp.zeros((1, side), F32)] * (width // side)
    same = []
    for k in range(0, total, side):
        down = jnp.broadcast_to(listed[:, k : k + side], (side, side)).T
        for m in range(width // side):
            block = jnp.where(down == lane + float(m * side), 1.0, 0.0)
            hits[m] = hits[m] + jnp.sum(block, 0, keepdims=True)
            hot_t_ref[k : k + side, m * side : (m + 1) * side] = block.astype(BF16)
        wide = jnp.concatenate([down] * (total // side), 1)
        same.append(jnp.where((wide == listed) & (wide >= 0.0), 1.0, 0.0))
    same = jnp.concatenate(same, 0)
    same_ref[...] = same.astype(BF16)
    inner = jnp.where(jnp.concatenate(hits, 1) > 0.0, 0.0, 1.0)
    inner_ref[...] = jnp.broadcast_to(inner, inner_ref.shape)
    n_pick = times(hot_t_ref[...], n_ref[0]).astype(BF16)
    n_pick_ref[...] = n_pick
    n_small_ref[...] = times(n_pick, hot).astype(BF16)
    earlier = lax.broadcasted_iota(jnp.int32, same.shape, 0) < lax.broadcasted_iota(jnp.int32, same.shape, 1)
    repeats = jnp.sum(jnp.where(earlier, same, 0.0), 0, keepdims=True)
    first = jnp.where(repeats > 0.0, 0.0, 1.0)
    high = weight.astype(BF16).astype(F32)
    middle = (weight - high).astype(BF16).astype(F32)
    low = weight - high - middle
    level = lax.broadcasted_iota(jnp.int32, (8, width), 0)
    pieces = jnp.where(level == 0, high, jnp.where(level == 1, middle, jnp.where(level == 2, low, 0.0)))
    pieces = times(pieces.astype(BF16), hot)
    chosen = (pieces[0:1] + pieces[1:2]) + pieces[2:3]
    row_ref[0:1] = chosen
    row_ref[1:2] = chosen * first
    row_ref[2:3] = first
    row_ref[3:8] = jnp.zeros((5, total), F32)
    mask = jnp.where(lax.broadcasted_iota(jnp.int32, mask_ref.shape, 1) < count_ref[0], 1.0, 0.0)
    mask_ref[...] = mask
    local = mask[:1] * turned_ref[...].astype(F32)
    local_ref[...] = local
    base_ref[...] = times_t((weight * local * inner).astype(BF16), n_pick)
    copy.wait()


def update_path_kernel(trips, links, plan, plan_out, step, last, *refs):
    first_ref, second_ref, *refs = refs
    same_ref, n_small_ref, row_ref, local_ref, base_ref = refs[:5]
    refs = refs[5:]
    residual = local_ref[...] + late_product(links, plan, first_ref[...], second_ref[...], same_ref)
    scaled = (row_ref[1:2] * residual).astype(BF16)
    sent = row_ref[0:1] * (base_ref[...] + times_t(scaled, n_small_ref[...]))
    if last:
        scatter(links, plan_out, refs, sent)
    elif step == 0:
        scatter(links, plan_out, refs[1:], sent)
        refs[0][...] = DAMPING * sent
    else:
        scatter(links, plan_out, refs[2:], sent)
        refs[1][...] = refs[0][...] + DAMPING * sent


def residual_path_kernel(trips, links, plan, plan_out, last, *refs):
    first_ref, second_ref, *refs = refs
    same_ref, s_small_ref, row_ref, base_ref, state_ref, local_ref = refs[:6]
    state = state_ref[...] + DAMPING * late_product(links, plan, first_ref[...], second_ref[...], same_ref)
    if last:
        refs = refs[6:]
    else:
        refs[6][...] = state
        refs = refs[7:]
    local = base_ref[...] - times((state * row_ref[2:3]).astype(BF16), s_small_ref[...])
    local_ref[...] = local
    scatter(links, plan_out, refs, local)


def corrected(links, plan, arrived_refs, hot_ref, n_ref, weight_ref, mask_ref, local_ref):
    weight = weight_ref[...]
    residual = local_ref[...] + times_t(gather(links, plan, arrived_refs), hot_ref[...])
    scaled = (weight * residual).astype(BF16)
    return mask_ref[:1] * weight * times_t(scaled, n_ref[0])


def first_update_kernel(trips, links, plan, *refs):
    arrived_refs, refs = refs[:trips], refs[trips:]
    hot_ref, hot_t_ref, n_ref, s_ref, weight_ref, mask_ref, inner_ref, local_ref, picked_ref = refs[:9]
    state_out_ref, base_ref, s_pick_ref, s_small_ref = refs[9:]
    state = DAMPING * corrected(links, plan, arrived_refs, hot_ref, n_ref, weight_ref, mask_ref, local_ref)
    state_out_ref[...] = state
    s_pick = times(s_ref[0], hot_ref[...]).astype(BF16)
    s_pick_ref[...] = s_pick
    s_small_ref[...] = times(hot_t_ref[...], s_pick).astype(BF16)
    base_ref[...] = picked_ref[...].astype(F32) - times((state * inner_ref[:1]).astype(BF16), s_pick)


def update_kernel(trips, links, plan, *refs):
    arrived_refs, refs = refs[:trips], refs[trips:]
    hot_ref, n_ref, weight_ref, mask_ref, inner_ref, local_ref, picked_ref, s_pick_ref, state_ref = refs[:9]
    state_out_ref, base_ref = refs[9:]
    state = state_ref[...] + DAMPING * corrected(links, plan, arrived_refs, hot_ref, n_ref, weight_ref, mask_ref, local_ref)
    state_out_ref[...] = state
    base_ref[...] = picked_ref[...].astype(F32) - times((state * inner_ref[:1]).astype(BF16), s_pick_ref[...])


def last_update_kernel(trips, links, plan, *refs):
    arrived_refs, refs = refs[:trips], refs[trips:]
    hot_ref, n_ref, weight_ref, mask_ref, local_ref, state_ref, state_out_ref = refs
    update = corrected(links, plan, arrived_refs, hot_ref, n_ref, weight_ref, mask_ref, local_ref)
    state_out_ref[...] = (state_ref[...] + DAMPING * update).T


def residual_kernel(trips, links, plan, *refs):
    arrived_refs, refs = refs[:trips], refs[trips:]
    hot_ref, s_ref, turned_ref, weight_ref, mask_ref, inner_ref, n_pick_ref, state_ref = refs[:8]
    state_out_ref, local_ref, base_ref = refs[8:]
    state = state_ref[...] + DAMPING * times_t(gather(links, plan, arrived_refs), hot_ref[...])
    state_out_ref[...] = state
    local = mask_ref[:1] * (turned_ref[...].astype(F32) - times(state.astype(BF16), s_ref[0]))
    local_ref[...] = local
    base_ref[...] = times_t((weight_ref[...] * local * inner_ref[:1]).astype(BF16), n_pick_ref[...])


def close_kernel(trips, links, plan, *refs):
    arrived_refs, (hot_ref, state_ref, out_ref, piece_ref, sems) = refs[:trips], refs[trips:]
    arrived = gather(links, plan, arrived_refs)
    rows = state_ref.shape[0] // PIECES
    copies = []
    for k in range(PIECES):
        part = pl.ds(k * rows, rows)
        piece_ref[part, :] = state_ref[part, :] + DAMPING * times_t(hot_ref[part, :], arrived)
        copies.append(pltpu.make_async_copy(piece_ref.at[part, :], out_ref.at[0, part, :], sems.at[k]))
        copies[k].start()
    for copy in copies:
        copy.wait()


def run(kernel, operands, results, flops, spaces=(), outputs=pltpu.VMEM, scratch=()):
    spaces = [dict(spaces).get(k, pltpu.VMEM) for k in range(len(operands))]
    moved = sum(a.size * a.dtype.itemsize for a in (*operands, *results))
    operands = [
        pltpu.with_memory_space_constraint(a, space) if space is pltpu.HBM else a for a, space in zip(operands, spaces)
    ]
    return pl.pallas_call(
        kernel,
        out_shape=results,
        in_specs=[pl.BlockSpec(memory_space=space) for space in spaces],
        out_specs=[pl.BlockSpec(memory_space=outputs)] * len(results),
        scratch_shapes=scratch,
        compiler_params=pltpu.CompilerParams(vmem_limit_bytes=LIMIT),
        cost_estimate=pl.CostEstimate(flops=flops, bytes_accessed=moved, transcendentals=0),
    )(*operands)


def body(right_side, schur, neumann, weights, neighbours, counts, shared_rows):
    width, leads = right_side.shape[1:]
    share = shared_rows.shape[2]
    subs = lax.axis_size("sub")
    plans = [min(k // 2, len(PLANS) - 1) for k in range(2 * ITERS)]
    trips = len(swaps(subs, plans[0]))
    links = len(slots_of(0, subs))
    total = links * share

    def array(rows, columns, kind=F32):
        return jax.ShapeDtypeStruct((rows, columns), kind)

    def same_as(a):
        return jax.ShapeDtypeStruct(a.shape, a.dtype)

    messages = [array(leads, share, BF16)] * trips
    full, some = array(leads, width), array(leads, total)
    small = array(total, total, BF16)
    row = array(8, width)
    picks = 2 * leads * total * width
    whole = 2 * leads * width * width
    path = 4 * leads * total * total

    def exchange(parts, plan):
        return [lax.ppermute(part, "sub", route) for part, route in zip(parts, swaps(subs, plan))]

    def bound(kernel, *settings):
        return functools.partial(kernel, trips, links, *settings)

    hot, turned, picked, listed, weight, n_mat, *sent = run(
        bound(open_kernel, plans[0], subs),
        [shared_rows, neighbours, right_side, weights, neumann],
        [
            array(width, total, BF16),
            array(leads, width, BF16),
            array(leads, total, BF16),
            array(8, total),
            same_as(weights),
            same_as(neumann),
            *messages,
        ],
        picks,
        spaces={k: pltpu.HBM for k in range(5)},
        scratch=[
            pltpu.VMEM(shared_rows.shape, jnp.int32),
            pltpu.VMEM(neighbours.shape, jnp.int32),
            pltpu.VMEM(right_side.shape, BF16),
            pltpu.SemaphoreType.DMA((5,)),
        ],
    )
    arrived = exchange(sent, plans[0])
    hot_t, n_pick, n_small, same, inner, mask, local, base, rows, s_mat = run(
        pick_n_kernel,
        [hot, turned, listed, n_mat, weight, counts, schur],
        [
            array(total, width, BF16),
            array(total, width, BF16),
            small,
            small,
            row,
            row,
            full,
            some,
            array(8, total),
            same_as(schur),
        ],
        2 * total * width * width + 2 * total * total * width + picks,
        spaces={5: pltpu.SMEM, 6: pltpu.HBM},
        scratch=[pltpu.SemaphoreType.DMA],
    )
    def early(came, plan, scale, at):
        kernel = functools.partial(early_kernel, links, plan, scale)
        (out,) = run(kernel, [came[2], came[3], same, at], [some], path // 2)
        return out

    near = picked
    near_state = None
    for step in range(ITERS):
        came, last = arrived, step == ITERS - 1
        plan, next_plan, after = (*plans[2 * step :], None)[:3]
        near = early(came, plan, 1.0, near)
        operands = [*came[:2], same, n_small, rows, near, base]
        if step and not last:
            operands.append(near_state)
        kernel = bound(update_path_kernel, plan, next_plan, step, last)
        if last:
            sent = run(kernel, operands, messages, path)
            arrived = exchange(sent, next_plan)
            (state,) = run(
                bound(last_update_kernel, plan),
                [*came, hot, n_mat, weight, mask, local, state],
                [array(width, leads)],
                whole + picks,
            )
            break
        near_state, *sent = run(kernel, operands, [some, *messages], path)
        arrived = exchange(sent, next_plan)
        if step == 0:
            state, base, s_pick, s_small = run(
                bound(first_update_kernel, plan),
                [*came, hot, hot_t, n_mat, s_mat, weight, mask, inner, local, picked],
                [full, some, array(width, total, BF16), small],
                whole + 2 * picks + 2 * total * width * (width + total),
            )
        else:
            state, base = run(
                bound(update_kernel, plan),
                [*came, hot, n_mat, weight, mask, inner, local, picked, s_pick, state],
                [full, some],
                whole + 2 * picks,
            )
        came = arrived
        ends = step == ITERS - 2
        near, *sent = run(
            bound(residual_path_kernel, next_plan, after, ends),
            [*came[:2], same, s_small, rows, base, early(came, next_plan, DAMPING, near_state)],
            [some, *([] if ends else [some]), *messages],
            path,
        )
        if not ends:
            near_state, *sent = sent
        arrived = exchange(sent, after)
        state, local, base = run(
            bound(residual_kernel, next_plan),
            [*came, hot, s_mat, turned, weight, mask, inner, n_pick, state],
            [full, full, some],
            whole + 2 * picks,
        )
    (out,) = run(
        bound(close_kernel, plans[-1]),
        [*arrived, hot, state],
        [jax.ShapeDtypeStruct((1, width, leads), F32)],
        picks,
        outputs=pltpu.HBM,
        scratch=[pltpu.VMEM((width, leads), F32), pltpu.SemaphoreType.DMA((PIECES,))],
    )
    return out


def solution(mesh):
    in_specs = (
        P("sub", None, None),
        P("sub", None, None),
        P("sub", None, None),
        P("sub", None),
        P("sub", None),
        P("sub"),
        P("sub", None, None),
    )
    out_specs = P("sub", None, None)
    return jax.shard_map(body, mesh=mesh, in_specs=in_specs, out_specs=out_specs, check_vma=False)
```

```python
import functools

import jax
import jax.numpy as jnp
from jax import lax
from jax.experimental import pallas as pl
from jax.experimental.pallas import tpu as pltpu
from jax.sharding import PartitionSpec as P

ITERS = 4
FAR = 16
DAMPING = 0.7
LIMIT = 16 * 2**20
PIECES = 4
F32 = jnp.float32
BF16 = jnp.bfloat16


PLANS = (
    (
        (0, 1, 2, 0, 2, 2, 2, 0, 0, 0, 0, 1, 2, 2, 2, 2),
        (0, 1, 1, 1, 1, 0, 0, 1, 0, 1, 1, 1, 2, 0, 1),
        (((6, 15), (22, 29)), ((0, 2), (14, 18), (25, 26), (28, 31)), ((3, 7), (19, 23), (24, 27))),
    ),
    (
        (0, 1, 1, 0, 0, 0, 0, 1, 1, 1, 1, 0, 0, 0, 0, 0),
        (0, 2, 1, 0, 0, 1, 2, 1, 0, 1, 1, 0, 0, 1, 1),
        ((), ((0, 3), (4, 13), (14, 31)), ((2, 5), (12, 15))),
    ),
)


def turns(count, plan):
    far_turns, odd_turns, _ = PLANS[plan]
    far = [far_turns[i % FAR] for i in range(count)]
    odd = [odd_turns[(i - 1) // 2] if 0 < i < count - 1 else -1 for i in range(count)]
    return far, odd


def mixed(count):
    return count == 2 * FAR


def swaps(count, plan):
    blocks = count // FAR
    near = [i ^ 1 for i in range(count)]
    far = [i ^ FAR for i in range(count)]
    odd = [(((i + 1) ^ 1) - 1) % count for i in range(count)]
    if mixed(count):
        far_turns, odd_turns = turns(count, plan)
        pairings = []
        for turn, fill in enumerate(PLANS[plan][2]):
            pairing = list(near)
            for i, j in fill:
                pairing[i], pairing[j] = j, i
            for i in range(count):
                if far_turns[i] == turn:
                    pairing[i] = far[i]
                elif odd_turns[i] == turn:
                    pairing[i] = odd[i]
            pairings.append(pairing)
        pairings.append(near)
    else:
        again = [(((i // FAR + 1) ^ 1) - 1) % blocks * FAR + i % FAR for i in range(count)]
        pairings = ([far] if blocks > 1 else []) + ([again] if blocks > 2 else []) + [odd, near]
    for pairing in pairings:
        assert all(pairing[j] == i != j for i, j in enumerate(pairing))
    return [list(enumerate(pairing)) for pairing in pairings]


def is_turn(own_turns, turn):
    bits = sum(1 << i for i, own in enumerate(own_turns) if own == turn)
    bits = bits - (1 << 32) if bits >> 31 else bits
    return lax.shift_right_logical(jnp.int32(bits), lax.axis_index("sub")) & 1 == 1


def slots_of(index, count):
    odd = lax.rem(index, 2)
    block = lax.rem(lax.div(index, FAR), 2)
    blocks = count // FAR
    far = [2 + block] if blocks > 1 else []
    again = [3 - block] if blocks > 2 else []
    return [*far, *again, 1 - odd, odd]


def times(a, b):
    return jnp.dot(a, b, preferred_element_type=F32)


def times_t(a, b):
    return lax.dot_general(a, b, (((1,), (1,)), ((), ())), preferred_element_type=F32)


def gather(links, plan, refs):
    parts = [ref[...] for ref in refs]
    if len(parts) > links:
        values = [part.astype(F32) for part in parts[:3]]
        picked = []
        for own in turns(2 * FAR, plan):
            later = jnp.where(is_turn(own, 1), values[1], values[2])
            picked.append(jnp.where(is_turn(own, 0), values[0], later).astype(BF16))
        parts = [*picked, parts[3]]
    return jnp.concatenate(parts, 1)


def scatter(links, plan, refs, block):
    share = refs[0].shape[1]
    parts = [block[:, k * share : (k + 1) * share].astype(F32) for k in range(links)]
    if len(refs) > links:
        far, odd, near = parts
        own, _ = turns(2 * FAR, plan)
        parts = [*(jnp.where(is_turn(own, turn), far, odd) for turn in range(3)), near]
    for ref, part in zip(refs, parts):
        ref[...] = part.astype(BF16)


def open_kernel(
    trips,
    links,
    plan_out,
    subs,
    rows_in,
    near_in,
    rhs_in,
    weight_in,
    n_in,
    hot_ref,
    turned_ref,
    picked_ref,
    list_ref,
    weight_ref,
    n_ref,
    *refs,
):
    out_refs, (rows_ref, near_ref, rhs_ref, sems) = refs[:trips], refs[trips:]
    pairs = [
        (rows_in, rows_ref),
        (near_in, near_ref),
        (rhs_in, rhs_ref),
        (weight_in, weight_ref),
        (n_in.at[0, :, pl.ds(0, n_ref.shape[1])], n_ref),
    ]
    copies = [pltpu.make_async_copy(source, target, sems.at[k]) for k, (source, target) in enumerate(pairs)]
    for copy in copies:
        copy.start()
    width, share = rhs_ref.shape[1], rows_ref.shape[2]
    slots = slots_of(lax.axis_index("sub"), subs)
    place = lax.broadcasted_iota(jnp.int32, (width, share), 0)
    copies[0].wait()
    copies[1].wait()
    near = near_ref[...].astype(F32)
    lane = lax.broadcasted_iota(jnp.int32, near.shape, 1)
    for k, slot in enumerate(slots):
        partner = jnp.sum(jnp.where(lane == slot, near, 0.0), 1, keepdims=True)
        row = jnp.where(partner >= 0.0, rows_ref[0, pl.ds(slot, 1), :], -1)
        list_ref[:, pl.ds(k * share, share)] = jnp.broadcast_to(row.astype(F32), (list_ref.shape[0], share))
        hot_ref[:, pl.ds(k * share, share)] = jnp.where(place == row, 1.0, 0.0).astype(BF16)
    copies[2].wait()
    turned = rhs_ref[0].T
    turned_ref[...] = turned
    picked = times(turned, hot_ref[...]).astype(BF16)
    picked_ref[...] = picked
    scatter(links, plan_out, out_refs, picked)
    for copy in copies[3:]:
        copy.wait()


def pick_n_kernel(
    hot_ref,
    turned_ref,
    list_ref,
    n_ref,
    weight_ref,
    count_ref,
    n_in,
    s_in,
    hot_t_ref,
    n_pick_ref,
    n_small_ref,
    same_ref,
    inner_ref,
    mask_ref,
    local_ref,
    base_ref,
    row_ref,
    n_rest_ref,
    s_ref,
    sems,
):
    cut = n_ref.shape[1]
    rest_copy = pltpu.make_async_copy(n_in.at[0, :, pl.ds(cut, n_rest_ref.shape[1])], n_rest_ref, sems.at[0])
    s_copy = pltpu.make_async_copy(s_in, s_ref, sems.at[1])
    rest_copy.start()
    s_copy.start()
    hot = hot_ref[...]
    width, total = hot.shape
    weight = weight_ref[...]
    side = 128
    listed = list_ref[:1]
    lane = lax.broadcasted_iota(jnp.int32, (side, side), 1).astype(F32)
    hits = [jnp.zeros((1, side), F32)] * (width // side)
    same = []
    for k in range(0, total, side):
        down = jnp.broadcast_to(listed[:, k : k + side], (side, side)).T
        for m in range(width // side):
            block = jnp.where(down == lane + float(m * side), 1.0, 0.0)
            hits[m] = hits[m] + jnp.sum(block, 0, keepdims=True)
            hot_t_ref[k : k + side, m * side : (m + 1) * side] = block.astype(BF16)
        wide = jnp.concatenate([down] * (total // side), 1)
        same.append(jnp.where((wide == listed) & (wide >= 0.0), 1.0, 0.0))
    same = jnp.concatenate(same, 0)
    same_ref[...] = same.astype(BF16)
    inner = jnp.where(jnp.concatenate(hits, 1) > 0.0, 0.0, 1.0)
    inner_ref[...] = jnp.broadcast_to(inner, inner_ref.shape)
    n_pick_ref[:, :cut] = times(hot_t_ref[...], n_ref[...]).astype(BF16)
    earlier = lax.broadcasted_iota(jnp.int32, same.shape, 0) < lax.broadcasted_iota(jnp.int32, same.shape, 1)
    repeats = jnp.sum(jnp.where(earlier, same, 0.0), 0, keepdims=True)
    first = jnp.where(repeats > 0.0, 0.0, 1.0)
    high = weight.astype(BF16).astype(F32)
    middle = (weight - high).astype(BF16).astype(F32)
    low = weight - high - middle
    level = lax.broadcasted_iota(jnp.int32, (8, width), 0)
    pieces = jnp.where(level == 0, high, jnp.where(level == 1, middle, jnp.where(level == 2, low, 0.0)))
    pieces = times(pieces.astype(BF16), hot)
    chosen = (pieces[0:1] + pieces[1:2]) + pieces[2:3]
    row_ref[0:1] = chosen
    row_ref[1:2] = chosen * first
    row_ref[2:3] = first
    row_ref[3:8] = jnp.zeros((5, total), F32)
    rest_copy.wait()
    n_pick_ref[:, cut:] = times(hot_t_ref[...], n_rest_ref[...]).astype(BF16)
    n_pick = n_pick_ref[...]
    n_small_ref[...] = times(n_pick, hot).astype(BF16)
    mask = jnp.where(lax.broadcasted_iota(jnp.int32, mask_ref.shape, 1) < count_ref[0], 1.0, 0.0)
    mask_ref[...] = mask
    local = mask[:1] * turned_ref[...].astype(F32)
    local_ref[...] = local
    base_ref[...] = times_t((weight * local * inner).astype(BF16), n_pick)
    s_copy.wait()


def update_path_kernel(trips, links, plan, plan_out, step, last, *refs):
    arrived_refs, refs = refs[:trips], refs[trips:]
    same_ref, n_small_ref, row_ref, local_ref, base_ref = refs[:5]
    refs = refs[5:]
    residual = local_ref[...].astype(F32) + times(gather(links, plan, arrived_refs), same_ref[...])
    scaled = (row_ref[1:2] * residual).astype(BF16)
    sent = row_ref[0:1] * (base_ref[...] + times_t(scaled, n_small_ref[...]))
    if last:
        scatter(links, plan_out, refs, sent)
    elif step == 0:
        scatter(links, plan_out, refs[1:], sent)
        refs[0][...] = DAMPING * sent
    else:
        scatter(links, plan_out, refs[2:], sent)
        refs[1][...] = refs[0][...] + DAMPING * sent


def residual_path_kernel(trips, links, plan, plan_out, last, *refs):
    arrived_refs, refs = refs[:trips], refs[trips:]
    same_ref, s_small_ref, row_ref, base_ref, state_ref, local_ref = refs[:6]
    state = state_ref[...] + DAMPING * times(gather(links, plan, arrived_refs), same_ref[...])
    if last:
        refs = refs[6:]
    else:
        refs[6][...] = state
        refs = refs[7:]
    local = base_ref[...] - times((state * row_ref[2:3]).astype(BF16), s_small_ref[...])
    local_ref[...] = local
    scatter(links, plan_out, refs, local)


def corrected(links, plan, arrived_refs, hot_ref, n_ref, n_rest_ref, weight_ref, mask_ref, local_ref):
    weight = weight_ref[...]
    residual = local_ref[...] + times_t(gather(links, plan, arrived_refs), hot_ref[...])
    scaled = (weight * residual).astype(BF16)
    cut = n_ref.shape[1]
    product = times_t(scaled[:, :cut], n_ref[...]) + times_t(scaled[:, cut:], n_rest_ref[...])
    return mask_ref[:1] * weight * product


def first_update_kernel(trips, links, plan, *refs):
    arrived_refs, refs = refs[:trips], refs[trips:]
    hot_ref, hot_t_ref, n_ref, n_rest_ref, s_ref, weight_ref, mask_ref, inner_ref, local_ref, picked_ref = refs[:10]
    state_out_ref, base_ref, s_pick_ref, s_small_ref = refs[10:]
    state = DAMPING * corrected(links, plan, arrived_refs, hot_ref, n_ref, n_rest_ref, weight_ref, mask_ref, local_ref)
    state_out_ref[...] = state
    s_pick = times(s_ref[0], hot_ref[...]).astype(BF16)
    s_pick_ref[...] = s_pick
    s_small_ref[...] = times(hot_t_ref[...], s_pick).astype(BF16)
    base_ref[...] = picked_ref[...].astype(F32) - times((state * inner_ref[:1]).astype(BF16), s_pick)


def update_kernel(trips, links, plan, *refs):
    arrived_refs, refs = refs[:trips], refs[trips:]
    hot_ref, n_ref, n_rest_ref, weight_ref, mask_ref, inner_ref, local_ref, picked_ref, s_pick_ref, state_ref = refs[:10]
    state_out_ref, base_ref = refs[10:]
    state = state_ref[...] + DAMPING * corrected(links, plan, arrived_refs, hot_ref, n_ref, n_rest_ref, weight_ref, mask_ref, local_ref)
    state_out_ref[...] = state
    base_ref[...] = picked_ref[...].astype(F32) - times((state * inner_ref[:1]).astype(BF16), s_pick_ref[...])


def last_update_kernel(trips, links, plan, *refs):
    arrived_refs, refs = refs[:trips], refs[trips:]
    hot_ref, n_ref, n_rest_ref, weight_ref, mask_ref, local_ref, state_ref, state_out_ref = refs
    update = corrected(links, plan, arrived_refs, hot_ref, n_ref, n_rest_ref, weight_ref, mask_ref, local_ref)
    state_out_ref[...] = (state_ref[...] + DAMPING * update).T


def residual_kernel(trips, links, plan, *refs):
    arrived_refs, refs = refs[:trips], refs[trips:]
    hot_ref, s_ref, turned_ref, weight_ref, mask_ref, inner_ref, n_pick_ref, state_ref = refs[:8]
    state_out_ref, local_ref, base_ref = refs[8:]
    state = state_ref[...] + DAMPING * times_t(gather(links, plan, arrived_refs), hot_ref[...])
    state_out_ref[...] = state
    local = mask_ref[:1] * (turned_ref[...].astype(F32) - times(state.astype(BF16), s_ref[0]))
    local_ref[...] = local
    base_ref[...] = times_t((weight_ref[...] * local * inner_ref[:1]).astype(BF16), n_pick_ref[...])


def close_kernel(trips, links, plan, *refs):
    arrived_refs, (hot_ref, state_ref, out_ref, piece_ref, sems) = refs[:trips], refs[trips:]
    arrived = gather(links, plan, arrived_refs)
    rows = state_ref.shape[0] // PIECES
    copies = []
    for k in range(PIECES):
        part = pl.ds(k * rows, rows)
        piece_ref[part, :] = state_ref[part, :] + DAMPING * times_t(hot_ref[part, :], arrived)
        copies.append(pltpu.make_async_copy(piece_ref.at[part, :], out_ref.at[0, part, :], sems.at[k]))
        copies[k].start()
    for copy in copies:
        copy.wait()


def run(kernel, operands, results, flops, spaces=(), outputs=pltpu.VMEM, scratch=()):
    spaces = [dict(spaces).get(k, pltpu.VMEM) for k in range(len(operands))]
    moved = sum(a.size * a.dtype.itemsize for a in (*operands, *results))
    operands = [
        pltpu.with_memory_space_constraint(a, space) if space is pltpu.HBM else a for a, space in zip(operands, spaces)
    ]
    return pl.pallas_call(
        kernel,
        out_shape=results,
        in_specs=[pl.BlockSpec(memory_space=space) for space in spaces],
        out_specs=[pl.BlockSpec(memory_space=outputs)] * len(results),
        scratch_shapes=scratch,
        compiler_params=pltpu.CompilerParams(vmem_limit_bytes=LIMIT),
        cost_estimate=pl.CostEstimate(flops=flops, bytes_accessed=moved, transcendentals=0),
    )(*operands)


def body(right_side, schur, neumann, weights, neighbours, counts, shared_rows):
    width, leads = right_side.shape[1:]
    share = shared_rows.shape[2]
    subs = lax.axis_size("sub")
    plans = [min(k // 2, len(PLANS) - 1) for k in range(2 * ITERS)]
    trips = len(swaps(subs, plans[0]))
    links = len(slots_of(0, subs))
    total = links * share

    def array(rows, columns, kind=F32):
        return jax.ShapeDtypeStruct((rows, columns), kind)

    def same_as(a):
        return jax.ShapeDtypeStruct(a.shape, a.dtype)

    messages = [array(leads, share, BF16)] * trips
    full, some = array(leads, width), array(leads, total)
    small = array(total, total, BF16)
    row = array(8, width)
    picks = 2 * leads * total * width
    whole = 2 * leads * width * width
    path = 4 * leads * total * total

    def exchange(parts, plan):
        return [lax.ppermute(part, "sub", route) for part, route in zip(parts, swaps(subs, plan))]

    def bound(kernel, *settings):
        return functools.partial(kernel, trips, links, *settings)

    hot, turned, picked, listed, weight, n_mat, *sent = run(
        bound(open_kernel, plans[0], subs),
        [shared_rows, neighbours, right_side, weights, neumann],
        [
            array(width, total, BF16),
            array(leads, width, BF16),
            array(leads, total, BF16),
            array(8, total),
            same_as(weights),
            array(width, width - width // 4, BF16),
            *messages,
        ],
        picks,
        spaces={k: pltpu.HBM for k in range(5)},
        scratch=[
            pltpu.VMEM(shared_rows.shape, jnp.int32),
            pltpu.VMEM(neighbours.shape, jnp.int32),
            pltpu.VMEM(right_side.shape, BF16),
            pltpu.SemaphoreType.DMA((5,)),
        ],
    )
    arrived = exchange(sent, plans[0])
    hot_t, n_pick, n_small, same, inner, mask, local, base, rows, n_rest, s_mat = run(
        pick_n_kernel,
        [hot, turned, listed, n_mat, weight, counts, neumann, schur],
        [
            array(total, width, BF16),
            array(total, width, BF16),
            small,
            small,
            row,
            row,
            full,
            some,
            array(8, total),
            array(width, width // 4, BF16),
            same_as(schur),
        ],
        2 * total * width * width + 2 * total * total * width + picks,
        spaces={5: pltpu.SMEM, 6: pltpu.HBM, 7: pltpu.HBM},
        scratch=[pltpu.SemaphoreType.DMA((2,))],
    )
    near = picked
    near_state = None
    for step in range(ITERS):
        came, last = arrived, step == ITERS - 1
        plan, next_plan, after = (*plans[2 * step :], None)[:3]
        operands = [*came, same, n_small, rows, near, base]
        if step and not last:
            operands.append(near_state)
        kernel = bound(update_path_kernel, plan, next_plan, step, last)
        if last:
            sent = run(kernel, operands, messages, path)
            arrived = exchange(sent, next_plan)
            (state,) = run(
                bound(last_update_kernel, plan),
                [*came, hot, n_mat, n_rest, weight, mask, local, state],
                [array(width, leads)],
                whole + picks,
            )
            break
        near_state, *sent = run(kernel, operands, [some, *messages], path)
        arrived = exchange(sent, next_plan)
        if step == 0:
            state, base, s_pick, s_small = run(
                bound(first_update_kernel, plan),
                [*came, hot, hot_t, n_mat, n_rest, s_mat, weight, mask, inner, local, picked],
                [full, some, array(width, total, BF16), small],
                whole + 2 * picks + 2 * total * width * (width + total),
            )
        else:
            state, base = run(
                bound(update_kernel, plan),
                [*came, hot, n_mat, n_rest, weight, mask, inner, local, picked, s_pick, state],
                [full, some],
                whole + 2 * picks,
            )
        came = arrived
        ends = step == ITERS - 2
        near, *sent = run(
            bound(residual_path_kernel, next_plan, after, ends),
            [*came, same, s_small, rows, base, near_state],
            [some, *([] if ends else [some]), *messages],
            path,
        )
        if not ends:
            near_state, *sent = sent
        arrived = exchange(sent, after)
        state, local, base = run(
            bound(residual_kernel, next_plan),
            [*came, hot, s_mat, turned, weight, mask, inner, n_pick, state],
            [full, full, some],
            whole + 2 * picks,
        )
    (out,) = run(
        bound(close_kernel, plans[-1]),
        [*arrived, hot, state],
        [jax.ShapeDtypeStruct((1, width, leads), F32)],
        picks,
        outputs=pltpu.HBM,
        scratch=[pltpu.VMEM((width, leads), F32), pltpu.SemaphoreType.DMA((PIECES,))],
    )
    return out


def solution(mesh):
    in_specs = (
        P("sub", None, None),
        P("sub", None, None),
        P("sub", None, None),
        P("sub", None),
        P("sub", None),
        P("sub"),
        P("sub", None, None),
    )
    out_specs = P("sub", None, None)
    return jax.shard_map(body, mesh=mesh, in_specs=in_specs, out_specs=out_specs, check_vma=False)
```

```python
import functools

import jax
import jax.numpy as jnp
from jax import lax
from jax.experimental import pallas as pl
from jax.experimental.pallas import tpu as pltpu
from jax.sharding import PartitionSpec as P

ITERS = 4
FAR = 16
DAMPING = 0.7
LIMIT = 16 * 2**20
PIECES = 4
F32 = jnp.float32
BF16 = jnp.bfloat16


PLANS = (
    (
        (0, 1, 2, 0, 2, 2, 2, 0, 0, 0, 0, 1, 2, 2, 2, 2),
        (0, 1, 1, 1, 1, 0, 0, 1, 0, 1, 1, 1, 2, 0, 1),
        (((6, 15), (22, 29)), ((0, 2), (14, 18), (25, 26), (28, 31)), ((3, 7), (19, 23), (24, 27))),
    ),
    (
        (0, 1, 1, 0, 0, 0, 0, 1, 1, 1, 1, 0, 0, 0, 0, 0),
        (0, 2, 1, 0, 0, 1, 2, 1, 0, 1, 1, 0, 0, 1, 1),
        ((), ((0, 3), (4, 13), (14, 31)), ((2, 5), (12, 15))),
    ),
)


def turns(count, plan):
    far_turns, odd_turns, _ = PLANS[plan]
    far = [far_turns[i % FAR] for i in range(count)]
    odd = [odd_turns[(i - 1) // 2] if 0 < i < count - 1 else -1 for i in range(count)]
    return far, odd


def mixed(count):
    return count == 2 * FAR


def swaps(count, plan):
    blocks = count // FAR
    near = [i ^ 1 for i in range(count)]
    far = [i ^ FAR for i in range(count)]
    odd = [(((i + 1) ^ 1) - 1) % count for i in range(count)]
    if mixed(count):
        far_turns, odd_turns = turns(count, plan)
        pairings = []
        for turn, fill in enumerate(PLANS[plan][2]):
            pairing = list(near)
            for i, j in fill:
                pairing[i], pairing[j] = j, i
            for i in range(count):
                if far_turns[i] == turn:
                    pairing[i] = far[i]
                elif odd_turns[i] == turn:
                    pairing[i] = odd[i]
            pairings.append(pairing)
        pairings.append(near)
    else:
        again = [(((i // FAR + 1) ^ 1) - 1) % blocks * FAR + i % FAR for i in range(count)]
        pairings = ([far] if blocks > 1 else []) + ([again] if blocks > 2 else []) + [odd, near]
    for pairing in pairings:
        assert all(pairing[j] == i != j for i, j in enumerate(pairing))
    return [list(enumerate(pairing)) for pairing in pairings]


def is_turn(own_turns, turn):
    bits = sum(1 << i for i, own in enumerate(own_turns) if own == turn)
    bits = bits - (1 << 32) if bits >> 31 else bits
    return lax.shift_right_logical(jnp.int32(bits), lax.axis_index("sub")) & 1 == 1


def slots_of(index, count):
    odd = lax.rem(index, 2)
    block = lax.rem(lax.div(index, FAR), 2)
    blocks = count // FAR
    far = [2 + block] if blocks > 1 else []
    again = [3 - block] if blocks > 2 else []
    return [*far, *again, 1 - odd, odd]


def times(a, b):
    return jnp.dot(a, b, preferred_element_type=F32)


def times_t(a, b):
    return lax.dot_general(a, b, (((1,), (1,)), ((), ())), preferred_element_type=F32)


def gather(links, plan, refs):
    parts = [ref[...] for ref in refs]
    if len(parts) > links:
        values = [part.astype(F32) for part in parts[:3]]
        picked = []
        for own in turns(2 * FAR, plan):
            later = jnp.where(is_turn(own, 1), values[1], values[2])
            picked.append(jnp.where(is_turn(own, 0), values[0], later).astype(BF16))
        parts = [*picked, parts[3]]
    return jnp.concatenate(parts, 1)


def scatter(links, plan, refs, block):
    share = refs[0].shape[1]
    parts = [block[:, k * share : (k + 1) * share].astype(F32) for k in range(links)]
    if len(refs) > links:
        far, odd, near = parts
        own, _ = turns(2 * FAR, plan)
        parts = [*(jnp.where(is_turn(own, turn), far, odd) for turn in range(3)), near]
    for ref, part in zip(refs, parts):
        ref[...] = part.astype(BF16)


def open_kernel(
    trips,
    links,
    plan_out,
    subs,
    rows_in,
    near_in,
    rhs_in,
    weight_in,
    n_in,
    hot_ref,
    turned_ref,
    picked_ref,
    list_ref,
    weight_ref,
    n_ref,
    *refs,
):
    out_refs, (rows_ref, near_ref, rhs_ref, sems) = refs[:trips], refs[trips:]
    pairs = [
        (rows_in, rows_ref),
        (near_in, near_ref),
        (rhs_in, rhs_ref),
        (weight_in, weight_ref),
        (n_in.at[0, :, pl.ds(0, n_ref.shape[1])], n_ref),
    ]
    copies = [pltpu.make_async_copy(source, target, sems.at[k]) for k, (source, target) in enumerate(pairs)]
    for copy in copies:
        copy.start()
    width, share = rhs_ref.shape[1], rows_ref.shape[2]
    slots = slots_of(lax.axis_index("sub"), subs)
    place = lax.broadcasted_iota(jnp.int32, (width, share), 0)
    copies[0].wait()
    copies[1].wait()
    near = near_ref[...].astype(F32)
    lane = lax.broadcasted_iota(jnp.int32, near.shape, 1)
    for k, slot in enumerate(slots):
        partner = jnp.sum(jnp.where(lane == slot, near, 0.0), 1, keepdims=True)
        row = jnp.where(partner >= 0.0, rows_ref[0, pl.ds(slot, 1), :], -1)
        list_ref[:, pl.ds(k * share, share)] = jnp.broadcast_to(row.astype(F32), (list_ref.shape[0], share))
        hot_ref[:, pl.ds(k * share, share)] = jnp.where(place == row, 1.0, 0.0).astype(BF16)
    copies[2].wait()
    turned = rhs_ref[0].T
    turned_ref[...] = turned
    picked = times(turned, hot_ref[...]).astype(BF16)
    picked_ref[...] = picked
    scatter(links, plan_out, out_refs, picked)
    for copy in copies[3:]:
        copy.wait()


def pick_n_kernel(
    hot_ref,
    turned_ref,
    list_ref,
    n_ref,
    weight_ref,
    count_ref,
    n_in,
    s_in,
    hot_t_ref,
    n_pick_ref,
    n_small_ref,
    same_ref,
    inner_ref,
    mask_ref,
    local_ref,
    base_ref,
    row_ref,
    n_rest_ref,
    s_ref,
    sems,
):
    cut = n_ref.shape[1]
    rest_copy = pltpu.make_async_copy(n_in.at[0, :, pl.ds(cut, n_rest_ref.shape[1])], n_rest_ref, sems.at[0])
    s_copy = pltpu.make_async_copy(s_in, s_ref, sems.at[1])
    rest_copy.start()
    s_copy.start()
    hot = hot_ref[...]
    width, total = hot.shape
    weight = weight_ref[...]
    side = 128
    listed = list_ref[:1]
    lane = lax.broadcasted_iota(jnp.int32, (side, side), 1).astype(F32)
    hits = [jnp.zeros((1, side), F32)] * (width // side)
    same = []
    for k in range(0, total, side):
        down = jnp.broadcast_to(listed[:, k : k + side], (side, side)).T
        for m in range(width // side):
            block = jnp.where(down == lane + float(m * side), 1.0, 0.0)
            hits[m] = hits[m] + jnp.sum(block, 0, keepdims=True)
            hot_t_ref[k : k + side, m * side : (m + 1) * side] = block.astype(BF16)
        wide = jnp.concatenate([down] * (total // side), 1)
        same.append(jnp.where((wide == listed) & (wide >= 0.0), 1.0, 0.0))
    same = jnp.concatenate(same, 0)
    same_ref[...] = same.astype(BF16)
    inner = jnp.where(jnp.concatenate(hits, 1) > 0.0, 0.0, 1.0)
    inner_ref[...] = jnp.broadcast_to(inner, inner_ref.shape)
    n_pick_ref[:, :cut] = times(hot_t_ref[...], n_ref[...]).astype(BF16)
    earlier = lax.broadcasted_iota(jnp.int32, same.shape, 0) < lax.broadcasted_iota(jnp.int32, same.shape, 1)
    repeats = jnp.sum(jnp.where(earlier, same, 0.0), 0, keepdims=True)
    first = jnp.where(repeats > 0.0, 0.0, 1.0)
    high = weight.astype(BF16).astype(F32)
    middle = (weight - high).astype(BF16).astype(F32)
    low = weight - high - middle
    level = lax.broadcasted_iota(jnp.int32, (8, width), 0)
    pieces = jnp.where(level == 0, high, jnp.where(level == 1, middle, jnp.where(level == 2, low, 0.0)))
    pieces = times(pieces.astype(BF16), hot)
    chosen = (pieces[0:1] + pieces[1:2]) + pieces[2:3]
    row_ref[0:1] = chosen
    row_ref[1:2] = chosen * first
    row_ref[2:3] = first
    row_ref[3:8] = jnp.zeros((5, total), F32)
    rest_copy.wait()
    n_pick_ref[:, cut:] = times(hot_t_ref[...], n_rest_ref[...]).astype(BF16)
    n_pick = n_pick_ref[...]
    n_small_ref[...] = times(n_pick, hot).astype(BF16)
    mask = jnp.where(lax.broadcasted_iota(jnp.int32, mask_ref.shape, 1) < count_ref[0], 1.0, 0.0)
    mask_ref[...] = mask
    local = mask[:1] * turned_ref[...].astype(F32)
    local_ref[...] = local
    base_ref[...] = times_t((weight * local * inner).astype(BF16), n_pick)
    s_copy.wait()


def update_path_kernel(trips, links, plan, plan_out, step, last, *refs):
    arrived_refs, refs = refs[:trips], refs[trips:]
    same_ref, n_small_ref, row_ref, local_ref, base_ref = refs[:5]
    refs = refs[5:]
    residual = local_ref[...].astype(F32) + times(gather(links, plan, arrived_refs), same_ref[...])
    scaled = (row_ref[1:2] * residual).astype(BF16)
    sent = row_ref[0:1] * (base_ref[...] + times_t(scaled, n_small_ref[...]))
    if last:
        scatter(links, plan_out, refs, sent)
    elif step == 0:
        scatter(links, plan_out, refs[1:], sent)
        refs[0][...] = DAMPING * sent
    else:
        scatter(links, plan_out, refs[2:], sent)
        refs[1][...] = refs[0][...] + DAMPING * sent


def residual_path_kernel(trips, links, plan, plan_out, last, *refs):
    arrived_refs, refs = refs[:trips], refs[trips:]
    same_ref, s_small_ref, row_ref, base_ref, state_ref, local_ref = refs[:6]
    state = state_ref[...] + DAMPING * times(gather(links, plan, arrived_refs), same_ref[...])
    if last:
        refs = refs[6:]
    else:
        refs[6][...] = state
        refs = refs[7:]
    local = base_ref[...] - times((state * row_ref[2:3]).astype(BF16), s_small_ref[...])
    local_ref[...] = local
    scatter(links, plan_out, refs, local)


def corrected(links, plan, arrived_refs, hot_ref, n_ref, n_rest_ref, weight_ref, mask_ref, local_ref):
    weight = weight_ref[...]
    residual = local_ref[...] + times_t(gather(links, plan, arrived_refs), hot_ref[...])
    scaled = (weight * residual).astype(BF16)
    cut = n_ref.shape[1]
    product = times_t(scaled[:, :cut], n_ref[...]) + times_t(scaled[:, cut:], n_rest_ref[...])
    return mask_ref[:1] * weight * product


def first_update_kernel(trips, links, plan, *refs):
    arrived_refs, refs = refs[:trips], refs[trips:]
    hot_ref, hot_t_ref, n_ref, n_rest_ref, s_ref, weight_ref, mask_ref, inner_ref, local_ref, picked_ref = refs[:10]
    state_out_ref, base_ref, s_pick_ref, s_small_ref = refs[10:]
    state = DAMPING * corrected(links, plan, arrived_refs, hot_ref, n_ref, n_rest_ref, weight_ref, mask_ref, local_ref)
    state_out_ref[...] = state
    s_pick = times(s_ref[0], hot_ref[...]).astype(BF16)
    s_pick_ref[...] = s_pick
    s_small_ref[...] = times(hot_t_ref[...], s_pick).astype(BF16)
    base_ref[...] = picked_ref[...].astype(F32) - times((state * inner_ref[:1]).astype(BF16), s_pick)


def update_kernel(trips, links, plan, *refs):
    arrived_refs, refs = refs[:trips], refs[trips:]
    hot_ref, n_ref, n_rest_ref, weight_ref, mask_ref, inner_ref, local_ref, picked_ref, s_pick_ref, state_ref = refs[:10]
    state_out_ref, base_ref = refs[10:]
    state = state_ref[...] + DAMPING * corrected(links, plan, arrived_refs, hot_ref, n_ref, n_rest_ref, weight_ref, mask_ref, local_ref)
    state_out_ref[...] = state
    base_ref[...] = picked_ref[...].astype(F32) - times((state * inner_ref[:1]).astype(BF16), s_pick_ref[...])


def last_update_kernel(trips, links, plan, *refs):
    arrived_refs, refs = refs[:trips], refs[trips:]
    hot_ref, n_ref, n_rest_ref, weight_ref, mask_ref, local_ref, state_ref, state_out_ref = refs
    update = corrected(links, plan, arrived_refs, hot_ref, n_ref, n_rest_ref, weight_ref, mask_ref, local_ref)
    state_out_ref[...] = (state_ref[...] + DAMPING * update).T


def residual_kernel(trips, links, plan, *refs):
    arrived_refs, refs = refs[:trips], refs[trips:]
    hot_ref, s_ref, turned_ref, weight_ref, mask_ref, inner_ref, n_pick_ref, state_ref = refs[:8]
    state_out_ref, local_ref, base_ref = refs[8:]
    state = state_ref[...] + DAMPING * times_t(gather(links, plan, arrived_refs), hot_ref[...])
    state_out_ref[...] = state
    local = mask_ref[:1] * (turned_ref[...].astype(F32) - times(state.astype(BF16), s_ref[0]))
    local_ref[...] = local
    base_ref[...] = times_t((weight_ref[...] * local * inner_ref[:1]).astype(BF16), n_pick_ref[...])


def close_kernel(trips, links, plan, *refs):
    arrived_refs, (hot_ref, state_ref, out_ref, piece_ref, sems) = refs[:trips], refs[trips:]
    arrived = gather(links, plan, arrived_refs)
    rows = state_ref.shape[0] // PIECES
    copies = []
    for k in range(PIECES):
        part = pl.ds(k * rows, rows)
        piece_ref[part, :] = state_ref[part, :] + DAMPING * times_t(hot_ref[part, :], arrived)
        copies.append(pltpu.make_async_copy(piece_ref.at[part, :], out_ref.at[0, part, :], sems.at[k]))
        copies[k].start()
    for copy in copies:
        copy.wait()


def run(kernel, operands, results, flops, spaces=(), outputs=pltpu.VMEM, scratch=()):
    spaces = [dict(spaces).get(k, pltpu.VMEM) for k in range(len(operands))]
    moved = sum(a.size * a.dtype.itemsize for a in (*operands, *results))
    operands = [
        pltpu.with_memory_space_constraint(a, space) if space is pltpu.HBM else a for a, space in zip(operands, spaces)
    ]
    return pl.pallas_call(
        kernel,
        out_shape=results,
        in_specs=[pl.BlockSpec(memory_space=space) for space in spaces],
        out_specs=[pl.BlockSpec(memory_space=outputs)] * len(results),
        scratch_shapes=scratch,
        compiler_params=pltpu.CompilerParams(vmem_limit_bytes=LIMIT),
        cost_estimate=pl.CostEstimate(flops=flops, bytes_accessed=moved, transcendentals=0),
    )(*operands)


def body(right_side, schur, neumann, weights, neighbours, counts, shared_rows):
    width, leads = right_side.shape[1:]
    share = shared_rows.shape[2]
    subs = lax.axis_size("sub")
    plans = [min(k // 2, len(PLANS) - 1) for k in range(2 * ITERS)]
    trips = len(swaps(subs, plans[0]))
    links = len(slots_of(0, subs))
    total = links * share

    def array(rows, columns, kind=F32):
        return jax.ShapeDtypeStruct((rows, columns), kind)

    def same_as(a):
        return jax.ShapeDtypeStruct(a.shape, a.dtype)

    messages = [array(leads, share, BF16)] * trips
    full, some = array(leads, width), array(leads, total)
    small = array(total, total, BF16)
    row = array(8, width)
    picks = 2 * leads * total * width
    whole = 2 * leads * width * width
    path = 4 * leads * total * total

    def exchange(parts, plan):
        return [lax.ppermute(part, "sub", route) for part, route in zip(parts, swaps(subs, plan))]

    def bound(kernel, *settings):
        return functools.partial(kernel, trips, links, *settings)

    hot, turned, picked, listed, weight, n_mat, *sent = run(
        bound(open_kernel, plans[0], subs),
        [shared_rows, neighbours, right_side, weights, neumann],
        [
            array(width, total, BF16),
            array(leads, width, BF16),
            array(leads, total, BF16),
            array(8, total),
            same_as(weights),
            array(width, width // 2, BF16),
            *messages,
        ],
        picks,
        spaces={k: pltpu.HBM for k in range(5)},
        scratch=[
            pltpu.VMEM(shared_rows.shape, jnp.int32),
            pltpu.VMEM(neighbours.shape, jnp.int32),
            pltpu.VMEM(right_side.shape, BF16),
            pltpu.SemaphoreType.DMA((5,)),
        ],
    )
    arrived = exchange(sent, plans[0])
    hot_t, n_pick, n_small, same, inner, mask, local, base, rows, n_rest, s_mat = run(
        pick_n_kernel,
        [hot, turned, listed, n_mat, weight, counts, neumann, schur],
        [
            array(total, width, BF16),
            array(total, width, BF16),
            small,
            small,
            row,
            row,
            full,
            some,
            array(8, total),
            array(width, width // 2, BF16),
            same_as(schur),
        ],
        2 * total * width * width + 2 * total * total * width + picks,
        spaces={5: pltpu.SMEM, 6: pltpu.HBM, 7: pltpu.HBM},
        scratch=[pltpu.SemaphoreType.DMA((2,))],
    )
    near = picked
    near_state = None
    for step in range(ITERS):
        came, last = arrived, step == ITERS - 1
        plan, next_plan, after = (*plans[2 * step :], None)[:3]
        operands = [*came, same, n_small, rows, near, base]
        if step and not last:
            operands.append(near_state)
        kernel = bound(update_path_kernel, plan, next_plan, step, last)
        if last:
            sent = run(kernel, operands, messages, path)
            arrived = exchange(sent, next_plan)
            (state,) = run(
                bound(last_update_kernel, plan),
                [*came, hot, n_mat, n_rest, weight, mask, local, state],
                [array(width, leads)],
                whole + picks,
            )
            break
        near_state, *sent = run(kernel, operands, [some, *messages], path)
        arrived = exchange(sent, next_plan)
        if step == 0:
            state, base, s_pick, s_small = run(
                bound(first_update_kernel, plan),
                [*came, hot, hot_t, n_mat, n_rest, s_mat, weight, mask, inner, local, picked],
                [full, some, array(width, total, BF16), small],
                whole + 2 * picks + 2 * total * width * (width + total),
            )
        else:
            state, base = run(
                bound(update_kernel, plan),
                [*came, hot, n_mat, n_rest, weight, mask, inner, local, picked, s_pick, state],
                [full, some],
                whole + 2 * picks,
            )
        came = arrived
        ends = step == ITERS - 2
        near, *sent = run(
            bound(residual_path_kernel, next_plan, after, ends),
            [*came, same, s_small, rows, base, near_state],
            [some, *([] if ends else [some]), *messages],
            path,
        )
        if not ends:
            near_state, *sent = sent
        arrived = exchange(sent, after)
        state, local, base = run(
            bound(residual_kernel, next_plan),
            [*came, hot, s_mat, turned, weight, mask, inner, n_pick, state],
            [full, full, some],
            whole + 2 * picks,
        )
    (out,) = run(
        bound(close_kernel, plans[-1]),
        [*arrived, hot, state],
        [jax.ShapeDtypeStruct((1, width, leads), F32)],
        picks,
        outputs=pltpu.HBM,
        scratch=[pltpu.VMEM((width, leads), F32), pltpu.SemaphoreType.DMA((PIECES,))],
    )
    return out


def solution(mesh):
    in_specs = (
        P("sub", None, None),
        P("sub", None, None),
        P("sub", None, None),
        P("sub", None),
        P("sub", None),
        P("sub"),
        P("sub", None, None),
    )
    out_specs = P("sub", None, None)
    return jax.shard_map(body, mesh=mesh, in_specs=in_specs, out_specs=out_specs, check_vma=False)
```

```python
import functools

import jax
import jax.numpy as jnp
from jax import lax
from jax.experimental import pallas as pl
from jax.experimental.pallas import tpu as pltpu
from jax.sharding import PartitionSpec as P

ITERS = 4
FAR = 16
DAMPING = 0.7
LIMIT = 16 * 2**20
PIECES = 8
F32 = jnp.float32
BF16 = jnp.bfloat16


PLANS = (
    (
        (0, 1, 2, 0, 2, 2, 2, 0, 0, 0, 0, 1, 2, 2, 2, 2),
        (0, 1, 1, 1, 1, 0, 0, 1, 0, 1, 1, 1, 2, 0, 1),
        (((6, 15), (22, 29)), ((0, 2), (14, 18), (25, 26), (28, 31)), ((3, 7), (19, 23), (24, 27))),
    ),
    (
        (0, 1, 1, 0, 0, 0, 0, 1, 1, 1, 1, 0, 0, 0, 0, 0),
        (0, 2, 1, 0, 0, 1, 2, 1, 0, 1, 1, 0, 0, 1, 1),
        ((), ((0, 3), (4, 13), (14, 31)), ((2, 5), (12, 15))),
    ),
)


def turns(count, plan):
    far_turns, odd_turns, _ = PLANS[plan]
    far = [far_turns[i % FAR] for i in range(count)]
    odd = [odd_turns[(i - 1) // 2] if 0 < i < count - 1 else -1 for i in range(count)]
    return far, odd


def mixed(count):
    return count == 2 * FAR


def swaps(count, plan):
    blocks = count // FAR
    near = [i ^ 1 for i in range(count)]
    far = [i ^ FAR for i in range(count)]
    odd = [(((i + 1) ^ 1) - 1) % count for i in range(count)]
    if mixed(count):
        far_turns, odd_turns = turns(count, plan)
        pairings = []
        for turn, fill in enumerate(PLANS[plan][2]):
            pairing = list(near)
            for i, j in fill:
                pairing[i], pairing[j] = j, i
            for i in range(count):
                if far_turns[i] == turn:
                    pairing[i] = far[i]
                elif odd_turns[i] == turn:
                    pairing[i] = odd[i]
            pairings.append(pairing)
        pairings.append(near)
    else:
        again = [(((i // FAR + 1) ^ 1) - 1) % blocks * FAR + i % FAR for i in range(count)]
        pairings = ([far] if blocks > 1 else []) + ([again] if blocks > 2 else []) + [odd, near]
    for pairing in pairings:
        assert all(pairing[j] == i != j for i, j in enumerate(pairing))
    return [list(enumerate(pairing)) for pairing in pairings]


def is_turn(own_turns, turn):
    bits = sum(1 << i for i, own in enumerate(own_turns) if own == turn)
    bits = bits - (1 << 32) if bits >> 31 else bits
    return lax.shift_right_logical(jnp.int32(bits), lax.axis_index("sub")) & 1 == 1


def slots_of(index, count):
    odd = lax.rem(index, 2)
    block = lax.rem(lax.div(index, FAR), 2)
    blocks = count // FAR
    far = [2 + block] if blocks > 1 else []
    again = [3 - block] if blocks > 2 else []
    return [*far, *again, 1 - odd, odd]


def times(a, b):
    return jnp.dot(a, b, preferred_element_type=F32)


def times_t(a, b):
    return lax.dot_general(a, b, (((1,), (1,)), ((), ())), preferred_element_type=F32)


def gather(links, plan, refs):
    parts = [ref[...] for ref in refs]
    if len(parts) > links:
        values = [part.astype(F32) for part in parts[:3]]
        picked = []
        for own in turns(2 * FAR, plan):
            later = jnp.where(is_turn(own, 1), values[1], values[2])
            picked.append(jnp.where(is_turn(own, 0), values[0], later).astype(BF16))
        parts = [*picked, parts[3]]
    return jnp.concatenate(parts, 1)


def scatter(links, plan, refs, block):
    share = refs[0].shape[1]
    parts = [block[:, k * share : (k + 1) * share].astype(F32) for k in range(links)]
    if len(refs) > links:
        far, odd, near = parts
        own, _ = turns(2 * FAR, plan)
        parts = [*(jnp.where(is_turn(own, turn), far, odd) for turn in range(3)), near]
    for ref, part in zip(refs, parts):
        ref[...] = part.astype(BF16)


def open_kernel(
    trips,
    links,
    plan_out,
    subs,
    rows_in,
    near_in,
    rhs_in,
    weight_in,
    n_in,
    hot_ref,
    turned_ref,
    picked_ref,
    list_ref,
    weight_ref,
    n_ref,
    *refs,
):
    out_refs, (rows_ref, near_ref, rhs_ref, sems) = refs[:trips], refs[trips:]
    pairs = [
        (rows_in, rows_ref),
        (near_in, near_ref),
        (rhs_in, rhs_ref),
        (weight_in, weight_ref),
        (n_in.at[0, :, pl.ds(0, n_ref.shape[1])], n_ref),
    ]
    copies = [pltpu.make_async_copy(source, target, sems.at[k]) for k, (source, target) in enumerate(pairs)]
    for copy in copies:
        copy.start()
    width, share = rhs_ref.shape[1], rows_ref.shape[2]
    slots = slots_of(lax.axis_index("sub"), subs)
    place = lax.broadcasted_iota(jnp.int32, (width, share), 0)
    copies[0].wait()
    copies[1].wait()
    near = near_ref[...].astype(F32)
    lane = lax.broadcasted_iota(jnp.int32, near.shape, 1)
    for k, slot in enumerate(slots):
        partner = jnp.sum(jnp.where(lane == slot, near, 0.0), 1, keepdims=True)
        row = jnp.where(partner >= 0.0, rows_ref[0, pl.ds(slot, 1), :], -1)
        list_ref[:, pl.ds(k * share, share)] = jnp.broadcast_to(row.astype(F32), (list_ref.shape[0], share))
        hot_ref[:, pl.ds(k * share, share)] = jnp.where(place == row, 1.0, 0.0).astype(BF16)
    copies[2].wait()
    turned = rhs_ref[0].T
    turned_ref[...] = turned
    picked = times(turned, hot_ref[...]).astype(BF16)
    picked_ref[...] = picked
    scatter(links, plan_out, out_refs, picked)
    for copy in copies[3:]:
        copy.wait()


def pick_n_kernel(
    hot_ref,
    turned_ref,
    list_ref,
    n_ref,
    weight_ref,
    count_ref,
    n_in,
    s_in,
    hot_t_ref,
    n_pick_ref,
    n_small_ref,
    same_ref,
    inner_ref,
    mask_ref,
    local_ref,
    base_ref,
    row_ref,
    n_rest_ref,
    s_ref,
    sems,
):
    cut = n_ref.shape[1]
    rest_copy = pltpu.make_async_copy(n_in.at[0, :, pl.ds(cut, n_rest_ref.shape[1])], n_rest_ref, sems.at[0])
    s_copy = pltpu.make_async_copy(s_in, s_ref, sems.at[1])
    rest_copy.start()
    s_copy.start()
    hot = hot_ref[...]
    width, total = hot.shape
    weight = weight_ref[...]
    side = 128
    listed = list_ref[:1]
    lane = lax.broadcasted_iota(jnp.int32, (side, side), 1).astype(F32)
    hits = [jnp.zeros((1, side), F32)] * (width // side)
    same = []
    for k in range(0, total, side):
        down = jnp.broadcast_to(listed[:, k : k + side], (side, side)).T
        for m in range(width // side):
            block = jnp.where(down == lane + float(m * side), 1.0, 0.0)
            hits[m] = hits[m] + jnp.sum(block, 0, keepdims=True)
            hot_t_ref[k : k + side, m * side : (m + 1) * side] = block.astype(BF16)
        wide = jnp.concatenate([down] * (total // side), 1)
        same.append(jnp.where((wide == listed) & (wide >= 0.0), 1.0, 0.0))
    same = jnp.concatenate(same, 0)
    same_ref[...] = same.astype(BF16)
    inner = jnp.where(jnp.concatenate(hits, 1) > 0.0, 0.0, 1.0)
    inner_ref[...] = jnp.broadcast_to(inner, inner_ref.shape)
    n_pick_ref[:, :cut] = times(hot_t_ref[...], n_ref[...]).astype(BF16)
    earlier = lax.broadcasted_iota(jnp.int32, same.shape, 0) < lax.broadcasted_iota(jnp.int32, same.shape, 1)
    repeats = jnp.sum(jnp.where(earlier, same, 0.0), 0, keepdims=True)
    first = jnp.where(repeats > 0.0, 0.0, 1.0)
    high = weight.astype(BF16).astype(F32)
    middle = (weight - high).astype(BF16).astype(F32)
    low = weight - high - middle
    level = lax.broadcasted_iota(jnp.int32, (8, width), 0)
    pieces = jnp.where(level == 0, high, jnp.where(level == 1, middle, jnp.where(level == 2, low, 0.0)))
    pieces = times(pieces.astype(BF16), hot)
    chosen = (pieces[0:1] + pieces[1:2]) + pieces[2:3]
    row_ref[0:1] = chosen
    row_ref[1:2] = chosen * first
    row_ref[2:3] = first
    row_ref[3:8] = jnp.zeros((5, total), F32)
    rest_copy.wait()
    n_pick_ref[:, cut:] = times(hot_t_ref[...], n_rest_ref[...]).astype(BF16)
    n_pick = n_pick_ref[...]
    n_small_ref[...] = times(n_pick, hot).astype(BF16)
    mask = jnp.where(lax.broadcasted_iota(jnp.int32, mask_ref.shape, 1) < count_ref[0], 1.0, 0.0)
    mask_ref[...] = mask
    local = mask[:1] * turned_ref[...].astype(F32)
    local_ref[...] = local
    base_ref[...] = times_t((weight * local * inner).astype(BF16), n_pick)
    s_copy.wait()


def update_path_kernel(trips, links, plan, plan_out, step, last, *refs):
    arrived_refs, refs = refs[:trips], refs[trips:]
    same_ref, n_small_ref, row_ref, local_ref, base_ref = refs[:5]
    refs = refs[5:]
    residual = local_ref[...].astype(F32) + times(gather(links, plan, arrived_refs), same_ref[...])
    scaled = (row_ref[1:2] * residual).astype(BF16)
    sent = row_ref[0:1] * (base_ref[...] + times_t(scaled, n_small_ref[...]))
    if last:
        scatter(links, plan_out, refs, sent)
    elif step == 0:
        scatter(links, plan_out, refs[1:], sent)
        refs[0][...] = DAMPING * sent
    else:
        scatter(links, plan_out, refs[2:], sent)
        refs[1][...] = refs[0][...] + DAMPING * sent


def residual_path_kernel(trips, links, plan, plan_out, last, *refs):
    arrived_refs, refs = refs[:trips], refs[trips:]
    same_ref, s_small_ref, row_ref, base_ref, state_ref, local_ref = refs[:6]
    state = state_ref[...] + DAMPING * times(gather(links, plan, arrived_refs), same_ref[...])
    if last:
        refs = refs[6:]
    else:
        refs[6][...] = state
        refs = refs[7:]
    local = base_ref[...] - times((state * row_ref[2:3]).astype(BF16), s_small_ref[...])
    local_ref[...] = local
    scatter(links, plan_out, refs, local)


def corrected(links, plan, arrived_refs, hot_ref, n_ref, n_rest_ref, weight_ref, mask_ref, local_ref):
    weight = weight_ref[...]
    residual = local_ref[...] + times_t(gather(links, plan, arrived_refs), hot_ref[...])
    scaled = (weight * residual).astype(BF16)
    cut = n_ref.shape[1]
    product = times_t(scaled[:, :cut], n_ref[...]) + times_t(scaled[:, cut:], n_rest_ref[...])
    return mask_ref[:1] * weight * product


def first_update_kernel(trips, links, plan, *refs):
    arrived_refs, refs = refs[:trips], refs[trips:]
    hot_ref, hot_t_ref, n_ref, n_rest_ref, s_ref, weight_ref, mask_ref, inner_ref, local_ref, picked_ref = refs[:10]
    state_out_ref, base_ref, s_pick_ref, s_small_ref = refs[10:]
    state = DAMPING * corrected(links, plan, arrived_refs, hot_ref, n_ref, n_rest_ref, weight_ref, mask_ref, local_ref)
    state_out_ref[...] = state
    s_pick = times(s_ref[0], hot_ref[...]).astype(BF16)
    s_pick_ref[...] = s_pick
    s_small_ref[...] = times(hot_t_ref[...], s_pick).astype(BF16)
    base_ref[...] = picked_ref[...].astype(F32) - times((state * inner_ref[:1]).astype(BF16), s_pick)


def update_kernel(trips, links, plan, *refs):
    arrived_refs, refs = refs[:trips], refs[trips:]
    hot_ref, n_ref, n_rest_ref, weight_ref, mask_ref, inner_ref, local_ref, picked_ref, s_pick_ref, state_ref = refs[:10]
    state_out_ref, base_ref = refs[10:]
    state = state_ref[...] + DAMPING * corrected(links, plan, arrived_refs, hot_ref, n_ref, n_rest_ref, weight_ref, mask_ref, local_ref)
    state_out_ref[...] = state
    base_ref[...] = picked_ref[...].astype(F32) - times((state * inner_ref[:1]).astype(BF16), s_pick_ref[...])


def last_update_kernel(trips, links, plan, *refs):
    arrived_refs, refs = refs[:trips], refs[trips:]
    hot_ref, n_ref, n_rest_ref, weight_ref, mask_ref, local_ref, state_ref, state_out_ref = refs
    update = corrected(links, plan, arrived_refs, hot_ref, n_ref, n_rest_ref, weight_ref, mask_ref, local_ref)
    state_out_ref[...] = (state_ref[...] + DAMPING * update).T


def residual_kernel(trips, links, plan, *refs):
    arrived_refs, refs = refs[:trips], refs[trips:]
    hot_ref, s_ref, turned_ref, weight_ref, mask_ref, inner_ref, n_pick_ref, state_ref = refs[:8]
    state_out_ref, local_ref, base_ref = refs[8:]
    state = state_ref[...] + DAMPING * times_t(gather(links, plan, arrived_refs), hot_ref[...])
    state_out_ref[...] = state
    local = mask_ref[:1] * (turned_ref[...].astype(F32) - times(state.astype(BF16), s_ref[0]))
    local_ref[...] = local
    base_ref[...] = times_t((weight_ref[...] * local * inner_ref[:1]).astype(BF16), n_pick_ref[...])


def close_kernel(trips, links, plan, *refs):
    arrived_refs, (hot_ref, state_ref, out_ref, piece_ref, sems) = refs[:trips], refs[trips:]
    arrived = gather(links, plan, arrived_refs)
    rows = state_ref.shape[0] // PIECES
    copies = []
    for k in range(PIECES):
        part = pl.ds(k * rows, rows)
        piece_ref[part, :] = state_ref[part, :] + DAMPING * times_t(hot_ref[part, :], arrived)
        copies.append(pltpu.make_async_copy(piece_ref.at[part, :], out_ref.at[0, part, :], sems.at[k]))
        copies[k].start()
    for copy in copies:
        copy.wait()


def run(kernel, operands, results, flops, spaces=(), outputs=pltpu.VMEM, scratch=()):
    spaces = [dict(spaces).get(k, pltpu.VMEM) for k in range(len(operands))]
    moved = sum(a.size * a.dtype.itemsize for a in (*operands, *results))
    operands = [
        pltpu.with_memory_space_constraint(a, space) if space is pltpu.HBM else a for a, space in zip(operands, spaces)
    ]
    return pl.pallas_call(
        kernel,
        out_shape=results,
        in_specs=[pl.BlockSpec(memory_space=space) for space in spaces],
        out_specs=[pl.BlockSpec(memory_space=outputs)] * len(results),
        scratch_shapes=scratch,
        compiler_params=pltpu.CompilerParams(vmem_limit_bytes=LIMIT),
        cost_estimate=pl.CostEstimate(flops=flops, bytes_accessed=moved, transcendentals=0),
    )(*operands)


def body(right_side, schur, neumann, weights, neighbours, counts, shared_rows):
    width, leads = right_side.shape[1:]
    share = shared_rows.shape[2]
    subs = lax.axis_size("sub")
    plans = [min(k // 2, len(PLANS) - 1) for k in range(2 * ITERS)]
    trips = len(swaps(subs, plans[0]))
    links = len(slots_of(0, subs))
    total = links * share

    def array(rows, columns, kind=F32):
        return jax.ShapeDtypeStruct((rows, columns), kind)

    def same_as(a):
        return jax.ShapeDtypeStruct(a.shape, a.dtype)

    messages = [array(leads, share, BF16)] * trips
    full, some = array(leads, width), array(leads, total)
    small = array(total, total, BF16)
    row = array(8, width)
    picks = 2 * leads * total * width
    whole = 2 * leads * width * width
    path = 4 * leads * total * total

    def exchange(parts, plan):
        return [lax.ppermute(part, "sub", route) for part, route in zip(parts, swaps(subs, plan))]

    def bound(kernel, *settings):
        return functools.partial(kernel, trips, links, *settings)

    hot, turned, picked, listed, weight, n_mat, *sent = run(
        bound(open_kernel, plans[0], subs),
        [shared_rows, neighbours, right_side, weights, neumann],
        [
            array(width, total, BF16),
            array(leads, width, BF16),
            array(leads, total, BF16),
            array(8, total),
            same_as(weights),
            array(width, width // 2, BF16),
            *messages,
        ],
        picks,
        spaces={k: pltpu.HBM for k in range(5)},
        scratch=[
            pltpu.VMEM(shared_rows.shape, jnp.int32),
            pltpu.VMEM(neighbours.shape, jnp.int32),
            pltpu.VMEM(right_side.shape, BF16),
            pltpu.SemaphoreType.DMA((5,)),
        ],
    )
    arrived = exchange(sent, plans[0])
    hot_t, n_pick, n_small, same, inner, mask, local, base, rows, n_rest, s_mat = run(
        pick_n_kernel,
        [hot, turned, listed, n_mat, weight, counts, neumann, schur],
        [
            array(total, width, BF16),
            array(total, width, BF16),
            small,
            small,
            row,
            row,
            full,
            some,
            array(8, total),
            array(width, width // 2, BF16),
            same_as(schur),
        ],
        2 * total * width * width + 2 * total * total * width + picks,
        spaces={5: pltpu.SMEM, 6: pltpu.HBM, 7: pltpu.HBM},
        scratch=[pltpu.SemaphoreType.DMA((2,))],
    )
    near = picked
    near_state = None
    for step in range(ITERS):
        came, last = arrived, step == ITERS - 1
        plan, next_plan, after = (*plans[2 * step :], None)[:3]
        operands = [*came, same, n_small, rows, near, base]
        if step and not last:
            operands.append(near_state)
        kernel = bound(update_path_kernel, plan, next_plan, step, last)
        if last:
            sent = run(kernel, operands, messages, path)
            arrived = exchange(sent, next_plan)
            (state,) = run(
                bound(last_update_kernel, plan),
                [*came, hot, n_mat, n_rest, weight, mask, local, state],
                [array(width, leads)],
                whole + picks,
            )
            break
        near_state, *sent = run(kernel, operands, [some, *messages], path)
        arrived = exchange(sent, next_plan)
        if step == 0:
            state, base, s_pick, s_small = run(
                bound(first_update_kernel, plan),
                [*came, hot, hot_t, n_mat, n_rest, s_mat, weight, mask, inner, local, picked],
                [full, some, array(width, total, BF16), small],
                whole + 2 * picks + 2 * total * width * (width + total),
            )
        else:
            state, base = run(
                bound(update_kernel, plan),
                [*came, hot, n_mat, n_rest, weight, mask, inner, local, picked, s_pick, state],
                [full, some],
                whole + 2 * picks,
            )
        came = arrived
        ends = step == ITERS - 2
        near, *sent = run(
            bound(residual_path_kernel, next_plan, after, ends),
            [*came, same, s_small, rows, base, near_state],
            [some, *([] if ends else [some]), *messages],
            path,
        )
        if not ends:
            near_state, *sent = sent
        arrived = exchange(sent, after)
        state, local, base = run(
            bound(residual_kernel, next_plan),
            [*came, hot, s_mat, turned, weight, mask, inner, n_pick, state],
            [full, full, some],
            whole + 2 * picks,
        )
    (out,) = run(
        bound(close_kernel, plans[-1]),
        [*arrived, hot, state],
        [jax.ShapeDtypeStruct((1, width, leads), F32)],
        picks,
        outputs=pltpu.HBM,
        scratch=[pltpu.VMEM((width, leads), F32), pltpu.SemaphoreType.DMA((PIECES,))],
    )
    return out


def solution(mesh):
    in_specs = (
        P("sub", None, None),
        P("sub", None, None),
        P("sub", None, None),
        P("sub", None),
        P("sub", None),
        P("sub"),
        P("sub", None, None),
    )
    out_specs = P("sub", None, None)
    return jax.shard_map(body, mesh=mesh, in_specs=in_specs, out_specs=out_specs, check_vma=False)
```
